128 devices in a mesh: pipe: 2 (over core), tensor: 8 (over x_hi, y), dp: 8 (over x_lo, z).
Axes of the slice: x: 4 (x_hi: 2, x_lo: 2; x = x_hi * 2 + x_lo), y: 4, z: 4, core: 2. Of those that a mesh axis runs over, the one named last changes fastest.
Arguments:
- inputs: bfloat16 [6144, 1024], P('dp'), may hold values from -6 to 6
- cotangent: bfloat16 [6144, 1024], P('dp'), may hold values from -6 to 6
- doc_ids: int32 [48, 128], P('dp'), may hold values from 0 to 5, never falling along the last dimension, each value on 1 to 96 neighbouring positions
- qkv_weight: bfloat16 [2, 1024, 3, 1024], P('pipe', None, None, 'tensor'), may hold values from -0.1875 to 0.1875
- qkv_bias: bfloat16 [2, 2, 1024], P('pipe', None, 'tensor'), may hold values from -2 to 2
- out_weight: bfloat16 [2, 1024, 1024], P('pipe', 'tensor'), may hold values from -0.5 to 0.5
- fc1_weight: bfloat16 [2, 1024, 4096], P('pipe', None, 'tensor'), may hold values from -0.1875 to 0.1875
- fc1_bias: bfloat16 [2, 4096], P('pipe', 'tensor'), may hold values from -2 to 2
- fc2_weight: bfloat16 [2, 4096, 1024], P('pipe', 'tensor'), may hold values from -0.09375 to 0.09375
- norm_gains: bfloat16 [2, 2, 1024], P('pipe'), may hold values from 0.5 to 1.5
- shifts: bfloat16 [2, 4, 1024], P('pipe'), may hold values from -2 to 2
Outputs:
- section_outputs: float32 [2, 6144, 1024], P('pipe', 'dp', 'tensor')
- input_grads: float32 [2, 6144, 1024], P('pipe', 'dp', 'tensor')
- grad_qkv: float32 [2, 1024, 3, 1024], P('pipe', 'dp', None, 'tensor')
- grad_qkv_bias: float32 [2, 2, 1024], P('pipe', None, ('tensor', 'dp'))
- grad_out: float32 [2, 1024, 1024], P('pipe', 'tensor', 'dp')
- grad_fc1: float32 [2, 1024, 4096], P('pipe', 'dp', 'tensor')
- grad_fc1_bias: float32 [2, 4096], P('pipe', ('tensor', 'dp'))
- grad_fc2: float32 [2, 4096, 1024], P('pipe', 'tensor', 'dp')
- grad_gains: float32 [2, 2, 1024], P('pipe', None, ('tensor', 'dp'))
- grad_shifts: float32 [2, 4, 1024], P('pipe', None, ('tensor', 'dp'))
The draws below stay inside these ranges and needn't reach their ends.
Inputs may be any that keep to these rules, and one draw needn't show every extreme that they name: Within each row of doc_ids the numbers never fall; each sequence holds 1 to 96 consecutive tokens, and one of them exactly that many.
All inputs are finite; a program needn't handle non-finite values.
Results may differ from the reference program's by a relative error of at most 0.033.
Values may be sent and summed in bfloat16 or wider, within the bound.
A program may use at most 192 MiB of HBM per device.

```python
import math
import jax
import jax.numpy as jnp
import numpy as np
from jax import lax

D = 1024
HEADS = 16
HD = 64
FF = 4096
TOK_MB = 128
MB = 6
TOKENS = 6144
N_DP = 8


def strengthened(entries, key, source, target, parts, factor):
    def block_of(dim):
        return (jnp.arange(entries.shape[dim]) // (entries.shape[dim] // parts)).reshape((-1,) + (1,) * (entries.ndim - 1 - dim))

    near = jax.random.permutation(key, parts)[block_of(target)]
    second = (block_of(target) + parts // 2) % parts
    return jnp.where((block_of(source) == near) | (block_of(source) == second), factor * entries, entries)


def level_of(rng, dims, shards, least, high):
    factor_of, own = 1.0, jax.random.fold_in(rng, 6)
    for dim, blocks in shards:
        steps = jnp.exp(jax.random.uniform(jax.random.fold_in(own, dim), (blocks,), jnp.float32, least / len(shards), high / len(shards)))
        factor_of = factor_of * jnp.repeat(steps, dims[dim] // blocks).reshape([-1 if axis == dim else 1 for axis in range(len(dims))])
    return factor_of


def length_profile(amount, total, most, slope):
    weights = [(1 << 20) // math.isqrt(rank ** slope) + 1 for rank in range(2, amount + 1)]
    spare, counts = total - most - (amount - 1), [1] * (amount - 1)
    while spare > 0:
        candidates = [i for i in range(amount - 1) if counts[i] < most]
        whole, left = sum([weights[i] for i in candidates]), spare
        for i in candidates:
            addition = min(most - counts[i], max(1, left * weights[i] // whole), spare)
            counts[i] = counts[i] + addition
            spare = spare - addition
    return np.array([most] + counts)


def uneven_parts(stream_key, count, total, reach, skew):
    if count == 2:
        one = jax.random.randint(stream_key, (), max(1, total - reach), min(reach, total - 1) + 1)
        return jnp.stack([one, total - one])
    tallies = jnp.asarray(length_profile(count, total, reach, skew), jnp.int32)
    pairs = (count - 1) // 2
    giver, receiver = tallies[1:1 + 2 * pairs:2], tallies[2:2 + 2 * pairs:2]
    slack = jnp.minimum(giver - 1, reach - receiver)
    moved = jax.random.randint(jax.random.fold_in(stream_key, 1), (pairs,), 0, 1 << 20) % (slack + 1)
    tallies = tallies.at[1:1 + 2 * pairs:2].set(giver - moved).at[2:2 + 2 * pairs:2].set(receiver + moved)
    return tallies[jax.random.permutation(jax.random.fold_in(stream_key, 2), count)]


def bell_draw(stream_key, extent, spread, bound, cuts=(), dtype=jnp.bfloat16):
    entries = jax.random.normal(stream_key, extent, jnp.float32) * spread
    if len(cuts) > 0:
        entries = level_of(stream_key, extent, cuts, -0.22, 0.18) * entries
    return jnp.clip(entries, min=-bound, max=bound).astype(dtype)


def noise_with(rng, shape, deviation, limit, cuts, heavy, kind=jnp.bfloat16):
    values = deviation * jax.random.normal(rng, shape, jnp.float32)
    if cuts:
        values = values * level_of(rng, shape, cuts, -0.22, 0.18)
    return jnp.clip(strengthened(values, jax.random.fold_in(rng, 3), *heavy), -limit, limit).astype(kind)


def setup_inputs(seed: int = 0) -> dict:
    key_list = jax.random.split(jax.random.key(seed), 12)
    inputs = bell_draw(key_list[0], (TOKENS, D), 1.0, 6.0, ((0, 8),))
    cotangent = noise_with(key_list[1], (TOKENS, D), 1.0, 6.0, ((0, 8),), (0, 1, 8, 2.0))
    doc_ids = jax.vmap(lambda own: jnp.searchsorted(jnp.cumsum(uneven_parts(own, 6, TOK_MB, 3 * TOK_MB // 4, 2)), jnp.arange(TOK_MB), side="right"))(jax.random.split(key_list[2], (N_DP * MB))).reshape((N_DP * MB, TOK_MB)).astype(jnp.int32)
    qkv_weight = bell_draw(key_list[3], (2, D, 3, D), D ** -0.5, 0.1875, ((0, 2), (3, 8)))
    qkv_bias = bell_draw(key_list[4], (2, 2, D), 0.3, 2.0, ((0, 2), (2, 8)))
    out_weight = bell_draw(key_list[5], (2, D, D), (D // 8) ** -0.5, 0.5, ((0, 2), (1, 8)))
    fc1_weight = bell_draw(key_list[6], (2, D, FF), D ** -0.5, 0.1875, ((0, 2), (2, 8)))
    fc1_bias = bell_draw(key_list[7], (2, FF), 0.3, 2.0, ((0, 2), (1, 8)))
    fc2_weight = bell_draw(key_list[8], (2, FF, D), FF ** -0.5, 0.09375, ((0, 2), (1, 8)))
    norm_gains = jnp.clip(1.0 + 0.1 * jax.random.normal(key_list[9], (2, 2, D), jnp.float32), 0.5, 1.5).astype(jnp.bfloat16)
    shifts = bell_draw(key_list[10], (2, 4, D), 0.3, 2.0, ((0, 2),))
    return {"inputs": inputs, "cotangent": cotangent, "doc_ids": doc_ids, "qkv_weight": qkv_weight, "qkv_bias": qkv_bias, "out_weight": out_weight, "fc1_weight": fc1_weight, "fc1_bias": fc1_bias, "fc2_weight": fc2_weight, "norm_gains": norm_gains, "shifts": shifts}


EPSILON = 1e-05
PRECISION_FULL = lax.Precision.HIGHEST

@jax.custom_vjp
def low(v):
    return lax.optimization_barrier(v.astype(jnp.bfloat16)).astype(jnp.float32)

@jax.custom_vjp
def lowered_backward(v):
    return v

def low_keep(v):
    return (low(v), None)

def low_pass(kept, grad):
    return (grad,)

def back_keep(v):
    return (v, None)

def back_low(kept, grad):
    return (low(grad),)
low.defvjp(low_keep, low_pass)
lowered_backward.defvjp(back_keep, back_low)

def normalize(hidden, gain_row, offset):
    centre = lax.optimization_barrier(jnp.mean(hidden, -1, keepdims=True))
    centered = hidden - centre
    variance = lax.optimization_barrier(jnp.mean(centered * centered, -1, keepdims=True))
    return centered * lax.rsqrt(variance + EPSILON) * gain_row + offset

def attend(packed):
    qkv_block, segment = packed
    length = qkv_block.shape[0]
    queries = qkv_block[:, 0].reshape(length, HEADS, HD)
    key_rows = qkv_block[:, 1].reshape(length, HEADS, HD)
    values = qkv_block[:, 2].reshape(length, HEADS, HD)
    scores = jnp.einsum('qhd,khd->hqk', queries, key_rows, precision=PRECISION_FULL) * HD ** (-0.5)
    scores = lowered_backward(scores)
    positions = jnp.arange(length)
    visible = (positions[None, :] <= positions[:, None]) & (segment[:, None] == segment[None, :])
    scores = jnp.where(visible, scores, -1e+30)
    highest = lax.optimization_barrier(jnp.max(scores, -1, keepdims=True))
    weights = jnp.exp(scores - highest)
    probability = low(weights / lax.optimization_barrier(jnp.sum(weights, -1, keepdims=True)))
    mixture = jnp.einsum('hqk,khd->qhd', probability, values, precision=PRECISION_FULL).reshape(length, HEADS * HD)
    return lowered_backward(low(mixture))

def block_layer(hidden, params, segments):
    qkv_weight, qkv_bias, out_weight, up_projection_weight, up_projection_bias, down_projection_weight, gains, shifts = params
    normed = low(normalize(hidden, gains[0], shifts[0]))
    projected = jnp.einsum('mrd,dce->mrce', normed, qkv_weight, precision=PRECISION_FULL)
    bias_rows = jnp.stack([qkv_bias[0], jnp.zeros_like(qkv_bias[0]), qkv_bias[1]])
    projected = lowered_backward(low(projected + bias_rows))
    attended = lax.map(jax.checkpoint(attend), (projected, segments))
    branch = lowered_backward(jnp.einsum('mrk,kd->mrd', attended, out_weight, precision=PRECISION_FULL) + shifts[1])
    middle = hidden + branch
    second_normed_rows = low(normalize(middle, gains[1], shifts[2]))
    input_before_norm = lowered_backward(jnp.einsum('ezl,lw->ezw', second_normed_rows, up_projection_weight, precision=PRECISION_FULL) + up_projection_bias)
    activated_hidden = low(jax.nn.gelu(input_before_norm, approximate=True))
    feed_forward_output = lowered_backward(jnp.einsum('cwl,lz->cwz', activated_hidden, down_projection_weight, precision=PRECISION_FULL) + shifts[3])
    return middle + feed_forward_output

def reference(inputs, cotangent, doc_ids, qkv_weight, qkv_bias, out_weight, fc1_weight, fc1_bias, fc2_weight, norm_gains, shifts):
    block_total = doc_ids.shape[0]
    row_count = doc_ids.shape[1]
    start = inputs.astype(jnp.float32).reshape(block_total, row_count, D)
    params = tuple((array.astype(jnp.float32) for array in (qkv_weight, qkv_bias, out_weight, fc1_weight, fc1_bias, fc2_weight, norm_gains, shifts)))

    def forward(start_rows, all_params, correction):
        first_params = tuple((array[0] for array in all_params))
        second_params = tuple((array[1] for array in all_params))
        section_one = block_layer(start_rows, first_params, doc_ids)
        section_two = block_layer(lowered_backward(low(section_one)) + correction, second_params, doc_ids)
        return (section_one, section_two)
    outputs, pull_back = jax.vjp(forward, start, params, jnp.zeros_like(start))
    seed_grad = cotangent.astype(jnp.float32).reshape(start.shape)
    grad_start, grad_params, grad_correction = pull_back((jnp.zeros_like(start), seed_grad))
    section_outputs = jnp.stack([outputs[0], outputs[1]]).reshape(2, block_total * row_count, D)
    input_grads = jnp.stack([grad_start, grad_correction]).reshape(2, block_total * row_count, D)
    return (section_outputs, input_grads, grad_params[0], grad_params[1], grad_params[2], grad_params[3], grad_params[4], grad_params[5], grad_params[6], grad_params[7])
```

```python
import functools

import jax
import jax.numpy as jnp
from jax import lax
from jax.experimental import pallas as pl
from jax.experimental.pallas import tpu as pltpu
from jax.sharding import PartitionSpec as P

MESH = pl.DeviceIdType.MESH
F32 = jnp.float32
BF16 = jnp.bfloat16
EPSILON = 1e-05
HD = 64
SCALE = HD**-0.5
D = 1024
ROWS = 128
T = 8
OWN = ROWS // T
GELU_C = 0.7978845608028654
GELU_A = 0.044715


def mm(a, b):
    return lax.dot_general(a, b, (((1,), (0,)), ((), ())), preferred_element_type=F32)


def mm_nt(a, b):
    return lax.dot_general(a, b, (((1,), (1,)), ((), ())), preferred_element_type=F32)


def mm_tn(a, b):
    return lax.dot_general(a, b, (((0,), (0,)), ((), ())), preferred_element_type=F32)


def standardize(rows):
    centered = rows - jnp.mean(rows, -1, keepdims=True)
    variance = jnp.mean(centered * centered, -1, keepdims=True)
    root = lax.rsqrt(variance + EPSILON)
    return centered * root, root


def norm_back(rows, gain, grad):
    unit, root = standardize(rows)
    e = grad * gain
    slope = root * (
        e - jnp.mean(e, -1, keepdims=True) - unit * jnp.mean(e * unit, -1, keepdims=True)
    )
    return slope, jnp.sum(grad * unit, 0, keepdims=True), jnp.sum(grad, 0, keepdims=True)


def kernel(
    chunks,
    x_ref,
    ct_ref,
    mask_ref,
    wqkv_in,
    wout_in,
    w1_in,
    w2_in,
    vec_in,
    sec_ref,
    ing_ref,
    gqkv_ref,
    gout_ref,
    g1_ref,
    g2_ref,
    gsmall_ref,
    gbias_ref,
    wqkv,
    wout,
    w1,
    w2,
    vec,
    n1,
    n2,
    dmr,
    dyr,
    qkv,
    mix,
    prob,
    up,
    act,
    dup,
    dqkv,
    hrow,
    mrow,
    part,
    rs,
    ostage,
    obuf,
    wsem,
    wsend,
    rsem,
    rsend,
    gsem,
    gsend,
    osem,
    osend,
):
    c = lax.axis_index("pipe")
    t = lax.axis_index("tensor")
    d = lax.axis_index("dp")

    barrier = pltpu.get_barrier_semaphore()
    for j in range(T):
        other = lax.rem(t + j, T)
        if j:
            pl.semaphore_signal(barrier, inc=1, device_id=(c, other, d), device_id_type=MESH)
        pl.semaphore_signal(barrier, inc=1, device_id=(1 - c, other, d), device_id_type=MESH)
    pl.semaphore_wait(barrier, 2 * T - 1)

    weights = ((vec_in, vec), (wqkv_in, wqkv), (wout_in, wout), (w1_in, w1), (w2_in, w2))
    for i, (own, both) in enumerate(weights):
        pltpu.make_async_copy(own, both.at[c], wsem.at[i, c]).start()
        pltpu.make_async_remote_copy(
            src_ref=own,
            dst_ref=both.at[c],
            send_sem=wsend.at[i],
            recv_sem=wsem.at[i, c],
            device_id=(1 - c, t, d),
            device_id_type=MESH,
        ).start()

    def need(i, layer):
        both = weights[i][1]
        pltpu.make_async_copy(both.at[layer], both.at[layer], wsem.at[i, layer]).wait()

    def span(k):
        return pl.ds(pl.multiple_of(k * ROWS, ROWS), ROWS)

    def mine(k, who):
        return pl.ds(pl.multiple_of(k * ROWS + who * OWN, OWN), OWN)

    def scatter_start(ph, k):
        for j in range(1, T):
            other = lax.rem(t + j, T)
            pltpu.make_async_remote_copy(
                src_ref=part.at[ph, mine(k, other)],
                dst_ref=rs.at[ph, k, j - 1],
                send_sem=rsend.at[ph],
                recv_sem=rsem.at[ph, k],
                device_id=(c, other, d),
                device_id_type=MESH,
            ).start()

    def scatter_finish(ph, k):
        pltpu.make_async_copy(rs.at[ph, k], rs.at[ph, k], rsem.at[ph, k]).wait()
        total = part[ph, mine(k, t)].astype(F32)
        for j in range(T - 1):
            total = total + rs[ph, k, j].astype(F32)
        return total

    def gather_start(which, buf, layer, k):
        for j in range(1, T):
            other = lax.rem(t + j, T)
            pltpu.make_async_remote_copy(
                src_ref=buf.at[layer, mine(k, t)],
                dst_ref=buf.at[layer, mine(k, t)],
                send_sem=gsend.at[which, layer],
                recv_sem=gsem.at[which, layer, k],
                device_id=(c, other, d),
                device_id_type=MESH,
            ).start()

    def gather_wait(which, buf, layer, k):
        view = buf.at[layer, pl.ds(0, (T - 1) * OWN)]
        pltpu.make_async_copy(view, view, gsem.at[which, layer, k]).wait()

    def emit(kind, layer, k, rows):
        low = rows.astype(BF16)
        for j in range(T):
            ostage[kind, layer, k, j] = low[:, j * 128 : (j + 1) * 128]
        target = pl.ds(pl.multiple_of(c * (chunks * ROWS) + k * ROWS + t * OWN, OWN), OWN)

        def remote(j):
            other = lax.rem(t + j, T)
            pltpu.make_async_remote_copy(
                src_ref=ostage.at[kind, layer, k, other],
                dst_ref=obuf.at[kind, target],
                send_sem=osend.at[kind, layer],
                recv_sem=osem.at[kind],
                device_id=(layer, other, d),
                device_id_type=MESH,
            ).start()

        for j in range(1, T):
            remote(j)

        @pl.when(c == layer)
        def _():
            pltpu.make_async_copy(
                ostage.at[kind, layer, k, t], obuf.at[kind, target], osem.at[kind]
            ).start()

        @pl.when(c != layer)
        def _():
            remote(0)

    left_half = lax.broadcasted_iota(jnp.int32, (ROWS, 128), 1) < HD

    def heads(value):
        zero = jnp.zeros_like(value)
        return jnp.where(left_half, value, zero), jnp.where(left_half, zero, value)

    def each(count, body):
        def step(i, carry):
            body(i)
            return carry

        lax.fori_loop(0, count, step, 0)

    def forward(layer):
        ph = layer * 2

        @pl.when(layer == 0)
        def _():
            need(0, 0)
            need(1, 0)
            gain = vec[0, 0:1]
            offset = vec[0, 2:3]

            def start(k):
                unit, _ = standardize(x_ref[span(k)].astype(F32))
                n1[0, span(k)] = (unit * gain + offset).astype(BF16)
                hrow[0, k] = x_ref[mine(k, t)].astype(F32)

            each(chunks, start)
            need(2, 0)

        @pl.when(layer == 1)
        def _():
            need(2, 1)

        def attention(k):
            @pl.when(layer == 1)
            def _():
                gather_wait(0, n1, 1, k)

            packed = mm(n1[layer, span(k)], wqkv[layer]) + vec[layer, 6:7, 0:384]
            packed = packed.astype(BF16)
            qkv[layer, span(k)] = packed
            queries, keys, values = packed[:, 0:128], packed[:, 128:256], packed[:, 256:384]
            visible = mask_ref[span(k)] > 0
            parts = []
            for head, query in enumerate(heads(queries)):
                scores = jnp.where(visible, mm_nt(query, keys) * SCALE, -1e30)
                weights_ = jnp.exp(scores - jnp.max(scores, -1, keepdims=True))
                p = weights_ / jnp.sum(weights_, -1, keepdims=True)
                prob[layer, k, head] = p
                parts.append(mm(p.astype(BF16), values))
            mixture = jnp.where(left_half, parts[0], parts[1]).astype(BF16)
            mix[layer, span(k)] = mixture
            part[ph, span(k)] = mm(mixture, wout[layer]).astype(BF16)
            scatter_start(ph, k)

        each(chunks, attention)

        def second_norm(k):
            rows = hrow[layer, k] + scatter_finish(ph, k) + vec[layer, 3:4]
            mrow[layer, k] = rows
            unit, _ = standardize(rows)
            n2[layer, mine(k, t)] = (unit * vec[layer, 1:2] + vec[layer, 4:5]).astype(BF16)
            gather_start(1, n2, layer, k)

        each(chunks, second_norm)
        need(3, layer)
        need(4, layer)

        def feed(k):
            gather_wait(1, n2, layer, k)
            u = mm(n2[layer, span(k)], w1[layer]) + vec[layer, 7:8, 0:512]
            up[layer, span(k)] = u
            g = 0.5 * u * (1.0 + jnp.tanh(GELU_C * (u + GELU_A * (u * u * u))))
            g = g.astype(BF16)
            act[layer, span(k)] = g
            part[ph + 1, span(k)] = mm(g, w2[layer]).astype(BF16)
            scatter_start(ph + 1, k)

        each(chunks, feed)

        @pl.when(layer == 0)
        def _():
            need(0, 1)
            need(1, 1)

        def finish(k):
            rows = mrow[layer, k] + scatter_finish(ph + 1, k) + vec[layer, 5:6]

            @pl.when(layer == 0)
            def _():
                entering = rows.astype(BF16).astype(F32)
                hrow[1, k] = entering
                unit, _ = standardize(entering)
                n1[1, mine(k, t)] = (unit * vec[1, 0:1] + vec[1, 2:3]).astype(BF16)
                gather_start(0, n1, 1, k)

            emit(0, layer, k, rows)

        each(chunks, finish)

    each(2, forward)

    def copy_ct(k):
        dyr[1, span(k)] = ct_ref[span(k)]

    each(chunks, copy_ct)
    gsmall_ref[...] = jnp.zeros_like(gsmall_ref)
    gbias_ref[...] = jnp.zeros_like(gbias_ref)

    def backward(i):
        layer = 1 - i
        ph = 4 + layer * 2

        def feed_back(k):
            @pl.when(layer == 0)
            def _():
                gather_wait(3, dyr, 0, k)

            grad = mm_nt(dyr[layer, span(k)], w2[layer])
            u = up[layer, span(k)]
            bend = jnp.tanh(GELU_C * (u + GELU_A * (u * u * u)))
            slope = 0.5 * (1.0 + bend) + (0.5 * u) * (1.0 - bend * bend) * (
                GELU_C * (1.0 + (3.0 * GELU_A) * (u * u))
            )
            du = (grad * slope).astype(BF16)
            dup[span(k)] = du
            part[ph, span(k)] = mm_nt(du, w1[layer]).astype(BF16)
            scatter_start(ph, k)
            gbias_ref[layer, 0:1, 384:896] += jnp.sum(du.astype(F32), 0, keepdims=True)

        each(chunks, feed_back)

        def grad_down(b):
            cols = pl.ds(pl.multiple_of(b * 128, 128), 128)
            g2_ref[layer, cols] = mm_tn(act[layer, :, cols], dyr[layer]).astype(BF16)

        each(4, grad_down)

        def grad_up(b):
            cols = pl.ds(pl.multiple_of(b * 256, 256), 256)
            g1_ref[layer, cols] = mm_tn(n2[layer, :, cols], dup[...]).astype(BF16)

        each(4, grad_up)

        def middle(k):
            grad = dyr[layer, mine(k, t)].astype(F32)
            slope, gain_grad, shift_grad = norm_back(
                mrow[layer, k], vec[layer, 1:2], scatter_finish(ph, k)
            )
            dm = grad + slope
            mrow[layer, k] = dm
            low = dm.astype(BF16)
            dmr[layer, mine(k, t)] = low
            gather_start(2, dmr, layer, k)
            gsmall_ref[layer, 1:2] += gain_grad
            gsmall_ref[layer, 3:4] += jnp.sum(low.astype(F32), 0, keepdims=True)
            gsmall_ref[layer, 4:5] += shift_grad
            gsmall_ref[layer, 5:6] += jnp.sum(grad, 0, keepdims=True)

        each(chunks, middle)

        def attention_back(k):
            gather_wait(2, dmr, layer, k)
            da = mm_nt(dmr[layer, span(k)], wout[layer]).astype(BF16)
            packed = qkv[layer, span(k)]
            queries, keys, values = packed[:, 0:128], packed[:, 128:256], packed[:, 256:384]
            dqs, dks, dvs = [], [], []
            for head, grad in enumerate(heads(da)):
                p = prob[layer, k, head]
                dvs.append(mm_tn(p.astype(BF16), da))
                dp = mm_nt(grad, values)
                ds = p * (dp - jnp.sum(p * dp, -1, keepdims=True))
                ds = ds.astype(BF16)
                dqs.append(mm(ds, keys))
                dks.append(mm_tn(ds, queries))
            grads = jnp.concatenate(
                [
                    jnp.where(left_half, dqs[0], dqs[1]) * SCALE,
                    jnp.where(left_half, dks[0], dks[1]) * SCALE,
                    jnp.where(left_half, dvs[0], dvs[1]),
                ],
                1,
            ).astype(BF16)
            dqkv[span(k)] = grads
            part[ph + 1, span(k)] = mm_nt(grads, wqkv[layer]).astype(BF16)
            scatter_start(ph + 1, k)
            gbias_ref[layer, 0:1, 0:384] += jnp.sum(grads.astype(F32), 0, keepdims=True)

        each(chunks, attention_back)

        gout_ref[layer] = mm_tn(mix[layer], dmr[layer]).astype(BF16)

        def grad_qkv(b):
            cols = pl.ds(pl.multiple_of(b * 256, 256), 256)
            gqkv_ref[layer, cols] = mm_tn(n1[layer, :, cols], dqkv[...]).astype(BF16)

        each(4, grad_qkv)

        def finish(k):
            slope, gain_grad, shift_grad = norm_back(
                hrow[layer, k], vec[layer, 0:1], scatter_finish(ph + 1, k)
            )
            rows = mrow[layer, k] + slope

            @pl.when(layer == 1)
            def _():
                dyr[0, mine(k, t)] = rows.astype(BF16)
                gather_start(3, dyr, 0, k)

            emit(1, layer, k, rows)
            gsmall_ref[layer, 0:1] += gain_grad
            gsmall_ref[layer, 2:3] += shift_grad

        each(chunks, finish)

    each(2, backward)

    for i, (own, both) in enumerate(weights):
        pltpu.make_async_copy(both.at[0], both.at[0], wsend.at[i]).wait()
    for ph in range(8):
        pltpu.make_async_copy(rs.at[ph], rs.at[ph], rsend.at[ph]).wait()
    for which, buf, layer in (
        (0, n1, 1),
        (1, n2, 0),
        (1, n2, 1),
        (2, dmr, 0),
        (2, dmr, 1),
        (3, dyr, 0),
    ):
        view = rs.at[0]
        pltpu.make_async_copy(view, view, gsend.at[which, layer]).wait()
    for kind in range(2):
        for layer in range(2):

            @pl.when(c == layer)
            def _():
                view = ostage.at[kind, layer, :, pl.ds(0, T - 1)]
                pltpu.make_async_copy(view, view, osend.at[kind, layer]).wait()

            @pl.when(c != layer)
            def _():
                view = ostage.at[kind, layer]
                pltpu.make_async_copy(view, view, osend.at[kind, layer]).wait()

    for kind, out in enumerate((sec_ref, ing_ref)):
        pltpu.make_async_copy(obuf.at[kind], obuf.at[kind], osem.at[kind]).wait()
        out[...] = obuf[kind].astype(F32)


def core(chunks, x, ct, mask, wqkv, wout, w1, w2, vec):
    n = chunks * ROWS
    vm = pl.BlockSpec(memory_space=pltpu.VMEM)
    hbm = pl.BlockSpec(memory_space=pl.ANY)
    out_shape = (
        jax.ShapeDtypeStruct((2 * n, 128), F32),
        jax.ShapeDtypeStruct((2 * n, 128), F32),
        jax.ShapeDtypeStruct((2, D, 384), BF16),
        jax.ShapeDtypeStruct((2, 128, D), BF16),
        jax.ShapeDtypeStruct((2, D, 512), BF16),
        jax.ShapeDtypeStruct((2, 512, D), BF16),
        jax.ShapeDtypeStruct((2, 8, D), F32),
        jax.ShapeDtypeStruct((2, 1, 896), F32),
    )
    dma = pltpu.SemaphoreType.DMA
    scratch = [
        pltpu.VMEM((2, D, 384), BF16),
        pltpu.VMEM((2, 128, D), BF16),
        pltpu.VMEM((2, D, 512), BF16),
        pltpu.VMEM((2, 512, D), BF16),
        pltpu.VMEM((2, 8, D), F32),
        pltpu.VMEM((2, n, D), BF16),
        pltpu.VMEM((2, n, D), BF16),
        pltpu.VMEM((2, n, D), BF16),
        pltpu.VMEM((2, n, D), BF16),
        pltpu.VMEM((2, n, 384), BF16),
        pltpu.VMEM((2, n, 128), BF16),
        pltpu.VMEM((2, chunks, 2, ROWS, ROWS), F32),
        pltpu.VMEM((2, n, 512), F32),
        pltpu.VMEM((2, n, 512), BF16),
        pltpu.VMEM((n, 512), BF16),
        pltpu.VMEM((n, 384), BF16),
        pltpu.VMEM((2, chunks, OWN, D), F32),
        pltpu.VMEM((2, chunks, OWN, D), F32),
        pltpu.VMEM((8, n, D), BF16),
        pltpu.VMEM((8, chunks, T - 1, OWN, D), BF16),
        pltpu.VMEM((2, 2, chunks, T, OWN, 128), BF16),
        pltpu.VMEM((2, 2 * n, 128), BF16),
        dma((5, 2)),
        dma((5,)),
        dma((8, chunks)),
        dma((8,)),
        dma((4, 2, chunks)),
        dma((4, 2)),
        dma((2,)),
        dma((2, 2)),
    ]
    return pl.pallas_call(
        functools.partial(kernel, chunks),
        out_shape=out_shape,
        in_specs=[vm, vm, vm, hbm, hbm, hbm, hbm, hbm],
        out_specs=[vm] * 8,
        scratch_shapes=scratch,
        compiler_params=pltpu.CompilerParams(
            collective_id=0, has_side_effects=True, vmem_limit_bytes=62 * 2**20
        ),
        name="layers",
    )(x, ct, mask, wqkv, wout, w1, w2, vec)


def shards(
    inputs,
    cotangent,
    doc_ids,
    qkv_weight,
    qkv_bias,
    out_weight,
    fc1_weight,
    fc1_bias,
    fc2_weight,
    norm_gains,
    shifts,
):
    c = lax.axis_index("pipe")
    t = lax.axis_index("tensor")
    n_dp = lax.axis_size("dp")
    chunks = doc_ids.shape[0] // 2
    n = chunks * ROWS
    x = lax.dynamic_slice_in_dim(inputs, c * n, n, 0)
    ct = lax.dynamic_slice_in_dim(cotangent, c * n, n, 0)
    docs = lax.dynamic_slice_in_dim(doc_ids, c * chunks, chunks, 0)
    place = jnp.arange(ROWS)
    visible = (place[None, :] <= place[:, None])[None] & (docs[:, :, None] == docs[:, None, :])
    mask = visible.astype(F32).reshape(n, ROWS)
    bias = jnp.concatenate([qkv_bias[0, 0], jnp.zeros_like(qkv_bias[0, 0]), qkv_bias[0, 1]])
    vec = jnp.concatenate(
        [
            norm_gains[0],
            shifts[0],
            jnp.pad(bias, (0, D - 384))[None],
            jnp.pad(fc1_bias[0], (0, D - 512))[None],
        ],
        0,
    ).astype(F32)
    sec, ing, gqkv, gout, g1, g2, gsmall, gbias = core(
        chunks,
        x,
        ct,
        mask,
        qkv_weight[0].reshape(D, 384),
        out_weight[0],
        fc1_weight[0],
        fc2_weight[0],
        vec,
    )
    m = n_dp
    packed = jnp.concatenate(
        [
            gqkv.reshape(2, m, -1),
            gout.reshape(2, 128, m, D // m).transpose(0, 2, 1, 3).reshape(2, m, -1),
            g1.reshape(2, m, -1),
            g2.reshape(2, 512, m, D // m).transpose(0, 2, 1, 3).reshape(2, m, -1),
        ],
        2,
    )
    own = lax.dynamic_index_in_dim(packed, c, 0, False)
    away = lax.dynamic_index_in_dim(packed, 1 - c, 0, False)
    came = lax.ppermute(away, "pipe", [(0, 1), (1, 0)])
    total = (own.astype(F32) + came.astype(F32)).astype(BF16)
    total = lax.psum_scatter(total, "dp", scatter_dimension=0, tiled=True).astype(F32)[0]
    sizes = [D * 384 // m, 128 * D // m, D * 512 // m, 512 * D // m]
    edges = [0]
    for size in sizes:
        edges.append(edges[-1] + size)
    pieces = [total[a:b] for a, b in zip(edges[:-1], edges[1:])]
    wide = jnp.zeros((2, T, 896), F32)
    wide = lax.dynamic_update_slice(wide, gbias.reshape(2, 1, 896), (0, t, 0))
    tiny = jnp.concatenate([gsmall[:, :6].reshape(2, -1), wide.reshape(2, -1)], 1)
    tiny = lax.psum(tiny, ("pipe", "tensor", "dp"))
    tiny = lax.dynamic_index_in_dim(tiny, c, 0, False)
    small = tiny[: 6 * D].reshape(6, D)
    share = D // (T * m)
    place = (t * m + lax.axis_index("dp")) * share
    small = lax.dynamic_slice_in_dim(small, place, share, 1)
    wide = tiny[6 * D :].reshape(T, 896)
    wide = lax.dynamic_index_in_dim(wide, t, 0, False)
    step = lax.axis_index("dp")
    qb = jnp.stack([wide[0:128], wide[256:384]])
    qb = lax.dynamic_slice_in_dim(qb, step * (128 // m), 128 // m, 1)
    ub = lax.dynamic_slice_in_dim(wide[384:896], step * (512 // m), 512 // m, 0)
    return (
        sec[None],
        ing[None],
        pieces[0].reshape(1, D // m, 3, 128),
        qb[None],
        pieces[1].reshape(1, 128, D // m),
        pieces[2].reshape(1, D // m, 512),
        ub[None],
        pieces[3].reshape(1, 512, D // m),
        small[None, 0:2],
        small[None, 2:6],
    )


def solution(mesh):
    return jax.shard_map(
        shards,
        mesh=mesh,
        in_specs=(
            P("dp", None),
            P("dp", None),
            P("dp", None),
            P("pipe", None, None, "tensor"),
            P("pipe", None, "tensor"),
            P("pipe", "tensor", None),
            P("pipe", None, "tensor"),
            P("pipe", "tensor"),
            P("pipe", "tensor", None),
            P("pipe", None, None),
            P("pipe", None, None),
        ),
        out_specs=(
            P("pipe", "dp", "tensor"),
            P("pipe", "dp", "tensor"),
            P("pipe", "dp", None, "tensor"),
            P("pipe", None, ("tensor", "dp")),
            P("pipe", "tensor", "dp"),
            P("pipe", "dp", "tensor"),
            P("pipe", ("tensor", "dp")),
            P("pipe", "tensor", "dp"),
            P("pipe", None, ("tensor", "dp")),
            P("pipe", None, ("tensor", "dp")),
        ),
        check_vma=False,
    )
```

```python
import functools

import jax
import jax.numpy as jnp
from jax import lax
from jax.experimental import pallas as pl
from jax.experimental.pallas import tpu as pltpu
from jax.sharding import PartitionSpec as P

MESH = pl.DeviceIdType.MESH
F32 = jnp.float32
BF16 = jnp.bfloat16
EPSILON = 1e-05
HD = 64
SCALE = HD**-0.5
D = 1024
ROWS = 128
T = 8
Y = 4
OWN = ROWS // T
GELU_C = 0.7978845608028654
GELU_A = 0.044715


def mm(a, b):
    return lax.dot_general(a, b, (((1,), (0,)), ((), ())), preferred_element_type=F32)


def mm_nt(a, b):
    return lax.dot_general(a, b, (((1,), (1,)), ((), ())), preferred_element_type=F32)


def mm_tn(a, b):
    return lax.dot_general(a, b, (((0,), (0,)), ((), ())), preferred_element_type=F32)


def standardize(rows):
    centered = rows - jnp.mean(rows, -1, keepdims=True)
    variance = jnp.mean(centered * centered, -1, keepdims=True)
    root = lax.rsqrt(variance + EPSILON)
    return centered * root, root


def norm_back(rows, gain, grad):
    unit, root = standardize(rows)
    e = grad * gain
    slope = root * (
        e - jnp.mean(e, -1, keepdims=True) - unit * jnp.mean(e * unit, -1, keepdims=True)
    )
    return slope, jnp.sum(grad * unit, 0, keepdims=True), jnp.sum(grad, 0, keepdims=True)


def kernel(
    chunks,
    nz,
    x_ref,
    ct_ref,
    mask_ref,
    wqkv_in,
    wout_in,
    w1_in,
    w2_in,
    vec_in,
    sec_ref,
    ing_ref,
    gqkv_ref,
    gout_ref,
    g1_ref,
    g2_ref,
    gsmall_ref,
    gbias_ref,
    wqkv,
    wout,
    w1,
    w2,
    vec,
    n1,
    n2,
    dmr,
    dyr,
    qkv,
    mix,
    prob,
    up,
    act,
    dup,
    dqkv,
    hrow,
    mrow,
    part,
    cbuf,
    psum,
    rs,
    ostage,
    obuf,
    gbufs,
    zrs,
    zsums,
    xrs,
    gpack,
    tsum,
    tr,
    wsem,
    wsend,
    wrelay,
    vsem,
    vsend,
    csem,
    csend,
    rsem,
    rsend,
    gsem,
    gsend,
    hsem,
    hsend,
    osem,
    osend,
    zsem,
    zsend,
    xsem,
    xsend,
    tsem,
    tsend,
):
    c = lax.axis_index("pipe")
    t = lax.axis_index("tensor")
    d = lax.axis_index("dp")
    xh = t // Y
    y = lax.rem(t, Y)
    xl = d // nz
    z = lax.rem(d, nz)
    sib = (1 - c, t, d)

    barrier = pltpu.get_barrier_semaphore()

    def greet(device):
        pl.semaphore_signal(barrier, inc=1, device_id=device, device_id_type=MESH)

    for j in range(T):
        other = lax.rem(t + j, T)
        if j:
            greet((c, other, d))
        greet((1 - c, other, d))
    far = (1 - xl) * nz + z
    for core_ in range(2):
        for j in range(2):
            greet((core_, j * Y + y, far))
    for j in range(1, nz):
        greet((c, t, xl * nz + lax.rem(z + j, nz)))
    pl.semaphore_wait(barrier, 2 * T - 1 + 4 + nz - 1)

    def remote(src, dst, send, recv, device):
        pltpu.make_async_remote_copy(
            src_ref=src,
            dst_ref=dst,
            send_sem=send,
            recv_sem=recv,
            device_id=device,
            device_id_type=MESH,
        ).start()

    def await_bytes(view, sem):
        pltpu.make_async_copy(view, view, sem).wait()

    weights = ((wqkv_in, wqkv), (wout_in, wout), (w1_in, w1), (w2_in, w2))
    native = c == xh
    partner = (xh, (1 - xh) * Y + y, far)
    home = (xh, t, d)

    def half(i, which):
        size = weights[i][1].shape[1] // 2
        return pl.ds(pl.multiple_of(which * size, size), size)

    def send_weight(i, whole):
        own, both = weights[i]

        @pl.when(native)
        def _():
            for h in range(2):
                pltpu.make_async_copy(
                    own.at[half(i, h)], both.at[c, half(i, h)], wsem.at[i, c, h]
                ).start()

        @pl.when(jnp.logical_not(native))
        def _():
            for h in range(2):
                remote(
                    own.at[half(i, h)],
                    both.at[c, half(i, h)],
                    wsend.at[i],
                    wsem.at[i, c, h],
                    home,
                )

        for h in (0, 1) if whole else (xl,):
            remote(
                own.at[half(i, h)],
                both.at[c, half(i, h)],
                wsend.at[i],
                wsem.at[i, c, h],
                partner,
            )

    def await_half(i, layer, h):
        await_bytes(weights[i][1].at[layer, half(i, h)], wsem.at[i, layer, h])

    def relay(i, layer):
        both = weights[i][1]

        @pl.when(jnp.logical_not(native))
        def _():
            await_half(i, layer, 1 - xl)
            piece = both.at[layer, half(i, 1 - xl)]
            remote(piece, piece, wrelay.at[i, layer], wsem.at[i, layer, 1 - xl], (c, t, far))

    def need(i, layer, whole=False):
        if whole:
            await_half(i, layer, 0)
            await_half(i, layer, 1)
        else:

            @pl.when(native)
            def _():
                await_half(i, layer, 1 - xl)

            await_half(i, layer, xl)

    def span(k):
        return pl.ds(pl.multiple_of(k * ROWS, ROWS), ROWS)

    def side(k, who):
        return pl.ds(pl.multiple_of(k * ROWS + who * (ROWS // 2), ROWS // 2), ROWS // 2)

    own_start = (c * Y + y) * OWN

    def mine(k):
        return pl.ds(pl.multiple_of(k * ROWS + own_start, OWN), OWN)

    def y_peer(j):
        return (c, xh * Y + lax.rem(y + j, Y), d)

    def reduce_start(ph, k):
        remote(
            part.at[ph, side(k, 1 - c)], cbuf.at[ph, k], csend.at[ph], csem.at[ph, k], sib
        )

    def reduce_middle(ph, k):
        await_bytes(cbuf.at[ph, k], csem.at[ph, k])
        psum[ph, k] = (part[ph, side(k, c)].astype(F32) + cbuf[ph, k].astype(F32)).astype(BF16)
        for j in range(1, Y):
            rows = pl.ds(pl.multiple_of(lax.rem(y + j, Y) * OWN, OWN), OWN)
            remote(
                psum.at[ph, k, rows], rs.at[ph, k, j - 1], rsend.at[ph], rsem.at[ph, k], y_peer(j)
            )

    def reduce_finish(ph, k):
        await_bytes(rs.at[ph, k], rsem.at[ph, k])
        rows = pl.ds(pl.multiple_of(y * OWN, OWN), OWN)
        total = psum[ph, k, rows].astype(F32)
        for j in range(Y - 1):
            total = total + rs[ph, k, j].astype(F32)
        return total

    def gather_start(which, buf, layer, k):
        for j in range(1, Y):
            view = buf.at[layer, mine(k)]
            remote(view, view, gsend.at[which, layer], gsem.at[which, layer, k], y_peer(j))

    def gather_middle(which, buf, layer, k):
        await_bytes(buf.at[layer, pl.ds(0, (Y - 1) * OWN)], gsem.at[which, layer, k])
        view = buf.at[layer, side(k, c)]
        remote(view, view, hsend.at[which, layer], hsem.at[which, layer, k], sib)

    def gather_finish(which, buf, layer, k):
        await_bytes(buf.at[layer, side(k, 1 - c)], hsem.at[which, layer, k])

    def emit(kind, layer, k, rows):
        low = rows.astype(BF16)
        for j in range(T):
            ostage[kind, layer, k, j] = low[:, j * 128 : (j + 1) * 128]
        first = xh * (chunks * ROWS) + k * ROWS + own_start
        target = pl.ds(pl.multiple_of(first, OWN), OWN)

        def away(j):
            other = lax.rem(t + j, T)
            remote(
                ostage.at[kind, layer, k, other],
                obuf.at[kind, target],
                osend.at[kind, layer],
                osem.at[kind],
                (layer, other, d),
            )

        for j in range(1, T):
            away(j)

        @pl.when(c == layer)
        def _():
            pltpu.make_async_copy(
                ostage.at[kind, layer, k, t], obuf.at[kind, target], osem.at[kind]
            ).start()

        @pl.when(c != layer)
        def _():
            away(0)

    slot = xh * 2 + xl

    def x_send(m, layer, source):
        for to in range(2):
            self_ = jnp.logical_and(jnp.logical_and(c == layer, native), xl == to)
            src, dst = source(to), xrs[m].at[slot]

            @pl.when(self_)
            def _():
                pltpu.make_async_copy(src, dst, xsem.at[m]).start()

            @pl.when(jnp.logical_not(self_))
            def _():
                remote(
                    src, dst, xsend.at[m, layer], xsem.at[m], (layer, c * Y + y, to * nz + z)
                )

    def z_peer(j):
        return (c, t, xl * nz + lax.rem(z + j, nz))

    def z_first_start(m, layer):
        for j in range(1, nz):
            for to in range(2):
                remote(
                    gbufs[m].at[layer, to * nz + lax.rem(z + j, nz)],
                    zrs[m].at[layer, j - 1, to],
                    zsend.at[m, layer],
                    zsem.at[m, layer],
                    z_peer(j),
                )

    def z_first_middle(m, layer):
        if nz > 1:
            await_bytes(zrs[m].at[layer], zsem.at[m, layer])
        for to in range(2):
            total = gbufs[m][layer, to * nz + z].astype(F32)
            for j in range(nz - 1):
                total = total + zrs[m][layer, j, to].astype(F32)
            zsums[m][layer, to] = total.astype(BF16)
        x_send(m, layer, lambda to: zsums[m].at[layer, to])

    def z_first_finish(m):
        await_bytes(xrs[m], xsem.at[m])
        return sum4(m)

    def sum4(m):
        total = xrs[m][0].astype(F32)
        for j in range(1, 4):
            total = total + xrs[m][j].astype(F32)
        return total

    def x_first_start(m, layer):
        x_send(m, layer, lambda to: gbufs[m].at[layer, pl.ds(to * nz, nz)])

    def x_first_middle(m):
        await_bytes(xrs[m], xsem.at[m])
        zsums[m][...] = sum4(m).astype(BF16)
        for j in range(1, nz):
            remote(
                zsums[m].at[lax.rem(z + j, nz)],
                zrs[m].at[j - 1],
                zsend.at[m, 0],
                zsem.at[m, 0],
                z_peer(j),
            )

    def x_first_finish(m):
        total = zsums[m][z].astype(F32)
        if nz > 1:
            await_bytes(zrs[m], zsem.at[m, 0])
        for j in range(nz - 1):
            total = total + zrs[m][j].astype(F32)
        return total

    left_half = lax.broadcasted_iota(jnp.int32, (ROWS, 128), 1) < HD

    def heads(value):
        zero = jnp.zeros_like(value)
        return jnp.where(left_half, value, zero), jnp.where(left_half, zero, value)

    def each(count, body):
        def step(i, carry):
            body(i)
            return carry

        lax.fori_loop(0, count, step, 0)

    def flow(before, work, after):
        def step(s):
            @pl.when(s < chunks)
            def _():
                before(s)

            @pl.when(jnp.logical_and(s >= 1, s < chunks + 1))
            def _():
                work(s - 1)

            @pl.when(s >= 2)
            def _():
                after(s - 2)

        each(chunks + 2, step)

    @pl.when(native)
    def _():
        pltpu.make_async_copy(vec_in, vec.at[c], vsem.at[c]).start()

    @pl.when(jnp.logical_not(native))
    def _():
        remote(vec_in, vec.at[c], vsend.at[0], vsem.at[c], home)

    remote(vec_in, vec.at[c], vsend.at[0], vsem.at[c], partner)

    @pl.when(c == 0)
    def _():
        send_weight(0, True)
        send_weight(1, True)

    await_bytes(vec.at[0], vsem.at[0])
    await_bytes(vec.at[1], vsem.at[1])
    gpack[...] = jnp.zeros_like(gpack)

    def start(k):
        unit, _ = standardize(x_ref[span(k)].astype(F32))
        n1[0, span(k)] = (unit * vec[0, 0:1] + vec[0, 2:3]).astype(BF16)
        hrow[0, k] = x_ref[mine(k)].astype(F32)
        dyr[1, span(k)] = ct_ref[span(k)]

    each(chunks, start)

    def forward(layer):
        ph = layer * 2

        @pl.when(layer == 0)
        def _():
            need(0, 0, True)

            @pl.when(c == 0)
            def _():
                send_weight(2, False)
                send_weight(3, False)

            need(1, 0, True)

        @pl.when(layer == 1)
        def _():
            need(0, 1)
            need(1, 1)

        def arrive(k):
            @pl.when(layer == 1)
            def _():
                gather_middle(0, n1, 1, k)

        def attention(k):
            @pl.when(layer == 1)
            def _():
                gather_finish(0, n1, 1, k)

            packed = mm(n1[layer, span(k)], wqkv[layer]) + vec[layer, 6:7, 0:384]
            packed = packed.astype(BF16)
            qkv[layer, span(k)] = packed
            queries, keys, values = packed[:, 0:128], packed[:, 128:256], packed[:, 256:384]
            visible = mask_ref[span(k)] > 0
            parts = []
            for head, query in enumerate(heads(queries)):
                scores = jnp.where(visible, mm_nt(query, keys) * SCALE, -1e30)
                weights_ = jnp.exp(scores - jnp.max(scores, -1, keepdims=True))
                p = weights_ / jnp.sum(weights_, -1, keepdims=True)
                prob[layer, k, head] = p
                parts.append(mm(p.astype(BF16), values))
            mixture = jnp.where(left_half, parts[0], parts[1]).astype(BF16)
            mix[layer, span(k)] = mixture
            part[ph, span(k)] = mm(mixture, wout[layer]).astype(BF16)
            reduce_start(ph, k)

        flow(arrive, attention, lambda k: reduce_middle(ph, k))

        relay(2, layer)

        def second_norm(k):
            rows = hrow[layer, k] + reduce_finish(ph, k) + vec[layer, 3:4]
            mrow[layer, k] = rows
            unit, _ = standardize(rows)
            n2[layer, mine(k)] = (unit * vec[layer, 1:2] + vec[layer, 4:5]).astype(BF16)
            gather_start(1, n2, layer, k)

        each(chunks, second_norm)
        relay(3, layer)
        need(2, layer)
        need(3, layer)

        def feed(k):
            gather_finish(1, n2, layer, k)
            u = mm(n2[layer, span(k)], w1[layer]) + vec[layer, 7:8, 0:512]
            up[layer, span(k)] = u
            g = 0.5 * u * (1.0 + jnp.tanh(GELU_C * (u + GELU_A * (u * u * u))))
            g = g.astype(BF16)
            act[layer, span(k)] = g
            part[ph + 1, span(k)] = mm(g, w2[layer]).astype(BF16)
            reduce_start(ph + 1, k)

        flow(
            lambda k: gather_middle(1, n2, layer, k),
            feed,
            lambda k: reduce_middle(ph + 1, k),
        )

        @pl.when(jnp.logical_and(layer == 0, c == 1))
        def _():
            send_weight(0, False)
            send_weight(1, False)

        def finish(k):
            rows = mrow[layer, k] + reduce_finish(ph + 1, k) + vec[layer, 5:6]

            @pl.when(layer == 0)
            def _():
                entering = rows.astype(BF16).astype(F32)
                hrow[1, k] = entering
                unit, _ = standardize(entering)
                n1[1, mine(k)] = (unit * vec[1, 0:1] + vec[1, 2:3]).astype(BF16)
                gather_start(0, n1, 1, k)

            emit(0, layer, k, rows)

        each(chunks, finish)

        @pl.when(layer == 0)
        def _():
            @pl.when(c == 1)
            def _():
                send_weight(2, False)
                send_weight(3, False)

            relay(0, 1)
            relay(1, 1)

    each(2, forward)

    def backward(i):
        layer = 1 - i
        ph = 4 + layer * 2

        def arrive(k):
            @pl.when(layer == 0)
            def _():
                gather_middle(3, dyr, 0, k)

        def feed_back(k):
            @pl.when(layer == 0)
            def _():
                gather_finish(3, dyr, 0, k)

            grad = mm_nt(dyr[layer, span(k)], w2[layer])
            u = up[layer, span(k)]
            bend = jnp.tanh(GELU_C * (u + GELU_A * (u * u * u)))
            slope = 0.5 * (1.0 + bend) + (0.5 * u) * (1.0 - bend * bend) * (
                GELU_C * (1.0 + (3.0 * GELU_A) * (u * u))
            )
            du = (grad * slope).astype(BF16)
            dup[span(k)] = du
            part[ph, span(k)] = mm_nt(du, w1[layer]).astype(BF16)
            reduce_start(ph, k)
            gpack[layer, 6:7, 384:896] += jnp.sum(du.astype(F32), 0, keepdims=True)

        flow(arrive, feed_back, lambda k: reduce_middle(ph, k))

        pieces = 2 * nz
        wide = D // pieces

        def grad_down(b):
            cols = pl.ds(pl.multiple_of(b * 128, 128), 128)
            block = mm_tn(act[layer, :, cols], dyr[layer]).astype(BF16)
            for q in range(pieces):
                gbufs[0][layer, q, cols] = block[:, q * wide : (q + 1) * wide]

        each(4, grad_down)
        z_first_start(0, layer)

        def middle(k):
            grad = dyr[layer, mine(k)].astype(F32)
            slope, gain_grad, shift_grad = norm_back(
                mrow[layer, k], vec[layer, 1:2], reduce_finish(ph, k)
            )
            dm = grad + slope
            mrow[layer, k] = dm
            low = dm.astype(BF16)
            dmr[layer, mine(k)] = low
            gather_start(2, dmr, layer, k)
            gpack[layer, 1:2] += gain_grad
            gpack[layer, 3:4] += jnp.sum(low.astype(F32), 0, keepdims=True)
            gpack[layer, 4:5] += shift_grad
            gpack[layer, 5:6] += jnp.sum(grad, 0, keepdims=True)

        each(chunks, middle)

        def grad_up(b):
            cols = pl.ds(pl.multiple_of(b * wide, wide), wide)
            gbufs[1][layer, b] = mm_tn(n2[layer, :, cols], dup[...]).astype(BF16)

        each(pieces, grad_up)
        x_first_start(1, layer)

        @pl.when(layer == 0)
        def _():
            collect_attention(1)

        def attention_back(k):
            gather_finish(2, dmr, layer, k)
            da = mm_nt(dmr[layer, span(k)], wout[layer]).astype(BF16)
            packed = qkv[layer, span(k)]
            queries, keys, values = packed[:, 0:128], packed[:, 128:256], packed[:, 256:384]
            dqs, dks, dvs = [], [], []
            for head, grad in enumerate(heads(da)):
                p = prob[layer, k, head]
                dvs.append(mm_tn(p.astype(BF16), da))
                dp = mm_nt(grad, values)
                ds = p * (dp - jnp.sum(p * dp, -1, keepdims=True))
                ds = ds.astype(BF16)
                dqs.append(mm(ds, keys))
                dks.append(mm_tn(ds, queries))
            grads = jnp.concatenate(
                [
                    jnp.where(left_half, dqs[0], dqs[1]) * SCALE,
                    jnp.where(left_half, dks[0], dks[1]) * SCALE,
                    jnp.where(left_half, dvs[0], dvs[1]),
                ],
                1,
            ).astype(BF16)
            dqkv[span(k)] = grads
            part[ph + 1, span(k)] = mm_nt(grads, wqkv[layer]).astype(BF16)
            reduce_start(ph + 1, k)
            gpack[layer, 6:7, 0:384] += jnp.sum(grads.astype(F32), 0, keepdims=True)

        flow(
            lambda k: gather_middle(2, dmr, layer, k),
            attention_back,
            lambda k: reduce_middle(ph + 1, k),
        )

        block = mm_tn(mix[layer], dmr[layer]).astype(BF16)
        for q in range(pieces):
            gbufs[4][layer, q] = block[:, q * wide : (q + 1) * wide]
        x_first_start(4, layer)

        def grad_qkv(b):
            cols = pl.ds(pl.multiple_of(b * wide, wide), wide)
            block = mm_tn(n1[layer, :, cols], dqkv[...]).astype(BF16)
            gbufs[2][layer, b] = block[:, 0:256]
            gbufs[3][layer, b] = block[:, 256:384]

        each(pieces, grad_qkv)
        z_first_start(2, layer)
        x_first_start(3, layer)

        def finish(k):
            slope, gain_grad, shift_grad = norm_back(
                hrow[layer, k], vec[layer, 0:1], reduce_finish(ph + 1, k)
            )
            rows = mrow[layer, k] + slope

            @pl.when(layer == 1)
            def _():
                dyr[0, mine(k)] = rows.astype(BF16)
                gather_start(3, dyr, 0, k)

            emit(1, layer, k, rows)
            gpack[layer, 0:1] += gain_grad
            gpack[layer, 2:3] += shift_grad

        each(chunks, finish)
        x_send(5, layer, lambda to: gpack.at[layer])
        z_first_middle(0, layer)

        @pl.when(c == layer)
        def _():
            x_first_middle(1)

    def collect_attention(layer):
        @pl.when(c == layer)
        def _():
            x_first_middle(4)
            x_first_middle(3)

        z_first_middle(2, layer)

        @pl.when(c == layer)
        def _():
            await_bytes(xrs[5], xsem.at[5])
            zsums[5][...] = sum4(5)
            for j in range(1, nz):
                remote(zsums[5], zrs[5].at[j - 1], zsend.at[5, 0], zsem.at[5, 0], z_peer(j))

    each(2, backward)
    collect_attention(0)

    total = zsums[5][...]
    if nz > 1:
        await_bytes(zrs[5], zsem.at[5, 0])
    for j in range(nz - 1):
        total = total + zrs[5][j]
    for j in range(T):
        tsum[j] = total[:, j * 128 : (j + 1) * 128]
    gbias_ref[...] = total
    for j in range(1, T):
        other = lax.rem(t + j, T)
        remote(tsum.at[other], tr.at[j - 1], tsend.at[0], tsem.at[0], (c, other, d))

    g1_ref[...] = x_first_finish(1)
    gout_ref[...] = x_first_finish(4)
    gqkv_ref[:, 256:384] = x_first_finish(3)
    g2_ref[...] = z_first_finish(0)
    gqkv_ref[:, 0:256] = z_first_finish(2)
    await_bytes(tr, tsem.at[0])
    small = tsum[t]
    for j in range(T - 1):
        small = small + tr[j]
    gsmall_ref[...] = small
    for kind, out in enumerate((sec_ref, ing_ref)):
        await_bytes(obuf.at[kind], osem.at[kind])
        out[...] = obuf[kind].astype(F32)

    for i in range(4):
        both = weights[i][1]
        early = i < 2

        @pl.when(jnp.logical_not(native))
        def _():
            await_bytes(both.at[0], wsend.at[i])
            for layer in range(2):
                if layer or not early:
                    await_bytes(both.at[0, half(i, 0)], wrelay.at[i, layer])

        await_bytes(both.at[0, half(i, 0)], wsend.at[i])
        if early:

            @pl.when(c == 0)
            def _():
                await_bytes(both.at[0, half(i, 0)], wsend.at[i])

    @pl.when(jnp.logical_not(native))
    def _():
        await_bytes(vec.at[0], vsend.at[0])

    await_bytes(vec.at[0], vsend.at[0])
    for ph in range(8):
        await_bytes(cbuf.at[ph], csend.at[ph])
        await_bytes(rs.at[ph], rsend.at[ph])
    for which, layer in ((0, 1), (1, 0), (1, 1), (2, 0), (2, 1), (3, 0)):
        await_bytes(rs.at[0], gsend.at[which, layer])
        await_bytes(cbuf.at[0], hsend.at[which, layer])
    for layer in range(2):
        for kind in range(2):

            @pl.when(c == layer)
            def _():
                view = ostage.at[kind, layer, :, pl.ds(0, T - 1)]
                await_bytes(view, osend.at[kind, layer])

            @pl.when(c != layer)
            def _():
                await_bytes(ostage.at[kind, layer], osend.at[kind, layer])

        self_ = jnp.logical_and(c == layer, native)
        for m in range(6):
            if nz > 1 and m in (0, 2):
                await_bytes(zrs[m].at[layer], zsend.at[m, layer])
            await_bytes(xrs[m].at[0], xsend.at[m, layer])

            @pl.when(jnp.logical_not(self_))
            def _():
                await_bytes(xrs[m].at[0], xsend.at[m, layer])

    if nz > 1:
        for m in (1, 3, 4, 5):
            await_bytes(zrs[m], zsend.at[m, 0])
    await_bytes(tr, tsend.at[0])


def core(chunks, nz, x, ct, mask, wqkv, wout, w1, w2, vec):
    n = chunks * ROWS
    vm = pl.BlockSpec(memory_space=pltpu.VMEM)
    hbm = pl.BlockSpec(memory_space=pl.ANY)
    pieces = 2 * nz
    wide = D // pieces
    out_shape = (
        jax.ShapeDtypeStruct((2 * n, 128), F32),
        jax.ShapeDtypeStruct((2 * n, 128), F32),
        jax.ShapeDtypeStruct((wide, 384), F32),
        jax.ShapeDtypeStruct((128, wide), F32),
        jax.ShapeDtypeStruct((wide, 512), F32),
        jax.ShapeDtypeStruct((512, wide), F32),
        jax.ShapeDtypeStruct((8, 128), F32),
        jax.ShapeDtypeStruct((8, D), F32),
    )
    dma = pltpu.SemaphoreType.DMA
    shape = ((512, wide), (wide, 512), (wide, 256), (wide, 128), (128, wide))
    back = max(nz - 1, 1)
    gbufs = [pltpu.VMEM((2, pieces) + s, BF16) for s in shape]
    zrs, zsums, xrs = [], [], []
    for m, s in enumerate(shape):
        if m in (0, 2):
            zrs.append(pltpu.VMEM((2, back, 2) + s, BF16))
            zsums.append(pltpu.VMEM((2, 2) + s, BF16))
            xrs.append(pltpu.VMEM((4,) + s, BF16))
        else:
            zrs.append(pltpu.VMEM((back,) + s, BF16))
            zsums.append(pltpu.VMEM((nz,) + s, BF16))
            xrs.append(pltpu.VMEM((4, nz) + s, BF16))
    zrs.append(pltpu.VMEM((back, 8, D), F32))
    zsums.append(pltpu.VMEM((8, D), F32))
    xrs.append(pltpu.VMEM((4, 8, D), F32))
    scratch = [
        pltpu.VMEM((2, D, 384), BF16),
        pltpu.VMEM((2, 128, D), BF16),
        pltpu.VMEM((2, D, 512), BF16),
        pltpu.VMEM((2, 512, D), BF16),
        pltpu.VMEM((2, 8, D), F32),
        pltpu.VMEM((2, n, D), BF16),
        pltpu.VMEM((2, n, D), BF16),
        pltpu.VMEM((2, n, D), BF16),
        pltpu.VMEM((2, n, D), BF16),
        pltpu.VMEM((2, n, 384), BF16),
        pltpu.VMEM((2, n, 128), BF16),
        pltpu.VMEM((2, chunks, 2, ROWS, ROWS), F32),
        pltpu.VMEM((2, n, 512), F32),
        pltpu.VMEM((2, n, 512), BF16),
        pltpu.VMEM((n, 512), BF16),
        pltpu.VMEM((n, 384), BF16),
        pltpu.VMEM((2, chunks, OWN, D), F32),
        pltpu.VMEM((2, chunks, OWN, D), F32),
        pltpu.VMEM((8, n, D), BF16),
        pltpu.VMEM((8, chunks, ROWS // 2, D), BF16),
        pltpu.VMEM((8, chunks, ROWS // 2, D), BF16),
        pltpu.VMEM((8, chunks, Y - 1, OWN, D), BF16),
        pltpu.VMEM((2, 2, chunks, T, OWN, 128), BF16),
        pltpu.VMEM((2, 2 * n, 128), BF16),
        gbufs,
        zrs,
        zsums,
        xrs,
        pltpu.VMEM((2, 8, D), F32),
        pltpu.VMEM((T, 8, 128), F32),
        pltpu.VMEM((T - 1, 8, 128), F32),
        dma((4, 2, 2)),
        dma((4,)),
        dma((4, 2)),
        dma((2,)),
        dma((1,)),
        dma((8, chunks)),
        dma((8,)),
        dma((8, chunks)),
        dma((8,)),
        dma((4, 2, chunks)),
        dma((4, 2)),
        dma((4, 2, chunks)),
        dma((4, 2)),
        dma((2,)),
        dma((2, 2)),
        dma((6, 2)),
        dma((6, 2)),
        dma((6,)),
        dma((6, 2)),
        dma((1,)),
        dma((1,)),
    ]
    return pl.pallas_call(
        functools.partial(kernel, chunks, nz),
        out_shape=out_shape,
        in_specs=[vm, vm, vm, hbm, hbm, hbm, hbm, hbm],
        out_specs=[vm] * 8,
        scratch_shapes=scratch,
        compiler_params=pltpu.CompilerParams(
            collective_id=0, has_side_effects=True, vmem_limit_bytes=62 * 2**20
        ),
        name="layers",
    )(x, ct, mask, wqkv, wout, w1, w2, vec)


def shards(
    inputs,
    cotangent,
    doc_ids,
    qkv_weight,
    qkv_bias,
    out_weight,
    fc1_weight,
    fc1_bias,
    fc2_weight,
    norm_gains,
    shifts,
):
    t = lax.axis_index("tensor")
    step = lax.axis_index("dp")
    m = lax.axis_size("dp")
    chunks = doc_ids.shape[0] // 2
    n = chunks * ROWS
    xh = t // Y
    x = lax.dynamic_slice_in_dim(inputs, xh * n, n, 0)
    ct = lax.dynamic_slice_in_dim(cotangent, xh * n, n, 0)
    docs = lax.dynamic_slice_in_dim(doc_ids, xh * chunks, chunks, 0)
    place = jnp.arange(ROWS)
    visible = (place[None, :] <= place[:, None])[None] & (docs[:, :, None] == docs[:, None, :])
    mask = visible.astype(F32).reshape(n, ROWS)
    bias = jnp.concatenate([qkv_bias[0, 0], jnp.zeros_like(qkv_bias[0, 0]), qkv_bias[0, 1]])
    vec = jnp.concatenate(
        [
            norm_gains[0],
            shifts[0],
            jnp.pad(bias, (0, D - 384))[None],
            jnp.pad(fc1_bias[0], (0, D - 512))[None],
        ],
        0,
    ).astype(F32)
    sec, ing, gqkv, gout, g1, g2, gsmall, gbias = core(
        chunks,
        m // 2,
        x,
        ct,
        mask,
        qkv_weight[0].reshape(D, 384),
        out_weight[0],
        fc1_weight[0],
        fc2_weight[0],
        vec,
    )
    share = D // (T * m)
    small = lax.dynamic_slice_in_dim(gsmall, step * share, share, 1)
    bias_row = gbias[6]
    qb = jnp.stack([bias_row[0:128], bias_row[256:384]])
    qb = lax.dynamic_slice_in_dim(qb, step * (128 // m), 128 // m, 1)
    ub = lax.dynamic_slice_in_dim(bias_row[384:896], step * (512 // m), 512 // m, 0)
    return (
        sec[None],
        ing[None],
        gqkv.reshape(1, D // m, 3, 128),
        qb[None],
        gout[None],
        g1[None],
        ub[None],
        g2[None],
        small[None, 0:2],
        small[None, 2:6],
    )


def solution(mesh):
    return jax.shard_map(
        shards,
        mesh=mesh,
        in_specs=(
            P("dp", None),
            P("dp", None),
            P("dp", None),
            P("pipe", None, None, "tensor"),
            P("pipe", None, "tensor"),
            P("pipe", "tensor", None),
            P("pipe", None, "tensor"),
            P("pipe", "tensor"),
            P("pipe", "tensor", None),
            P("pipe", None, None),
            P("pipe", None, None),
        ),
        out_specs=(
            P("pipe", "dp", "tensor"),
            P("pipe", "dp", "tensor"),
            P("pipe", "dp", None, "tensor"),
            P("pipe", None, ("tensor", "dp")),
            P("pipe", "tensor", "dp"),
            P("pipe", "dp", "tensor"),
            P("pipe", ("tensor", "dp")),
            P("pipe", "tensor", "dp"),
            P("pipe", None, ("tensor", "dp")),
            P("pipe", None, ("tensor", "dp")),
        ),
        check_vma=False,
    )
```

```python
import functools

import jax
import jax.numpy as jnp
from jax import lax
from jax.experimental import pallas as pl
from jax.experimental.pallas import tpu as pltpu
from jax.sharding import PartitionSpec as P

MESH = pl.DeviceIdType.MESH
F32 = jnp.float32
BF16 = jnp.bfloat16
EPSILON = 1e-05
HD = 64
SCALE = HD**-0.5
D = 1024
ROWS = 128
T = 8
Y = 4
OWN = ROWS // T
GELU_C = 0.7978845608028654
GELU_A = 0.044715


def mm(a, b):
    return lax.dot_general(a, b, (((1,), (0,)), ((), ())), preferred_element_type=F32)


def mm_nt(a, b):
    return lax.dot_general(a, b, (((1,), (1,)), ((), ())), preferred_element_type=F32)


def mm_tn(a, b):
    return lax.dot_general(a, b, (((0,), (0,)), ((), ())), preferred_element_type=F32)


def standardize(rows):
    centered = rows - jnp.mean(rows, -1, keepdims=True)
    variance = jnp.mean(centered * centered, -1, keepdims=True)
    root = lax.rsqrt(variance + EPSILON)
    return centered * root, root


def norm_back(rows, gain, grad):
    unit, root = standardize(rows)
    e = grad * gain
    slope = root * (
        e - jnp.mean(e, -1, keepdims=True) - unit * jnp.mean(e * unit, -1, keepdims=True)
    )
    return slope, jnp.sum(grad * unit, 0, keepdims=True), jnp.sum(grad, 0, keepdims=True)


def kernel(
    chunks,
    nz,
    x_in,
    ct_in,
    docs_ref,
    wqkv_in,
    wout_in,
    w1_in,
    w2_in,
    qb_in,
    b1_in,
    gains_in,
    shifts_in,
    rows_ref,
    gqkv_ref,
    gout_ref,
    g1_ref,
    g2_ref,
    gsmall_ref,
    gbias_ref,
    x_ref,
    mask_ref,
    vec_in,
    wqkv,
    wout,
    w1,
    w2,
    vec,
    n1,
    n2,
    dmr,
    dyr,
    qkv,
    mix,
    prob,
    up,
    act,
    dup,
    dqkv,
    hrow,
    mrow,
    part,
    cbuf,
    psum,
    rs,
    ostage,
    obuf,
    gbufs,
    zrs,
    zsums,
    xrs,
    gpack,
    tsum,
    tr,
    insem,
    wsem,
    wsend,
    whome,
    wrelay,
    vsem,
    vsend,
    csem,
    csend,
    rsem,
    rsend,
    gsem,
    gsend,
    hsem,
    hsend,
    osem,
    osend,
    zsem,
    zsend,
    xsem,
    xsend,
    tsem,
    tsend,
):
    c = lax.axis_index("pipe")
    t = lax.axis_index("tensor")
    d = lax.axis_index("dp")
    xh = t // Y
    y = lax.rem(t, Y)
    xl = d // nz
    z = lax.rem(d, nz)
    sib = (1 - c, t, d)

    first_row = pl.ds(pl.multiple_of(xh * (chunks * ROWS), ROWS), chunks * ROWS)
    x_copy = pltpu.make_async_copy(x_in.at[first_row], x_ref, insem.at[0])
    ct_copy = pltpu.make_async_copy(ct_in.at[first_row], dyr.at[1], insem.at[1])
    x_copy.start()
    ct_copy.start()

    barrier = pltpu.get_barrier_semaphore()

    def greet(device):
        pl.semaphore_signal(barrier, inc=1, device_id=device, device_id_type=MESH)

    for j in range(T):
        other = lax.rem(t + j, T)
        if j:
            greet((c, other, d))
        greet((1 - c, other, d))
    far = (1 - xl) * nz + z
    for core_ in range(2):
        for j in range(2):
            greet((core_, j * Y + y, far))
    for j in range(1, nz):
        greet((c, t, xl * nz + lax.rem(z + j, nz)))
    vec_in[...] = jnp.zeros_like(vec_in)
    vec_in[0:2] = gains_in[0].astype(F32)
    vec_in[2:6] = shifts_in[0].astype(F32)
    vec_in[6:7, 0:128] = qb_in[0, 0:1].astype(F32)
    vec_in[6:7, 256:384] = qb_in[0, 1:2].astype(F32)
    vec_in[7:8, 0:512] = b1_in[...].astype(F32)
    pl.semaphore_wait(barrier, 2 * T - 1 + 4 + nz - 1)

    def remote(src, dst, send, recv, device):
        pltpu.make_async_remote_copy(
            src_ref=src,
            dst_ref=dst,
            send_sem=send,
            recv_sem=recv,
            device_id=device,
            device_id_type=MESH,
        ).start()

    def await_bytes(view, sem):
        pltpu.make_async_copy(view, view, sem).wait()

    weights = ((wqkv_in, wqkv), (wout_in, wout), (w1_in, w1), (w2_in, w2))
    native = c == xh
    partner = (xh, (1 - xh) * Y + y, far)
    home = (xh, t, d)

    def half(i, which):
        size = weights[i][1].shape[1] // 2
        return pl.ds(pl.multiple_of(which * size, size), size)

    def send_weight(i):
        own, both = weights[i]

        @pl.when(native)
        def _():
            for h in range(2):
                pltpu.make_async_copy(
                    own.at[half(i, h)], both.at[c, half(i, h)], wsem.at[i, c, h]
                ).start()

        @pl.when(jnp.logical_not(native))
        def _():
            for h in range(2):
                remote(
                    own.at[half(i, h)],
                    both.at[c, half(i, h)],
                    whome.at[i],
                    wsem.at[i, c, h],
                    home,
                )

        remote(
            own.at[half(i, xl)],
            both.at[c, half(i, xl)],
            wsend.at[i],
            wsem.at[i, c, xl],
            partner,
        )

    def weight_left(i):
        await_bytes(weights[i][1].at[0, half(i, 0)], wsend.at[i])

    def await_half(i, layer, h):
        await_bytes(weights[i][1].at[layer, half(i, h)], wsem.at[i, layer, h])

    def relay(i, layer):
        both = weights[i][1]

        @pl.when(jnp.logical_not(native))
        def _():
            await_half(i, layer, 1 - xl)
            piece = both.at[layer, half(i, 1 - xl)]
            remote(piece, piece, wrelay.at[i, layer], wsem.at[i, layer, 1 - xl], (c, t, far))

    def need(i, layer):
        @pl.when(native)
        def _():
            await_half(i, layer, 1 - xl)

        await_half(i, layer, xl)

    def span(k):
        return pl.ds(pl.multiple_of(k * ROWS, ROWS), ROWS)

    def side(k, who):
        return pl.ds(pl.multiple_of(k * ROWS + who * (ROWS // 2), ROWS // 2), ROWS // 2)

    own_start = (c * Y + y) * OWN

    def mine(k):
        return pl.ds(pl.multiple_of(k * ROWS + own_start, OWN), OWN)

    def y_peer(j):
        return (c, xh * Y + lax.rem(y + j, Y), d)

    def reduce_start(ph, k):
        remote(
            part.at[ph, side(k, 1 - c)], cbuf.at[ph, k], csend.at[ph], csem.at[ph, k], sib
        )

    def reduce_middle(ph, k):
        await_bytes(cbuf.at[ph, k], csem.at[ph, k])
        psum[ph, k] = (part[ph, side(k, c)].astype(F32) + cbuf[ph, k].astype(F32)).astype(BF16)
        for j in range(1, Y):
            rows = pl.ds(pl.multiple_of(lax.rem(y + j, Y) * OWN, OWN), OWN)
            remote(
                psum.at[ph, k, rows], rs.at[ph, k, j - 1], rsend.at[ph], rsem.at[ph, k], y_peer(j)
            )

    def reduce_finish(ph, k):
        await_bytes(rs.at[ph, k], rsem.at[ph, k])
        rows = pl.ds(pl.multiple_of(y * OWN, OWN), OWN)
        total = psum[ph, k, rows].astype(F32)
        for j in range(Y - 1):
            total = total + rs[ph, k, j].astype(F32)
        return total

    def gather_start(which, buf, layer, k):
        for j in range(1, Y):
            view = buf.at[layer, mine(k)]
            remote(view, view, gsend.at[which, layer], gsem.at[which, layer, k], y_peer(j))

    def gather_middle(which, buf, layer, k):
        await_bytes(buf.at[layer, pl.ds(0, (Y - 1) * OWN)], gsem.at[which, layer, k])
        view = buf.at[layer, side(k, c)]
        remote(view, view, hsend.at[which, layer], hsem.at[which, layer, k], sib)

    def gather_finish(which, buf, layer, k):
        await_bytes(buf.at[layer, side(k, 1 - c)], hsem.at[which, layer, k])

    def emit(kind, layer, k, rows):
        low = rows.astype(BF16)
        for j in range(T):
            ostage[kind, layer, k, j] = low[:, j * 128 : (j + 1) * 128]
        first = xh * (chunks * ROWS) + k * ROWS + own_start
        target = pl.ds(pl.multiple_of(first, OWN), OWN)

        def away(j):
            other = lax.rem(t + j, T)
            remote(
                ostage.at[kind, layer, k, other],
                obuf.at[kind, target],
                osend.at[kind, layer],
                osem.at[kind],
                (layer, other, d),
            )

        for j in range(1, T):
            away(j)

        @pl.when(c == layer)
        def _():
            pltpu.make_async_copy(
                ostage.at[kind, layer, k, t], obuf.at[kind, target], osem.at[kind]
            ).start()

        @pl.when(c != layer)
        def _():
            away(0)

    slot = xh * 2 + xl

    def x_send(m, layer, source):
        for to in range(2):
            self_ = jnp.logical_and(jnp.logical_and(c == layer, native), xl == to)
            src, dst = source(to), xrs[m].at[slot]

            @pl.when(self_)
            def _():
                pltpu.make_async_copy(src, dst, xsem.at[m]).start()

            @pl.when(jnp.logical_not(self_))
            def _():
                remote(
                    src, dst, xsend.at[m, layer], xsem.at[m], (layer, c * Y + y, to * nz + z)
                )

    def z_peer(j):
        return (c, t, xl * nz + lax.rem(z + j, nz))

    def z_first_start(m, layer):
        for j in range(1, nz):
            for to in range(2):
                remote(
                    gbufs[m].at[layer, to * nz + lax.rem(z + j, nz)],
                    zrs[m].at[layer, j - 1, to],
                    zsend.at[m, layer],
                    zsem.at[m, layer],
                    z_peer(j),
                )

    def z_first_middle(m, layer):
        if nz > 1:
            await_bytes(zrs[m].at[layer], zsem.at[m, layer])
        for to in range(2):
            total = gbufs[m][layer, to * nz + z].astype(F32)
            for j in range(nz - 1):
                total = total + zrs[m][layer, j, to].astype(F32)
            zsums[m][layer, to] = total.astype(BF16)
        x_send(m, layer, lambda to: zsums[m].at[layer, to])

    def z_first_finish(m):
        await_bytes(xrs[m], xsem.at[m])
        return sum4(m)

    def sum4(m):
        total = xrs[m][0].astype(F32)
        for j in range(1, 4):
            total = total + xrs[m][j].astype(F32)
        return total

    def x_first_start(m, layer):
        x_send(m, layer, lambda to: gbufs[m].at[layer, pl.ds(to * nz, nz)])

    def x_first_middle(m):
        await_bytes(xrs[m], xsem.at[m])
        zsums[m][...] = sum4(m).astype(BF16)
        for j in range(1, nz):
            remote(
                zsums[m].at[lax.rem(z + j, nz)],
                zrs[m].at[j - 1],
                zsend.at[m, 0],
                zsem.at[m, 0],
                z_peer(j),
            )

    def x_first_finish(m):
        total = zsums[m][z].astype(F32)
        if nz > 1:
            await_bytes(zrs[m], zsem.at[m, 0])
        for j in range(nz - 1):
            total = total + zrs[m][j].astype(F32)
        return total

    left_half = lax.broadcasted_iota(jnp.int32, (ROWS, 128), 1) < HD

    def heads(value):
        zero = jnp.zeros_like(value)
        return jnp.where(left_half, value, zero), jnp.where(left_half, zero, value)

    def each(count, body):
        def step(i, carry):
            body(i)
            return carry

        lax.fori_loop(0, count, step, 0)

    def flow(before, work, after):
        def step(s):
            @pl.when(s < chunks)
            def _():
                before(s)

            @pl.when(jnp.logical_and(s >= 1, s < chunks + 1))
            def _():
                work(s - 1)

            @pl.when(s >= 2)
            def _():
                after(s - 2)

        each(chunks + 2, step)

    @pl.when(native)
    def _():
        pltpu.make_async_copy(vec_in, vec.at[c], vsem.at[c]).start()

    @pl.when(jnp.logical_not(native))
    def _():
        remote(vec_in, vec.at[c], vsend.at[0], vsem.at[c], home)

    remote(vec_in, vec.at[c], vsend.at[0], vsem.at[c], partner)

    @pl.when(c == 0)
    def _():
        send_weight(0)
        send_weight(1)

    gpack[...] = jnp.zeros_like(gpack)
    x_copy.wait()
    ct_copy.wait()
    await_bytes(vec.at[0], vsem.at[0])
    await_bytes(vec.at[1], vsem.at[1])
    lanes = lax.broadcasted_iota(jnp.int32, (ROWS, ROWS), 1)
    places = lax.broadcasted_iota(jnp.int32, (ROWS, ROWS), 0)

    def start(k):
        unit, _ = standardize(x_ref[span(k)].astype(F32))
        n1[0, span(k)] = (unit * vec[0, 0:1] + vec[0, 2:3]).astype(BF16)
        hrow[0, k] = x_ref[mine(k)].astype(F32)
        segment = docs_ref[pl.ds(xh * chunks + k, 1)].astype(F32)
        segment = jnp.broadcast_to(segment, (ROWS, ROWS))
        visible = jnp.logical_and(lanes <= places, segment == segment.T)
        mask_ref[span(k)] = jnp.where(visible, 1.0, 0.0)

    each(chunks, start)

    def forward(layer):
        ph = layer * 2

        @pl.when(layer == 0)
        def _():
            relay(0, 0)
            relay(1, 0)

            @pl.when(c == 0)
            def _():
                weight_left(0)
                send_weight(2)

        need(0, layer)
        need(1, layer)

        def arrive(k):
            @pl.when(layer == 1)
            def _():
                gather_middle(0, n1, 1, k)

        def attention(k):
            @pl.when(layer == 1)
            def _():
                gather_finish(0, n1, 1, k)

            packed = mm(n1[layer, span(k)], wqkv[layer]) + vec[layer, 6:7, 0:384]
            packed = packed.astype(BF16)
            qkv[layer, span(k)] = packed
            queries, keys, values = packed[:, 0:128], packed[:, 128:256], packed[:, 256:384]
            visible = mask_ref[span(k)] > 0
            parts = []
            for head, query in enumerate(heads(queries)):
                scores = jnp.where(visible, mm_nt(query, keys) * SCALE, -1e30)
                weights_ = jnp.exp(scores - jnp.max(scores, -1, keepdims=True))
                p = weights_ / jnp.sum(weights_, -1, keepdims=True)
                prob[layer, k, head] = p
                parts.append(mm(p.astype(BF16), values))
            mixture = jnp.where(left_half, parts[0], parts[1]).astype(BF16)
            mix[layer, span(k)] = mixture
            part[ph, span(k)] = mm(mixture, wout[layer]).astype(BF16)
            reduce_start(ph, k)

        flow(arrive, attention, lambda k: reduce_middle(ph, k))

        @pl.when(jnp.logical_and(layer == 0, c == 0))
        def _():
            send_weight(3)

        @pl.when(layer == 0)
        def _():
            relay(2, 0)

        @pl.when(layer == 1)
        def _():
            relay(3, 1)

        def second_norm(k):
            rows = hrow[layer, k] + reduce_finish(ph, k) + vec[layer, 3:4]
            mrow[layer, k] = rows
            unit, _ = standardize(rows)
            n2[layer, mine(k)] = (unit * vec[layer, 1:2] + vec[layer, 4:5]).astype(BF16)
            gather_start(1, n2, layer, k)

        each(chunks, second_norm)

        @pl.when(layer == 0)
        def _():
            relay(3, 0)

            @pl.when(c == 1)
            def _():
                send_weight(0)
                send_weight(1)

        need(2, layer)
        need(3, layer)

        def feed(k):
            gather_finish(1, n2, layer, k)
            u = mm(n2[layer, span(k)], w1[layer]) + vec[layer, 7:8, 0:512]
            up[layer, span(k)] = u
            g = 0.5 * u * (1.0 + jnp.tanh(GELU_C * (u + GELU_A * (u * u * u))))
            g = g.astype(BF16)
            act[layer, span(k)] = g
            part[ph + 1, span(k)] = mm(g, w2[layer]).astype(BF16)
            reduce_start(ph + 1, k)

        flow(
            lambda k: gather_middle(1, n2, layer, k),
            feed,
            lambda k: reduce_middle(ph + 1, k),
        )

        @pl.when(layer == 0)
        def _():
            @pl.when(c == 1)
            def _():
                send_weight(2)

            relay(0, 1)
            relay(1, 1)

        def finish(k):
            rows = mrow[layer, k] + reduce_finish(ph + 1, k) + vec[layer, 5:6]

            @pl.when(layer == 0)
            def _():
                entering = rows.astype(BF16).astype(F32)
                hrow[1, k] = entering
                unit, _ = standardize(entering)
                n1[1, mine(k)] = (unit * vec[1, 0:1] + vec[1, 2:3]).astype(BF16)
                gather_start(0, n1, 1, k)

            emit(0, layer, k, rows)

        each(chunks, finish)

        @pl.when(layer == 0)
        def _():
            @pl.when(c == 1)
            def _():
                send_weight(3)

            relay(2, 1)

    each(2, forward)

    def backward(i):
        layer = 1 - i
        ph = 4 + layer * 2

        def arrive(k):
            @pl.when(layer == 0)
            def _():
                gather_middle(3, dyr, 0, k)

        def feed_back(k):
            @pl.when(layer == 0)
            def _():
                gather_finish(3, dyr, 0, k)

            grad = mm_nt(dyr[layer, span(k)], w2[layer])
            u = up[layer, span(k)]
            bend = jnp.tanh(GELU_C * (u + GELU_A * (u * u * u)))
            slope = 0.5 * (1.0 + bend) + (0.5 * u) * (1.0 - bend * bend) * (
                GELU_C * (1.0 + (3.0 * GELU_A) * (u * u))
            )
            du = (grad * slope).astype(BF16)
            dup[span(k)] = du
            part[ph, span(k)] = mm_nt(du, w1[layer]).astype(BF16)
            reduce_start(ph, k)
            gpack[layer, 6:7, 384:896] += jnp.sum(du.astype(F32), 0, keepdims=True)

        flow(arrive, feed_back, lambda k: reduce_middle(ph, k))

        pieces = 2 * nz
        wide = D // pieces

        def grad_down(b):
            cols = pl.ds(pl.multiple_of(b * 128, 128), 128)
            block = mm_tn(act[layer, :, cols], dyr[layer]).astype(BF16)
            for q in range(pieces):
                gbufs[0][layer, q, cols] = block[:, q * wide : (q + 1) * wide]

        each(4, grad_down)
        z_first_start(0, layer)

        def middle(k):
            grad = dyr[layer, mine(k)].astype(F32)
            slope, gain_grad, shift_grad = norm_back(
                mrow[layer, k], vec[layer, 1:2], reduce_finish(ph, k)
            )
            dm = grad + slope
            mrow[layer, k] = dm
            low = dm.astype(BF16)
            dmr[layer, mine(k)] = low
            gather_start(2, dmr, layer, k)
            gpack[layer, 1:2] += gain_grad
            gpack[layer, 3:4] += jnp.sum(low.astype(F32), 0, keepdims=True)
            gpack[layer, 4:5] += shift_grad
            gpack[layer, 5:6] += jnp.sum(grad, 0, keepdims=True)

        each(chunks, middle)

        def grad_up(b):
            cols = pl.ds(pl.multiple_of(b * wide, wide), wide)
            gbufs[1][layer, b] = mm_tn(n2[layer, :, cols], dup[...]).astype(BF16)

        each(pieces, grad_up)
        x_first_start(1, layer)

        @pl.when(layer == 0)
        def _():
            collect_attention(1)

        def attention_back(k):
            gather_finish(2, dmr, layer, k)
            da = mm_nt(dmr[layer, span(k)], wout[layer]).astype(BF16)
            packed = qkv[layer, span(k)]
            queries, keys, values = packed[:, 0:128], packed[:, 128:256], packed[:, 256:384]
            dqs, dks, dvs = [], [], []
            for head, grad in enumerate(heads(da)):
                p = prob[layer, k, head]
                dvs.append(mm_tn(p.astype(BF16), da))
                dp = mm_nt(grad, values)
                ds = p * (dp - jnp.sum(p * dp, -1, keepdims=True))
                ds = ds.astype(BF16)
                dqs.append(mm(ds, keys))
                dks.append(mm_tn(ds, queries))
            grads = jnp.concatenate(
                [
                    jnp.where(left_half, dqs[0], dqs[1]) * SCALE,
                    jnp.where(left_half, dks[0], dks[1]) * SCALE,
                    jnp.where(left_half, dvs[0], dvs[1]),
                ],
                1,
            ).astype(BF16)
            dqkv[span(k)] = grads
            part[ph + 1, span(k)] = mm_nt(grads, wqkv[layer]).astype(BF16)
            reduce_start(ph + 1, k)
            gpack[layer, 6:7, 0:384] += jnp.sum(grads.astype(F32), 0, keepdims=True)

        flow(
            lambda k: gather_middle(2, dmr, layer, k),
            attention_back,
            lambda k: reduce_middle(ph + 1, k),
        )

        block = mm_tn(mix[layer], dmr[layer]).astype(BF16)
        for q in range(pieces):
            gbufs[4][layer, q] = block[:, q * wide : (q + 1) * wide]
        x_first_start(4, layer)

        def grad_qkv(b):
            cols = pl.ds(pl.multiple_of(b * wide, wide), wide)
            block = mm_tn(n1[layer, :, cols], dqkv[...]).astype(BF16)
            gbufs[2][layer, b] = block[:, 0:256]
            gbufs[3][layer, b] = block[:, 256:384]

        each(pieces, grad_qkv)
        z_first_start(2, layer)
        x_first_start(3, layer)

        def finish(k):
            slope, gain_grad, shift_grad = norm_back(
                hrow[layer, k], vec[layer, 0:1], reduce_finish(ph + 1, k)
            )
            rows = mrow[layer, k] + slope

            @pl.when(layer == 1)
            def _():
                dyr[0, mine(k)] = rows.astype(BF16)
                gather_start(3, dyr, 0, k)

            emit(1, layer, k, rows)
            gpack[layer, 0:1] += gain_grad
            gpack[layer, 2:3] += shift_grad

        each(chunks, finish)
        x_send(5, layer, lambda to: gpack.at[layer])
        z_first_middle(0, layer)

        @pl.when(c == layer)
        def _():
            x_first_middle(1)

    def collect_attention(layer):
        @pl.when(c == layer)
        def _():
            x_first_middle(4)
            x_first_middle(3)

        z_first_middle(2, layer)

        @pl.when(c == layer)
        def _():
            await_bytes(xrs[5], xsem.at[5])
            zsums[5][...] = sum4(5)
            for j in range(1, nz):
                remote(zsums[5], zrs[5].at[j - 1], zsend.at[5, 0], zsem.at[5, 0], z_peer(j))

    each(2, backward)
    collect_attention(0)

    total = zsums[5][...]
    if nz > 1:
        await_bytes(zrs[5], zsem.at[5, 0])
    for j in range(nz - 1):
        total = total + zrs[5][j]
    for j in range(T):
        tsum[j] = total[:, j * 128 : (j + 1) * 128]
    gbias_ref[...] = total
    for j in range(1, T):
        other = lax.rem(t + j, T)
        remote(tsum.at[other], tr.at[j - 1], tsend.at[0], tsem.at[0], (c, other, d))

    g1_ref[...] = x_first_finish(1)
    gout_ref[...] = x_first_finish(4)
    gqkv_ref[:, 256:384] = x_first_finish(3)
    g2_ref[...] = z_first_finish(0)
    gqkv_ref[:, 0:256] = z_first_finish(2)
    await_bytes(tr, tsem.at[0])
    small = tsum[t]
    for j in range(T - 1):
        small = small + tr[j]
    gsmall_ref[...] = small
    for kind in range(2):
        await_bytes(obuf.at[kind], osem.at[kind])
    rows_ref[...] = obuf[...]

    for i in range(4):
        both = weights[i][1]

        @pl.when(jnp.logical_not(native))
        def _():
            await_bytes(both.at[0], whome.at[i])
            for layer in range(2):
                await_bytes(both.at[0, half(i, 0)], wrelay.at[i, layer])

        if i:
            weight_left(i)

    @pl.when(c == 1)
    def _():
        weight_left(0)

    @pl.when(jnp.logical_not(native))
    def _():
        await_bytes(vec.at[0], vsend.at[0])

    await_bytes(vec.at[0], vsend.at[0])
    for ph in range(8):
        await_bytes(cbuf.at[ph], csend.at[ph])
        await_bytes(rs.at[ph], rsend.at[ph])
    for which, layer in ((0, 1), (1, 0), (1, 1), (2, 0), (2, 1), (3, 0)):
        await_bytes(rs.at[0], gsend.at[which, layer])
        await_bytes(cbuf.at[0], hsend.at[which, layer])
    for layer in range(2):
        for kind in range(2):

            @pl.when(c == layer)
            def _():
                view = ostage.at[kind, layer, :, pl.ds(0, T - 1)]
                await_bytes(view, osend.at[kind, layer])

            @pl.when(c != layer)
            def _():
                await_bytes(ostage.at[kind, layer], osend.at[kind, layer])

        self_ = jnp.logical_and(c == layer, native)
        for m in range(6):
            if nz > 1 and m in (0, 2):
                await_bytes(zrs[m].at[layer], zsend.at[m, layer])
            await_bytes(xrs[m].at[0], xsend.at[m, layer])

            @pl.when(jnp.logical_not(self_))
            def _():
                await_bytes(xrs[m].at[0], xsend.at[m, layer])

    if nz > 1:
        for m in (1, 3, 4, 5):
            await_bytes(zrs[m], zsend.at[m, 0])
    await_bytes(tr, tsend.at[0])


def core(chunks, nz, x, ct, docs, wqkv, wout, w1, w2, qb, b1, gains, shifts):
    n = chunks * ROWS
    vm = pl.BlockSpec(memory_space=pltpu.VMEM)
    hbm = pl.BlockSpec(memory_space=pl.ANY)
    pieces = 2 * nz
    wide = D // pieces
    out_shape = (
        jax.ShapeDtypeStruct((2, 2 * n, 128), BF16),
        jax.ShapeDtypeStruct((wide, 384), F32),
        jax.ShapeDtypeStruct((128, wide), F32),
        jax.ShapeDtypeStruct((wide, 512), F32),
        jax.ShapeDtypeStruct((512, wide), F32),
        jax.ShapeDtypeStruct((8, 128), F32),
        jax.ShapeDtypeStruct((8, D), F32),
    )
    dma = pltpu.SemaphoreType.DMA
    shape = ((512, wide), (wide, 512), (wide, 256), (wide, 128), (128, wide))
    back = max(nz - 1, 1)
    gbufs = [pltpu.VMEM((2, pieces) + s, BF16) for s in shape]
    zrs, zsums, xrs = [], [], []
    for m, s in enumerate(shape):
        if m in (0, 2):
            zrs.append(pltpu.VMEM((2, back, 2) + s, BF16))
            zsums.append(pltpu.VMEM((2, 2) + s, BF16))
            xrs.append(pltpu.VMEM((4,) + s, BF16))
        else:
            zrs.append(pltpu.VMEM((back,) + s, BF16))
            zsums.append(pltpu.VMEM((nz,) + s, BF16))
            xrs.append(pltpu.VMEM((4, nz) + s, BF16))
    zrs.append(pltpu.VMEM((back, 8, D), F32))
    zsums.append(pltpu.VMEM((8, D), F32))
    xrs.append(pltpu.VMEM((4, 8, D), F32))
    scratch = [
        pltpu.VMEM((n, D), BF16),
        pltpu.VMEM((n, ROWS), F32),
        pltpu.VMEM((8, D), F32),
        pltpu.VMEM((2, D, 384), BF16),
        pltpu.VMEM((2, 128, D), BF16),
        pltpu.VMEM((2, D, 512), BF16),
        pltpu.VMEM((2, 512, D), BF16),
        pltpu.VMEM((2, 8, D), F32),
        pltpu.VMEM((2, n, D), BF16),
        pltpu.VMEM((2, n, D), BF16),
        pltpu.VMEM((2, n, D), BF16),
        pltpu.VMEM((2, n, D), BF16),
        pltpu.VMEM((2, n, 384), BF16),
        pltpu.VMEM((2, n, 128), BF16),
        pltpu.VMEM((2, chunks, 2, ROWS, ROWS), F32),
        pltpu.VMEM((2, n, 512), F32),
        pltpu.VMEM((2, n, 512), BF16),
        pltpu.VMEM((n, 512), BF16),
        pltpu.VMEM((n, 384), BF16),
        pltpu.VMEM((2, chunks, OWN, D), F32),
        pltpu.VMEM((2, chunks, OWN, D), F32),
        pltpu.VMEM((8, n, D), BF16),
        pltpu.VMEM((8, chunks, ROWS // 2, D), BF16),
        pltpu.VMEM((8, chunks, ROWS // 2, D), BF16),
        pltpu.VMEM((8, chunks, Y - 1, OWN, D), BF16),
        pltpu.VMEM((2, 2, chunks, T, OWN, 128), BF16),
        pltpu.VMEM((2, 2 * n, 128), BF16),
        gbufs,
        zrs,
        zsums,
        xrs,
        pltpu.VMEM((2, 8, D), F32),
        pltpu.VMEM((T, 8, 128), F32),
        pltpu.VMEM((T - 1, 8, 128), F32),
        dma((2,)),
        dma((4, 2, 2)),
        dma((4,)),
        dma((4,)),
        dma((4, 2)),
        dma((2,)),
        dma((1,)),
        dma((8, chunks)),
        dma((8,)),
        dma((8, chunks)),
        dma((8,)),
        dma((4, 2, chunks)),
        dma((4, 2)),
        dma((4, 2, chunks)),
        dma((4, 2)),
        dma((2,)),
        dma((2, 2)),
        dma((6, 2)),
        dma((6, 2)),
        dma((6,)),
        dma((6, 2)),
        dma((1,)),
        dma((1,)),
    ]
    return pl.pallas_call(
        functools.partial(kernel, chunks, nz),
        out_shape=out_shape,
        in_specs=[hbm, hbm, vm, hbm, hbm, hbm, hbm, vm, vm, vm, vm],
        out_specs=[vm] * 7,
        scratch_shapes=scratch,
        compiler_params=pltpu.CompilerParams(
            collective_id=0, has_side_effects=True, vmem_limit_bytes=62 * 2**20
        ),
        name="layers",
    )(x, ct, docs, wqkv, wout, w1, w2, qb, b1, gains, shifts)


def closing(
    m,
    rows,
    gqkv,
    gout,
    g1,
    g2,
    small,
    bias,
    sec_out,
    ing_out,
    gqkv_out,
    qb_out,
    gout_out,
    g1_out,
    b1_out,
    g2_out,
    gains_out,
    shifts_out,
):
    d = lax.axis_index("dp")
    sec_out[0] = rows[0].astype(F32)
    ing_out[0] = rows[1].astype(F32)
    for j in range(3):
        gqkv_out[0, :, j, :] = gqkv[:, j * 128 : (j + 1) * 128]
    gout_out[0] = gout[...]
    g1_out[0] = g1[...]
    g2_out[0] = g2[...]
    share = 128 // m
    shift = lax.rem(128 - d * share, 128)
    rolled = pltpu.roll(small[...], shift, 1)
    gains_out[0] = rolled[0:2, 0:share]
    shifts_out[0] = rolled[2:6, 0:share]
    for j in range(2):
        rolled = pltpu.roll(bias[:, j * 256 : j * 256 + 128], shift, 1)
        qb_out[0, j : j + 1] = rolled[6:7, 0:share]
    wide = 512 // m
    if wide >= 128:
        b1_out[...] = bias[6:7, pl.ds(pl.multiple_of(384 + d * wide, 128), wide)]
    else:
        per = 128 // wide
        block = bias[:, pl.ds(pl.multiple_of(384 + d // per * 128, 128), 128)]
        rolled = pltpu.roll(block, lax.rem(128 - lax.rem(d, per) * wide, 128), 1)
        b1_out[...] = rolled[6:7, 0:wide]


def shards(
    inputs,
    cotangent,
    doc_ids,
    qkv_weight,
    qkv_bias,
    out_weight,
    fc1_weight,
    fc1_bias,
    fc2_weight,
    norm_gains,
    shifts,
):
    m = lax.axis_size("dp")
    chunks = doc_ids.shape[0] // 2
    n = chunks * ROWS
    results = core(
        chunks,
        m // 2,
        inputs,
        cotangent,
        doc_ids,
        qkv_weight[0].reshape(D, 384),
        out_weight[0],
        fc1_weight[0],
        fc2_weight[0],
        qkv_bias,
        fc1_bias,
        norm_gains,
        shifts,
    )
    vm = pl.BlockSpec(memory_space=pltpu.VMEM)
    shapes = (
        (1, 2 * n, 128),
        (1, 2 * n, 128),
        (1, D // m, 3, 128),
        (1, 2, 128 // m),
        (1, 128, D // m),
        (1, D // m, 512),
        (1, 512 // m),
        (1, 512, D // m),
        (1, 2, 128 // m),
        (1, 4, 128 // m),
    )
    return pl.pallas_call(
        functools.partial(closing, m),
        out_shape=[jax.ShapeDtypeStruct(shape, F32) for shape in shapes],
        in_specs=[vm] * 7,
        out_specs=[vm] * 10,
        compiler_params=pltpu.CompilerParams(vmem_limit_bytes=48 * 2**20),
        name="closing",
    )(*results)


def solution(mesh):
    return jax.shard_map(
        shards,
        mesh=mesh,
        in_specs=(
            P("dp", None),
            P("dp", None),
            P("dp", None),
            P("pipe", None, None, "tensor"),
            P("pipe", None, "tensor"),
            P("pipe", "tensor", None),
            P("pipe", None, "tensor"),
            P("pipe", "tensor"),
            P("pipe", "tensor", None),
            P("pipe", None, None),
            P("pipe", None, None),
        ),
        out_specs=(
            P("pipe", "dp", "tensor"),
            P("pipe", "dp", "tensor"),
            P("pipe", "dp", None, "tensor"),
            P("pipe", None, ("tensor", "dp")),
            P("pipe", "tensor", "dp"),
            P("pipe", "dp", "tensor"),
            P("pipe", ("tensor", "dp")),
            P("pipe", "tensor", "dp"),
            P("pipe", None, ("tensor", "dp")),
            P("pipe", None, ("tensor", "dp")),
        ),
        check_vma=False,
    )
```

```python
import functools

import jax
import jax.numpy as jnp
from jax import lax
from jax.experimental import pallas as pl
from jax.experimental.pallas import tpu as pltpu
from jax.sharding import PartitionSpec as P

MESH = pl.DeviceIdType.MESH
F32 = jnp.float32
BF16 = jnp.bfloat16
EPSILON = 1e-05
HD = 64
SCALE = HD**-0.5
D = 1024
ROWS = 128
T = 8
Y = 4
PARTS = 2
OWN = ROWS // T
GELU_C = 0.7978845608028654
GELU_A = 0.044715


def mm(a, b):
    return lax.dot_general(a, b, (((1,), (0,)), ((), ())), preferred_element_type=F32)


def mm_nt(a, b):
    return lax.dot_general(a, b, (((1,), (1,)), ((), ())), preferred_element_type=F32)


def mm_tn(a, b):
    return lax.dot_general(a, b, (((0,), (0,)), ((), ())), preferred_element_type=F32)


def standardize(rows):
    centered = rows - jnp.mean(rows, -1, keepdims=True)
    variance = jnp.mean(centered * centered, -1, keepdims=True)
    root = lax.rsqrt(variance + EPSILON)
    return centered * root, root


def norm_back(rows, gain, grad):
    unit, root = standardize(rows)
    e = grad * gain
    slope = root * (
        e - jnp.mean(e, -1, keepdims=True) - unit * jnp.mean(e * unit, -1, keepdims=True)
    )
    return slope, jnp.sum(grad * unit, 0, keepdims=True), jnp.sum(grad, 0, keepdims=True)


def kernel(
    chunks,
    nz,
    x_in,
    ct_in,
    docs_ref,
    wqkv_in,
    wout_in,
    w1_in,
    w2_in,
    qb_in,
    b1_in,
    gains_in,
    shifts_in,
    rows_ref,
    grads_ref,
    x_ref,
    mask_ref,
    vec_in,
    wqkv,
    wout,
    w1,
    w2,
    vec,
    n1,
    n2,
    dmr,
    dyr,
    qkv,
    mix,
    prob,
    up,
    act,
    dup,
    dqkv,
    hrow,
    mrow,
    part,
    cbuf,
    psum,
    rs,
    ostage,
    obuf,
    gbufs,
    zrs,
    zsums,
    xrs,
    gpack,
    sstage,
    sbias,
    sgot,
    ssum,
    sall,
    insem,
    wsem,
    wsend,
    whome,
    wrelay,
    vsem,
    vsend,
    csem,
    csend,
    rsem,
    rsend,
    gsem,
    gsend,
    hsem,
    hsend,
    osem,
    osend,
    zsem,
    zsend,
    xsem,
    xsend,
    ssem,
    ssend,
):
    c = lax.axis_index("pipe")
    t = lax.axis_index("tensor")
    d = lax.axis_index("dp")
    xh = t // Y
    y = lax.rem(t, Y)
    xl = d // nz
    z = lax.rem(d, nz)
    sib = (1 - c, t, d)

    first_row = pl.ds(pl.multiple_of(xh * (chunks * ROWS), ROWS), chunks * ROWS)
    x_copy = pltpu.make_async_copy(x_in.at[first_row], x_ref, insem.at[0])
    ct_copy = pltpu.make_async_copy(ct_in.at[first_row], dyr.at[1], insem.at[1])
    x_copy.start()
    ct_copy.start()

    barrier = pltpu.get_barrier_semaphore()

    def greet(device):
        pl.semaphore_signal(barrier, inc=1, device_id=device, device_id_type=MESH)

    for j in range(T):
        other = lax.rem(t + j, T)
        if j:
            greet((c, other, d))
        greet((1 - c, other, d))
    far = (1 - xl) * nz + z
    for core_ in range(2):
        for j in range(2):
            greet((core_, j * Y + y, far))
    for j in range(1, nz):
        greet((c, t, xl * nz + lax.rem(z + j, nz)))
        greet((c, t, (1 - xl) * nz + lax.rem(z + j, nz)))
    vec_in[...] = jnp.zeros_like(vec_in)
    vec_in[0:2] = gains_in[0].astype(F32)
    vec_in[2:6] = shifts_in[0].astype(F32)
    vec_in[6:7, 0:128] = qb_in[0, 0:1].astype(F32)
    vec_in[6:7, 256:384] = qb_in[0, 1:2].astype(F32)
    vec_in[7:8, 0:512] = b1_in[...].astype(F32)
    pl.semaphore_wait(barrier, 2 * T - 1 + 4 + 2 * (nz - 1))

    def remote(src, dst, send, recv, device):
        pltpu.make_async_remote_copy(
            src_ref=src,
            dst_ref=dst,
            send_sem=send,
            recv_sem=recv,
            device_id=device,
            device_id_type=MESH,
        ).start()

    def await_bytes(view, sem):
        pltpu.make_async_copy(view, view, sem).wait()

    weights = ((wqkv_in, wqkv), (wout_in, wout), (w1_in, w1), (w2_in, w2))
    native = c == xh
    partner = (xh, (1 - xh) * Y + y, far)
    home = (xh, t, d)

    def half(i, which, q):
        size = weights[i][1].shape[1] // (2 * PARTS)
        return pl.ds(pl.multiple_of((which * PARTS + q) * size, size), size)

    def send_weight(i):
        own, both = weights[i]
        for q in range(PARTS):
            piece = half(i, xl, q)
            remote(
                own.at[piece], both.at[c, piece], wsend.at[i], wsem.at[i, c, xl, q], partner
            )
        for h in range(2):
            for q in range(PARTS):
                src, dst = own.at[half(i, h, q)], both.at[c, half(i, h, q)]

                @pl.when(native)
                def _():
                    pltpu.make_async_copy(src, dst, wsem.at[i, c, h, q]).start()

                @pl.when(jnp.logical_not(native))
                def _():
                    remote(src, dst, whome.at[i], wsem.at[i, c, h, q], home)

    def whole_half(i):
        return weights[i][1].at[0, pl.ds(0, weights[i][1].shape[1] // 2)]

    def weight_left(i):
        await_bytes(whole_half(i), wsend.at[i])

    def await_half(i, layer, h, q):
        await_bytes(weights[i][1].at[layer, half(i, h, q)], wsem.at[i, layer, h, q])

    def relay(i, layer):
        both = weights[i][1]

        @pl.when(jnp.logical_not(native))
        def _():
            for q in range(PARTS):
                await_half(i, layer, 1 - xl, q)
                piece = both.at[layer, half(i, 1 - xl, q)]
                remote(
                    piece, piece, wrelay.at[i, layer], wsem.at[i, layer, 1 - xl, q], (c, t, far)
                )

    def need(i, layer):
        for q in range(PARTS):

            @pl.when(native)
            def _():
                await_half(i, layer, 1 - xl, q)

            await_half(i, layer, xl, q)

    def span(k):
        return pl.ds(pl.multiple_of(k * ROWS, ROWS), ROWS)

    def side(k, who):
        return pl.ds(pl.multiple_of(k * ROWS + who * (ROWS // 2), ROWS // 2), ROWS // 2)

    own_start = (c * Y + y) * OWN

    def mine(k):
        return pl.ds(pl.multiple_of(k * ROWS + own_start, OWN), OWN)

    def y_peer(j):
        return (c, xh * Y + lax.rem(y + j, Y), d)

    def reduce_start(ph, k):
        remote(
            part.at[ph, side(k, 1 - c)], cbuf.at[ph, k], csend.at[ph], csem.at[ph, k], sib
        )

    def reduce_middle(ph, k):
        await_bytes(cbuf.at[ph, k], csem.at[ph, k])
        psum[ph, k] = (part[ph, side(k, c)].astype(F32) + cbuf[ph, k].astype(F32)).astype(BF16)
        for j in range(1, Y):
            rows = pl.ds(pl.multiple_of(lax.rem(y + j, Y) * OWN, OWN), OWN)
            remote(
                psum.at[ph, k, rows], rs.at[ph, k, j - 1], rsend.at[ph], rsem.at[ph, k], y_peer(j)
            )

    def reduce_finish(ph, k):
        await_bytes(rs.at[ph, k], rsem.at[ph, k])
        rows = pl.ds(pl.multiple_of(y * OWN, OWN), OWN)
        total = psum[ph, k, rows].astype(F32)
        for j in range(Y - 1):
            total = total + rs[ph, k, j].astype(F32)
        return total

    def gather_start(which, buf, layer, k):
        for j in range(1, Y):
            view = buf.at[layer, mine(k)]
            remote(view, view, gsend.at[which, layer], gsem.at[which, layer, k], y_peer(j))

    def gather_middle(which, buf, layer, k):
        await_bytes(buf.at[layer, pl.ds(0, (Y - 1) * OWN)], gsem.at[which, layer, k])
        view = buf.at[layer, side(k, c)]
        remote(view, view, hsend.at[which, layer], hsem.at[which, layer, k], sib)

    def gather_finish(which, buf, layer, k):
        await_bytes(buf.at[layer, side(k, 1 - c)], hsem.at[which, layer, k])

    def emit(kind, layer, k, rows):
        low = rows.astype(BF16)
        for j in range(T):
            ostage[kind, layer, k, j] = low[:, j * 128 : (j + 1) * 128]
        first = xh * (chunks * ROWS) + k * ROWS + own_start
        target = pl.ds(pl.multiple_of(first, OWN), OWN)

        def away(j):
            other = lax.rem(t + j, T)
            remote(
                ostage.at[kind, layer, k, other],
                obuf.at[kind, target],
                osend.at[kind, layer],
                osem.at[kind],
                (layer, other, d),
            )

        for j in range(1, T):
            away(j)

        @pl.when(c == layer)
        def _():
            pltpu.make_async_copy(
                ostage.at[kind, layer, k, t], obuf.at[kind, target], osem.at[kind]
            ).start()

        @pl.when(c != layer)
        def _():
            away(0)

    slot = xh * 2 + xl

    def x_send(m, layer, source):
        for to in range(2):
            self_ = jnp.logical_and(jnp.logical_and(c == layer, native), xl == to)
            src, dst = source(to), xrs[m].at[slot]

            @pl.when(self_)
            def _():
                pltpu.make_async_copy(src, dst, xsem.at[m]).start()

            @pl.when(jnp.logical_not(self_))
            def _():
                remote(
                    src, dst, xsend.at[m, layer], xsem.at[m], (layer, c * Y + y, to * nz + z)
                )

    def z_peer(j):
        return (c, t, xl * nz + lax.rem(z + j, nz))

    def z_first_start(m, layer):
        for j in range(1, nz):
            for to in range(2):
                remote(
                    gbufs[m].at[layer, to * nz + lax.rem(z + j, nz)],
                    zrs[m].at[layer, j - 1, to],
                    zsend.at[m, layer],
                    zsem.at[m, layer],
                    z_peer(j),
                )

    def z_first_middle(m, layer):
        if nz > 1:
            await_bytes(zrs[m].at[layer], zsem.at[m, layer])
        for to in range(2):
            total = gbufs[m][layer, to * nz + z].astype(F32)
            for j in range(nz - 1):
                total = total + zrs[m][layer, j, to].astype(F32)
            zsums[m][layer, to] = total.astype(BF16)
        x_send(m, layer, lambda to: zsums[m].at[layer, to])

    def z_first_finish(m):
        await_bytes(xrs[m], xsem.at[m])
        return sum4(m)

    def sum4(m):
        total = xrs[m][0].astype(F32)
        for j in range(1, 4):
            total = total + xrs[m][j].astype(F32)
        return total

    def x_first_start(m, layer):
        x_send(m, layer, lambda to: gbufs[m].at[layer, pl.ds(to * nz, nz)])

    def x_first_middle(m):
        await_bytes(xrs[m], xsem.at[m])
        zsums[m][...] = sum4(m).astype(BF16)
        for j in range(1, nz):
            remote(
                zsums[m].at[lax.rem(z + j, nz)],
                zrs[m].at[j - 1],
                zsend.at[m, 0],
                zsem.at[m, 0],
                z_peer(j),
            )

    def x_first_finish(m):
        total = zsums[m][z].astype(F32)
        if nz > 1:
            await_bytes(zrs[m], zsem.at[m, 0])
        for j in range(nz - 1):
            total = total + zrs[m][j].astype(F32)
        return total

    left_half = lax.broadcasted_iota(jnp.int32, (ROWS, 128), 1) < HD

    def heads(value):
        zero = jnp.zeros_like(value)
        return jnp.where(left_half, value, zero), jnp.where(left_half, zero, value)

    def each(count, body):
        def step(i, carry):
            body(i)
            return carry

        lax.fori_loop(0, count, step, 0)

    @pl.when(native)
    def _():
        pltpu.make_async_copy(vec_in, vec.at[c], vsem.at[c]).start()

    @pl.when(jnp.logical_not(native))
    def _():
        remote(vec_in, vec.at[c], vsend.at[0], vsem.at[c], home)

    remote(vec_in, vec.at[c], vsend.at[0], vsem.at[c], partner)

    @pl.when(c == 0)
    def _():
        send_weight(0)
        send_weight(1)

    gpack[...] = jnp.zeros_like(gpack)
    x_copy.wait()
    ct_copy.wait()
    await_bytes(vec.at[0], vsem.at[0])
    await_bytes(vec.at[1], vsem.at[1])
    lanes = lax.broadcasted_iota(jnp.int32, (ROWS, ROWS), 1)
    places = lax.broadcasted_iota(jnp.int32, (ROWS, ROWS), 0)

    def start(k):
        unit, _ = standardize(x_ref[span(k)].astype(F32))
        n1[0, span(k)] = (unit * vec[0, 0:1] + vec[0, 2:3]).astype(BF16)
        hrow[0, k] = x_ref[mine(k)].astype(F32)
        segment = docs_ref[pl.ds(xh * chunks + k, 1)].astype(F32)
        segment = jnp.broadcast_to(segment, (ROWS, ROWS))
        visible = jnp.logical_and(lanes <= places, segment == segment.T)
        mask_ref[span(k)] = jnp.where(visible, 1.0, 0.0)

    each(chunks, start)

    relay(0, 0)
    relay(1, 0)

    @pl.when(c == 0)
    def _():
        weight_left(0)
        send_weight(2)

    need(0, 0)
    need(1, 0)

    @pl.when(c == 0)
    def _():
        send_weight(3)

    def attention(layer, k):
        ph = layer * 2

        @pl.when(layer == 1)
        def _():
            gather_finish(0, n1, 1, k)

        packed = mm(n1[layer, span(k)], wqkv[layer]) + vec[layer, 6:7, 0:384]
        packed = packed.astype(BF16)
        qkv[layer, span(k)] = packed
        queries, keys, values = packed[:, 0:128], packed[:, 128:256], packed[:, 256:384]
        visible = mask_ref[span(k)] > 0
        parts = []
        for head, query in enumerate(heads(queries)):
            scores = jnp.where(visible, mm_nt(query, keys) * SCALE, -1e30)
            weights_ = jnp.exp(scores - jnp.max(scores, -1, keepdims=True))
            p = weights_ / jnp.sum(weights_, -1, keepdims=True)
            prob[layer, k, head] = p
            parts.append(mm(p.astype(BF16), values))
        mixture = jnp.where(left_half, parts[0], parts[1]).astype(BF16)
        mix[layer, span(k)] = mixture
        part[ph, span(k)] = mm(mixture, wout[layer]).astype(BF16)
        reduce_start(ph, k)

    def second_norm(layer, k):
        rows = hrow[layer, k] + reduce_finish(layer * 2, k) + vec[layer, 3:4]
        mrow[layer, k] = rows
        unit, _ = standardize(rows)
        n2[layer, mine(k)] = (unit * vec[layer, 1:2] + vec[layer, 4:5]).astype(BF16)
        gather_start(1, n2, layer, k)

    def feed(layer, k):
        ph = layer * 2 + 1
        gather_finish(1, n2, layer, k)
        u = mm(n2[layer, span(k)], w1[layer]) + vec[layer, 7:8, 0:512]
        up[layer, span(k)] = u
        g = 0.5 * u * (1.0 + jnp.tanh(GELU_C * (u + GELU_A * (u * u * u))))
        g = g.astype(BF16)
        act[layer, span(k)] = g
        part[ph, span(k)] = mm(g, w2[layer]).astype(BF16)
        reduce_start(ph, k)

    def finish(layer, k):
        rows = mrow[layer, k] + reduce_finish(layer * 2 + 1, k) + vec[layer, 5:6]

        @pl.when(layer == 0)
        def _():
            entering = rows.astype(BF16).astype(F32)
            hrow[1, k] = entering
            unit, _ = standardize(entering)
            n1[1, mine(k)] = (unit * vec[1, 0:1] + vec[1, 2:3]).astype(BF16)
            gather_start(0, n1, 1, k)

        emit(0, layer, k, rows)

    def feed_back(layer, k):
        ph = 6 - layer * 2

        @pl.when(layer == 0)
        def _():
            gather_finish(3, dyr, 0, k)

        grad = mm_nt(dyr[layer, span(k)], w2[layer])
        u = up[layer, span(k)]
        bend = jnp.tanh(GELU_C * (u + GELU_A * (u * u * u)))
        slope = 0.5 * (1.0 + bend) + (0.5 * u) * (1.0 - bend * bend) * (
            GELU_C * (1.0 + (3.0 * GELU_A) * (u * u))
        )
        du = (grad * slope).astype(BF16)
        dup[span(k)] = du
        part[ph, span(k)] = mm_nt(du, w1[layer]).astype(BF16)
        reduce_start(ph, k)
        gpack[layer, 6:7, 384:896] += jnp.sum(du.astype(F32), 0, keepdims=True)

    def middle(layer, k):
        grad = dyr[layer, mine(k)].astype(F32)
        slope, gain_grad, shift_grad = norm_back(
            mrow[layer, k], vec[layer, 1:2], reduce_finish(6 - layer * 2, k)
        )
        dm = grad + slope
        mrow[layer, k] = dm
        low = dm.astype(BF16)
        dmr[layer, mine(k)] = low
        gather_start(2, dmr, layer, k)
        gpack[layer, 1:2] += gain_grad
        gpack[layer, 3:4] += jnp.sum(low.astype(F32), 0, keepdims=True)
        gpack[layer, 4:5] += shift_grad
        gpack[layer, 5:6] += jnp.sum(grad, 0, keepdims=True)

    def attention_back(layer, k):
        ph = 7 - layer * 2
        gather_finish(2, dmr, layer, k)
        da = mm_nt(dmr[layer, span(k)], wout[layer]).astype(BF16)
        packed = qkv[layer, span(k)]
        queries, keys, values = packed[:, 0:128], packed[:, 128:256], packed[:, 256:384]
        dqs, dks, dvs = [], [], []
        for head, grad in enumerate(heads(da)):
            p = prob[layer, k, head]
            dvs.append(mm_tn(p.astype(BF16), da))
            dp = mm_nt(grad, values)
            ds = p * (dp - jnp.sum(p * dp, -1, keepdims=True))
            ds = ds.astype(BF16)
            dqs.append(mm(ds, keys))
            dks.append(mm_tn(ds, queries))
        grads = jnp.concatenate(
            [
                jnp.where(left_half, dqs[0], dqs[1]) * SCALE,
                jnp.where(left_half, dks[0], dks[1]) * SCALE,
                jnp.where(left_half, dvs[0], dvs[1]),
            ],
            1,
        ).astype(BF16)
        dqkv[span(k)] = grads
        part[ph, span(k)] = mm_nt(grads, wqkv[layer]).astype(BF16)
        reduce_start(ph, k)
        gpack[layer, 6:7, 0:384] += jnp.sum(grads.astype(F32), 0, keepdims=True)

    def last(layer, k):
        slope, gain_grad, shift_grad = norm_back(
            hrow[layer, k], vec[layer, 0:1], reduce_finish(7 - layer * 2, k)
        )
        rows = mrow[layer, k] + slope

        @pl.when(layer == 1)
        def _():
            dyr[0, mine(k)] = rows.astype(BF16)
            gather_start(3, dyr, 0, k)

        emit(1, layer, k, rows)
        gpack[layer, 0:1] += gain_grad
        gpack[layer, 2:3] += shift_grad

    pieces = 2 * nz
    wide = D // pieces

    def grad_down(layer, b):
        cols = pl.ds(pl.multiple_of(b * 128, 128), 128)
        block = mm_tn(act[layer, :, cols], dyr[layer]).astype(BF16)
        for q in range(pieces):
            gbufs[0][layer, q, cols] = block[:, q * wide : (q + 1) * wide]

    up_wide = max(256 // wide, 1)
    up_steps = pieces // up_wide

    def grad_up(layer, b):
        size = wide * up_wide
        cols = pl.ds(pl.multiple_of(b * size, size), size)
        block = mm_tn(n2[layer, :, cols], dup[...]).astype(BF16)
        for q in range(up_wide):
            gbufs[1][layer, b * up_wide + q] = block[q * wide : (q + 1) * wide]

    def grad_out(layer):
        block = mm_tn(mix[layer], dmr[layer]).astype(BF16)
        for q in range(pieces):
            gbufs[4][layer, q] = block[:, q * wide : (q + 1) * wide]

    def grad_qkv(layer, b):
        size = wide * up_wide
        cols = pl.ds(pl.multiple_of(b * size, size), size)
        block = mm_tn(n1[layer, :, cols], dqkv[...]).astype(BF16)
        for q in range(up_wide):
            rows = slice(q * wide, (q + 1) * wide)
            gbufs[2][layer, b * up_wide + q] = block[rows, 0:256]
            gbufs[3][layer, b * up_wide + q] = block[rows, 256:384]

    def small_start(layer):
        for j in range(T):
            sstage[layer, j] = gpack[layer, :, j * 128 : (j + 1) * 128]
            sbias[layer, j : j + 1] = gpack[layer, 6:7, j * 128 : (j + 1) * 128]

        def send(src, dst, to, self_):
            @pl.when(self_)
            def _():
                pltpu.make_async_copy(src, dst, ssem.at[0]).start()

            @pl.when(jnp.logical_not(self_))
            def _():
                remote(src, dst, ssend.at[layer], ssem.at[0], (layer, to, d))

        for j in range(T):
            to = lax.rem(t + j, T)
            src, dst = sstage.at[layer, to], sgot.at[c * T + t]
            if j:
                remote(src, dst, ssend.at[layer], ssem.at[0], (layer, to, d))
            else:
                send(src, dst, to, c == layer)
        send(
            sbias.at[layer],
            sgot.at[2 * T + xh],
            c * Y + y,
            jnp.logical_and(c == layer, native),
        )

    def small_middle():
        await_bytes(sgot, ssem.at[0])
        total = sgot[0]
        for j in range(1, 2 * T):
            total = total + sgot[j]
        ssum[0] = total
        ssum[1] = sgot[2 * T] + sgot[2 * T + 1]
        for j in range(1, 2 * nz):
            to = lax.rem(d + j, 2 * nz)
            remote(ssum, sall.at[j - 1], ssend.at[2], ssem.at[1], (c, t, to))

    def small_finish():
        await_bytes(sall, ssem.at[1])
        total = ssum[...]
        for j in range(2 * nz - 1):
            total = total + sall[j]
        return total

    def collect_attention(layer):
        z_first_middle(2, layer)

        @pl.when(c == layer)
        def _():
            x_first_middle(3)
            x_first_middle(4)
            small_middle()

    def collect_feed(layer):
        z_first_middle(0, layer)

        @pl.when(c == layer)
        def _():
            x_first_middle(1)

    def on(condition, body, *args):
        @pl.when(condition)
        def _():
            body(*args)

    def stage_body(stage):
        odd = lax.rem(stage, 2)
        ahead = stage < 4
        layer = jnp.where(ahead, stage // 2, 3 - stage // 2)
        front_even = jnp.logical_and(ahead, odd == 0)
        front_odd = jnp.logical_and(ahead, odd == 1)
        back_even = jnp.logical_and(stage >= 4, odd == 0)
        back_odd = jnp.logical_and(stage >= 4, odd == 1)

        @pl.when(stage == 1)
        def _():
            need(2, 0)
            need(3, 0)

        @pl.when(stage == 2)
        def _():
            need(0, 1)
            need(1, 1)

        @pl.when(stage == 3)
        def _():
            need(2, 1)
            need(3, 1)

        def step(s):
            @pl.when(s < chunks)
            def _():
                on(front_odd, gather_middle, 1, n2, layer, s)
                on(stage == 2, gather_middle, 0, n1, 1, s)
                on(back_odd, gather_middle, 2, dmr, layer, s)
                on(stage == 6, gather_middle, 3, dyr, 0, s)

            @pl.when(jnp.logical_and(s >= 1, s < chunks + 1))
            def _():
                on(front_even, attention, layer, s - 1)
                on(front_odd, feed, layer, s - 1)
                on(back_even, feed_back, layer, s - 1)
                on(back_odd, attention_back, layer, s - 1)

            @pl.when(s >= 2)
            def _():
                reduce_middle(stage, s - 2)

            @pl.when(s == 2)
            def _():
                on(stage == 0, relay, 2, 0)
                on(stage == 2, relay, 2, 1)

        each(chunks + 2, step)

        @pl.when(stage == 0)
        def _():
            relay(3, 0)

            @pl.when(c == 1)
            def _():
                send_weight(0)
                send_weight(1)

        @pl.when(stage == 1)
        def _():
            relay(0, 1)
            relay(1, 1)

            @pl.when(c == 1)
            def _():
                send_weight(3)

        @pl.when(stage == 2)
        def _():
            relay(3, 1)

        @pl.when(stage == 4)
        def _():
            each(chunks, lambda k: finish(1, k))

        @pl.when(back_even)
        def _():
            each(4, lambda b: grad_down(layer, b))
            z_first_start(0, layer)

        @pl.when(back_odd)
        def _():
            grad_out(layer)
            x_first_start(4, layer)
            each(up_steps, lambda b: grad_qkv(layer, b))
            z_first_start(2, layer)
            x_first_start(3, layer)

        def settle(k):
            on(front_even, second_norm, layer, k)
            on(stage == 1, finish, 0, k)
            on(back_even, middle, layer, k)
            on(back_odd, last, layer, k)

        on(stage != 3, each, chunks, settle)

        @pl.when(jnp.logical_and(stage == 0, c == 1))
        def _():
            send_weight(2)

        @pl.when(back_even)
        def _():
            each(up_steps, lambda b: grad_up(layer, b))
            x_first_start(1, layer)

        on(back_odd, small_start, layer)
        on(stage == 5, collect_feed, 1)
        on(stage == 6, collect_attention, 1)

    each(8, stage_body)
    collect_feed(0)
    collect_attention(0)

    places_ = layout(nz)

    def put(name, value, start=0):
        rows = value.shape[0]
        first = places_[name] + start * rows
        for j in range(value.shape[1] // 128):
            grads_ref[first + j * rows : first + (j + 1) * rows] = value[:, j * 128 : (j + 1) * 128]

    put("down", z_first_finish(0))
    put("up", x_first_finish(1))
    put("qkv", z_first_finish(2))
    put("qkv", x_first_finish(3), 2)
    put("out", x_first_finish(4))
    small = small_finish()
    put("small", small[0])
    put("bias", small[1])
    for kind in range(2):
        await_bytes(obuf.at[kind], osem.at[kind])
    rows_ref[...] = obuf[...]

    for i in range(4):
        both = weights[i][1]

        @pl.when(jnp.logical_not(native))
        def _():
            await_bytes(both.at[0], whome.at[i])
            for layer in range(2):
                await_bytes(whole_half(i), wrelay.at[i, layer])

        if i:
            weight_left(i)

    @pl.when(c == 1)
    def _():
        weight_left(0)

    @pl.when(jnp.logical_not(native))
    def _():
        await_bytes(vec.at[0], vsend.at[0])

    await_bytes(vec.at[0], vsend.at[0])
    for ph in range(8):
        await_bytes(cbuf.at[ph], csend.at[ph])
        await_bytes(rs.at[ph], rsend.at[ph])
    for which, layer in ((0, 1), (1, 0), (1, 1), (2, 0), (2, 1), (3, 0)):
        await_bytes(rs.at[0], gsend.at[which, layer])
        await_bytes(cbuf.at[0], hsend.at[which, layer])
    for layer in range(2):
        for kind in range(2):

            @pl.when(c == layer)
            def _():
                view = ostage.at[kind, layer, :, pl.ds(0, T - 1)]
                await_bytes(view, osend.at[kind, layer])

            @pl.when(c != layer)
            def _():
                await_bytes(ostage.at[kind, layer], osend.at[kind, layer])

        self_ = jnp.logical_and(c == layer, native)
        for m in range(5):
            if nz > 1 and m in (0, 2):
                await_bytes(zrs[m].at[layer], zsend.at[m, layer])
            await_bytes(xrs[m].at[0], xsend.at[m, layer])

            @pl.when(jnp.logical_not(self_))
            def _():
                await_bytes(xrs[m].at[0], xsend.at[m, layer])

        await_bytes(sgot.at[pl.ds(0, T - 1)], ssend.at[layer])

        @pl.when(c != layer)
        def _():
            await_bytes(sgot.at[0], ssend.at[layer])

        @pl.when(jnp.logical_not(self_))
        def _():
            await_bytes(sgot.at[0], ssend.at[layer])

    if nz > 1:
        for m in (1, 3, 4):
            await_bytes(zrs[m], zsend.at[m, 0])
    await_bytes(sall, ssend.at[2])


def layout(nz):
    wide = D // (2 * nz)
    sizes = (
        ("qkv", 3 * wide),
        ("up", 4 * wide),
        ("down", 4 * wide),
        ("out", wide),
        ("small", 8),
        ("bias", 8),
    )
    places, first = {}, 0
    for name, size in sizes:
        places[name] = first
        first += size
    places["end"] = first
    return places


def core(chunks, nz, x, ct, docs, wqkv, wout, w1, w2, qb, b1, gains, shifts):
    n = chunks * ROWS
    vm = pl.BlockSpec(memory_space=pltpu.VMEM)
    hbm = pl.BlockSpec(memory_space=pl.ANY)
    pieces = 2 * nz
    wide = D // pieces
    out_shape = (
        jax.ShapeDtypeStruct((2, 2 * n, 128), BF16),
        jax.ShapeDtypeStruct((layout(nz)["end"], 128), F32),
    )
    dma = pltpu.SemaphoreType.DMA
    shape = ((512, wide), (wide, 512), (wide, 256), (wide, 128), (128, wide))
    back = max(nz - 1, 1)
    gbufs = [pltpu.VMEM((2, pieces) + s, BF16) for s in shape]
    zrs, zsums, xrs = [], [], []
    for m, s in enumerate(shape):
        if m in (0, 2):
            zrs.append(pltpu.VMEM((2, back, 2) + s, BF16))
            zsums.append(pltpu.VMEM((2, 2) + s, BF16))
            xrs.append(pltpu.VMEM((4,) + s, BF16))
        else:
            zrs.append(pltpu.VMEM((back,) + s, BF16))
            zsums.append(pltpu.VMEM((nz,) + s, BF16))
            xrs.append(pltpu.VMEM((4, nz) + s, BF16))
    scratch = [
        pltpu.VMEM((n, D), BF16),
        pltpu.VMEM((n, ROWS), F32),
        pltpu.VMEM((8, D), F32),
        pltpu.VMEM((2, D, 384), BF16),
        pltpu.VMEM((2, 128, D), BF16),
        pltpu.VMEM((2, D, 512), BF16),
        pltpu.VMEM((2, 512, D), BF16),
        pltpu.VMEM((2, 8, D), F32),
        pltpu.VMEM((2, n, D), BF16),
        pltpu.VMEM((2, n, D), BF16),
        pltpu.VMEM((2, n, D), BF16),
        pltpu.VMEM((2, n, D), BF16),
        pltpu.VMEM((2, n, 384), BF16),
        pltpu.VMEM((2, n, 128), BF16),
        pltpu.VMEM((2, chunks, 2, ROWS, ROWS), F32),
        pltpu.VMEM((2, n, 512), F32),
        pltpu.VMEM((2, n, 512), BF16),
        pltpu.VMEM((n, 512), BF16),
        pltpu.VMEM((n, 384), BF16),
        pltpu.VMEM((2, chunks, OWN, D), F32),
        pltpu.VMEM((2, chunks, OWN, D), F32),
        pltpu.VMEM((8, n, D), BF16),
        pltpu.VMEM((8, chunks, ROWS // 2, D), BF16),
        pltpu.VMEM((8, chunks, ROWS // 2, D), BF16),
        pltpu.VMEM((8, chunks, Y - 1, OWN, D), BF16),
        pltpu.VMEM((2, 2, chunks, T, OWN, 128), BF16),
        pltpu.VMEM((2, 2 * n, 128), BF16),
        gbufs,
        zrs,
        zsums,
        xrs,
        pltpu.VMEM((2, 8, D), F32),
        pltpu.VMEM((2, T, 8, 128), F32),
        pltpu.VMEM((2, 8, 128), F32),
        pltpu.VMEM((2 * T + 2, 8, 128), F32),
        pltpu.VMEM((2, 8, 128), F32),
        pltpu.VMEM((pieces - 1, 2, 8, 128), F32),
        dma((2,)),
        dma((4, 2, 2, PARTS)),
        dma((4,)),
        dma((4,)),
        dma((4, 2)),
        dma((2,)),
        dma((1,)),
        dma((8, chunks)),
        dma((8,)),
        dma((8, chunks)),
        dma((8,)),
        dma((4, 2, chunks)),
        dma((4, 2)),
        dma((4, 2, chunks)),
        dma((4, 2)),
        dma((2,)),
        dma((2, 2)),
        dma((5, 2)),
        dma((5, 2)),
        dma((5,)),
        dma((5, 2)),
        dma((2,)),
        dma((3,)),
    ]
    return pl.pallas_call(
        functools.partial(kernel, chunks, nz),
        out_shape=out_shape,
        in_specs=[hbm, hbm, vm, hbm, hbm, hbm, hbm, vm, vm, vm, vm],
        out_specs=[vm] * 2,
        scratch_shapes=scratch,
        compiler_params=pltpu.CompilerParams(
            collective_id=0, has_side_effects=True, vmem_limit_bytes=62 * 2**20
        ),
        name="layers",
    )(x, ct, docs, wqkv, wout, w1, w2, qb, b1, gains, shifts)


def closing(
    m,
    rows,
    grads,
    sec_out,
    ing_out,
    gqkv_out,
    qb_out,
    gout_out,
    g1_out,
    b1_out,
    g2_out,
    gains_out,
    shifts_out,
):
    d = lax.axis_index("dp")
    sec_out[0] = rows[0].astype(F32)
    ing_out[0] = rows[1].astype(F32)
    places = layout(m // 2)
    width = D // m

    def get(name, height, j):
        first = places[name] + j * height
        return grads[first : first + height]

    for j in range(3):
        gqkv_out[0, :, j, :] = get("qkv", width, j)
    for j in range(4):
        g1_out[0, :, j * 128 : (j + 1) * 128] = get("up", width, j)
    for j in range(width // 128):
        gout_out[0, :, j * 128 : (j + 1) * 128] = get("out", 128, j)
        g2_out[0, :, j * 128 : (j + 1) * 128] = get("down", 512, j)
    share = 128 // m
    shift = lax.rem(128 - d * share, 128)
    rolled = pltpu.roll(get("small", 8, 0), shift, 1)
    gains_out[0] = rolled[0:2, 0:share]
    shifts_out[0] = rolled[2:6, 0:share]
    bias = get("bias", 8, 0)
    rolled = pltpu.roll(bias, shift, 1)
    for j in range(2):
        qb_out[0, j : j + 1] = rolled[2 * j : 2 * j + 1, 0:share]
    lines = lax.broadcasted_iota(jnp.int32, (8, 128), 0)

    def line(block, which):
        return jnp.sum(jnp.where(lines == which, block, 0.0), 0, keepdims=True)

    wide = 512 // m
    if wide >= 128:
        for j in range(wide // 128):
            b1_out[:, j * 128 : (j + 1) * 128] = line(bias, 3 + d * (wide // 128) + j)
    else:
        per = 128 // wide
        rolled = pltpu.roll(bias, lax.rem(128 - lax.rem(d, per) * wide, 128), 1)
        b1_out[...] = line(rolled, 3 + d // per)[:, 0:wide]


def shards(
    inputs,
    cotangent,
    doc_ids,
    qkv_weight,
    qkv_bias,
    out_weight,
    fc1_weight,
    fc1_bias,
    fc2_weight,
    norm_gains,
    shifts,
):
    m = lax.axis_size("dp")
    chunks = doc_ids.shape[0] // 2
    n = chunks * ROWS
    results = core(
        chunks,
        m // 2,
        inputs,
        cotangent,
        doc_ids,
        qkv_weight[0].reshape(D, 384),
        out_weight[0],
        fc1_weight[0],
        fc2_weight[0],
        qkv_bias,
        fc1_bias,
        norm_gains,
        shifts,
    )
    vm = pl.BlockSpec(memory_space=pltpu.VMEM)
    shapes = (
        (1, 2 * n, 128),
        (1, 2 * n, 128),
        (1, D // m, 3, 128),
        (1, 2, 128 // m),
        (1, 128, D // m),
        (1, D // m, 512),
        (1, 512 // m),
        (1, 512, D // m),
        (1, 2, 128 // m),
        (1, 4, 128 // m),
    )
    return pl.pallas_call(
        functools.partial(closing, m),
        out_shape=[jax.ShapeDtypeStruct(shape, F32) for shape in shapes],
        in_specs=[vm] * 2,
        out_specs=[vm] * 10,
        compiler_params=pltpu.CompilerParams(vmem_limit_bytes=48 * 2**20),
        name="closing",
    )(*results)


def solution(mesh):
    return jax.shard_map(
        shards,
        mesh=mesh,
        in_specs=(
            P("dp", None),
            P("dp", None),
            P("dp", None),
            P("pipe", None, None, "tensor"),
            P("pipe", None, "tensor"),
            P("pipe", "tensor", None),
            P("pipe", None, "tensor"),
            P("pipe", "tensor"),
            P("pipe", "tensor", None),
            P("pipe", None, None),
            P("pipe", None, None),
        ),
        out_specs=(
            P("pipe", "dp", "tensor"),
            P("pipe", "dp", "tensor"),
            P("pipe", "dp", None, "tensor"),
            P("pipe", None, ("tensor", "dp")),
            P("pipe", "tensor", "dp"),
            P("pipe", "dp", "tensor"),
            P("pipe", ("tensor", "dp")),
            P("pipe", "tensor", "dp"),
            P("pipe", None, ("tensor", "dp")),
            P("pipe", None, ("tensor", "dp")),
        ),
        check_vma=False,
    )
```

```python
import functools

import jax
import jax.numpy as jnp
from jax import lax
from jax.experimental import pallas as pl
from jax.experimental.pallas import tpu as pltpu
from jax.sharding import PartitionSpec as P

MESH = pl.DeviceIdType.MESH
F32 = jnp.float32
BF16 = jnp.bfloat16
EPSILON = 1e-05
HD = 64
SCALE = HD**-0.5
D = 1024
ROWS = 128
T = 8
Y = 4
PARTS = 2
OWN = ROWS // T
GELU_C = 0.7978845608028654
GELU_A = 0.044715


def mm(a, b):
    return lax.dot_general(a, b, (((1,), (0,)), ((), ())), preferred_element_type=F32)


def mm_nt(a, b):
    return lax.dot_general(a, b, (((1,), (1,)), ((), ())), preferred_element_type=F32)


def mm_tn(a, b):
    return lax.dot_general(a, b, (((0,), (0,)), ((), ())), preferred_element_type=F32)


def standardize(rows):
    centered = rows - jnp.mean(rows, -1, keepdims=True)
    variance = jnp.mean(centered * centered, -1, keepdims=True)
    root = lax.rsqrt(variance + EPSILON)
    return centered * root, root


def norm_back(rows, gain, grad):
    unit, root = standardize(rows)
    e = grad * gain
    slope = root * (
        e - jnp.mean(e, -1, keepdims=True) - unit * jnp.mean(e * unit, -1, keepdims=True)
    )
    return slope, grad * unit


def kernel(
    chunks,
    nz,
    x_in,
    ct_in,
    docs_ref,
    wqkv_in,
    wout_in,
    w1_in,
    w2_in,
    qb_in,
    b1_in,
    gains_in,
    shifts_in,
    rows_ref,
    grads_ref,
    x_ref,
    mask_ref,
    vec_in,
    wqkv,
    wout,
    w1,
    w2,
    vec,
    n1,
    n2,
    dmr,
    dyr,
    qkv,
    mix,
    prob,
    up,
    act,
    dup,
    dqkv,
    hrow,
    mrow,
    ledger,
    part,
    cbuf,
    psum,
    rs,
    ostage,
    obuf,
    gbufs,
    zrs,
    zsums,
    xrs,
    gpack,
    sstage,
    sbias,
    sgot,
    ssum,
    sall,
    insem,
    wsem,
    wsend,
    whome,
    wrelay,
    vsem,
    vsend,
    csem,
    csend,
    rsem,
    rsend,
    gsem,
    gsend,
    hsem,
    hsend,
    osem,
    osend,
    zsem,
    zsend,
    xsem,
    xsend,
    ssem,
    ssend,
):
    c = lax.axis_index("pipe")
    t = lax.axis_index("tensor")
    d = lax.axis_index("dp")
    xh = t // Y
    y = lax.rem(t, Y)
    xl = d // nz
    z = lax.rem(d, nz)
    sib = (1 - c, t, d)

    first_row = pl.ds(pl.multiple_of(xh * (chunks * ROWS), ROWS), chunks * ROWS)
    x_copy = pltpu.make_async_copy(x_in.at[first_row], x_ref, insem.at[0])
    ct_copy = pltpu.make_async_copy(ct_in.at[first_row], dyr.at[1], insem.at[1])
    x_copy.start()
    ct_copy.start()

    barrier = pltpu.get_barrier_semaphore()

    def greet(device):
        pl.semaphore_signal(barrier, inc=1, device_id=device, device_id_type=MESH)

    for j in range(T):
        other = lax.rem(t + j, T)
        if j:
            greet((c, other, d))
        greet((1 - c, other, d))
    far = (1 - xl) * nz + z
    for core_ in range(2):
        for j in range(2):
            greet((core_, j * Y + y, far))
    for j in range(1, nz):
        greet((c, t, xl * nz + lax.rem(z + j, nz)))
        greet((c, t, (1 - xl) * nz + lax.rem(z + j, nz)))
    vec_in[...] = jnp.zeros_like(vec_in)
    vec_in[0:2] = gains_in[0].astype(F32)
    vec_in[2:6] = shifts_in[0].astype(F32)
    vec_in[6:7, 0:128] = qb_in[0, 0:1].astype(F32)
    vec_in[6:7, 256:384] = qb_in[0, 1:2].astype(F32)
    vec_in[7:8, 0:512] = b1_in[...].astype(F32)
    pl.semaphore_wait(barrier, 2 * T - 1 + 4 + 2 * (nz - 1))

    def remote(src, dst, send, recv, device):
        pltpu.make_async_remote_copy(
            src_ref=src,
            dst_ref=dst,
            send_sem=send,
            recv_sem=recv,
            device_id=device,
            device_id_type=MESH,
        ).start()

    def await_bytes(view, sem):
        pltpu.make_async_copy(view, view, sem).wait()

    weights = ((wqkv_in, wqkv), (wout_in, wout), (w1_in, w1), (w2_in, w2))
    native = c == xh
    partner = (xh, (1 - xh) * Y + y, far)
    home = (xh, t, d)

    def half(i, which, q):
        size = weights[i][1].shape[1] // (2 * PARTS)
        return pl.ds(pl.multiple_of((which * PARTS + q) * size, size), size)

    def views(i, h, q):
        own, both = weights[i]
        piece = half(i, h, q)
        if i:
            return [(own.at[piece], both.at[c, piece])]
        return [
            (own.at[j, piece], both.at[c, piece, pl.ds(j * 128, 128)]) for j in range(3)
        ]

    def send_weight(i):
        for q in range(PARTS):
            for src, dst in views(i, xl, q):
                remote(src, dst, wsend.at[i], wsem.at[i, c, xl, q], partner)
        for h in range(2):
            for q in range(PARTS):
                for src, dst in views(i, h, q):

                    @pl.when(native)
                    def _():
                        pltpu.make_async_copy(src, dst, wsem.at[i, c, h, q]).start()

                    @pl.when(jnp.logical_not(native))
                    def _():
                        remote(src, dst, whome.at[i], wsem.at[i, c, h, q], home)

    def whole_half(i):
        return weights[i][1].at[0, pl.ds(0, weights[i][1].shape[1] // 2)]

    def weight_left(i):
        await_bytes(whole_half(i), wsend.at[i])

    def await_half(i, layer, h, q):
        await_bytes(weights[i][1].at[layer, half(i, h, q)], wsem.at[i, layer, h, q])

    def relay(i, layer, parts=tuple(range(PARTS))):
        both = weights[i][1]

        @pl.when(jnp.logical_not(native))
        def _():
            for q in parts:
                await_half(i, layer, 1 - xl, q)
                piece = both.at[layer, half(i, 1 - xl, q)]
                remote(
                    piece, piece, wrelay.at[i, layer], wsem.at[i, layer, 1 - xl, q], (c, t, far)
                )

    def need(i, layer):
        for q in range(PARTS):

            @pl.when(native)
            def _():
                await_half(i, layer, 1 - xl, q)

            await_half(i, layer, xl, q)

    def span(k):
        return pl.ds(pl.multiple_of(k * ROWS, ROWS), ROWS)

    def side(k, who):
        return pl.ds(pl.multiple_of(k * ROWS + who * (ROWS // 2), ROWS // 2), ROWS // 2)

    own_start = (c * Y + y) * OWN

    def mine(k):
        return pl.ds(pl.multiple_of(k * ROWS + own_start, OWN), OWN)

    def y_peer(j):
        return (c, xh * Y + lax.rem(y + j, Y), d)

    def reduce_start(ph, k):
        remote(
            part.at[ph, side(k, 1 - c)], cbuf.at[ph, k], csend.at[ph], csem.at[ph, k], sib
        )

    def reduce_middle(ph, k):
        await_bytes(cbuf.at[ph, k], csem.at[ph, k])
        psum[ph, k] = (part[ph, side(k, c)].astype(F32) + cbuf[ph, k].astype(F32)).astype(BF16)
        for j in range(1, Y):
            rows = pl.ds(pl.multiple_of(lax.rem(y + j, Y) * OWN, OWN), OWN)
            remote(
                psum.at[ph, k, rows], rs.at[ph, k, j - 1], rsend.at[ph], rsem.at[ph, k], y_peer(j)
            )

    def reduce_finish(ph, k):
        await_bytes(rs.at[ph, k], rsem.at[ph, k])
        rows = pl.ds(pl.multiple_of(y * OWN, OWN), OWN)
        total = psum[ph, k, rows].astype(F32)
        for j in range(Y - 1):
            total = total + rs[ph, k, j].astype(F32)
        return total

    def gather_start(which, buf, layer, k):
        for j in range(1, Y):
            view = buf.at[layer, mine(k)]
            remote(view, view, gsend.at[which, layer], gsem.at[which, layer, k], y_peer(j))

    def gather_middle(which, buf, layer, k):
        await_bytes(buf.at[layer, pl.ds(0, (Y - 1) * OWN)], gsem.at[which, layer, k])
        view = buf.at[layer, side(k, c)]
        remote(view, view, hsend.at[which, layer], hsem.at[which, layer, k], sib)

    def gather_finish(which, buf, layer, k):
        await_bytes(buf.at[layer, side(k, 1 - c)], hsem.at[which, layer, k])

    def emit(kind, layer, k, rows):
        low = rows.astype(BF16)
        for j in range(T):
            ostage[kind, layer, k, j] = low[:, j * 128 : (j + 1) * 128]
        first = xh * (chunks * ROWS) + k * ROWS + own_start
        target = pl.ds(pl.multiple_of(first, OWN), OWN)

        def away(j):
            other = lax.rem(t + j, T)
            remote(
                ostage.at[kind, layer, k, other],
                obuf.at[kind, target],
                osend.at[kind, layer],
                osem.at[kind],
                (layer, other, d),
            )

        for j in range(1, T):
            away(j)

        @pl.when(c == layer)
        def _():
            pltpu.make_async_copy(
                ostage.at[kind, layer, k, t], obuf.at[kind, target], osem.at[kind]
            ).start()

        @pl.when(c != layer)
        def _():
            away(0)

    slot = xh * 2 + xl

    def x_send(m, layer, source):
        for to in range(2):
            self_ = jnp.logical_and(jnp.logical_and(c == layer, native), xl == to)
            src, dst = source(to), xrs[m].at[slot]

            @pl.when(self_)
            def _():
                pltpu.make_async_copy(src, dst, xsem.at[m]).start()

            @pl.when(jnp.logical_not(self_))
            def _():
                remote(
                    src, dst, xsend.at[m, layer], xsem.at[m], (layer, c * Y + y, to * nz + z)
                )

    def z_peer(j):
        return (c, t, xl * nz + lax.rem(z + j, nz))

    def z_first_start(m, layer):
        for j in range(1, nz):
            for to in range(2):
                remote(
                    gbufs[m].at[layer, to * nz + lax.rem(z + j, nz)],
                    zrs[m].at[layer, j - 1, to],
                    zsend.at[m, layer],
                    zsem.at[m, layer],
                    z_peer(j),
                )

    def z_first_middle(m, layer):
        if nz > 1:
            await_bytes(zrs[m].at[layer], zsem.at[m, layer])
        for to in range(2):
            total = gbufs[m][layer, to * nz + z].astype(F32)
            for j in range(nz - 1):
                total = total + zrs[m][layer, j, to].astype(F32)
            zsums[m][layer, to] = total.astype(BF16)
        x_send(m, layer, lambda to: zsums[m].at[layer, to])

    def z_first_finish(m):
        await_bytes(xrs[m], xsem.at[m])
        return sum4(m)

    def sum4(m):
        total = xrs[m][0].astype(F32)
        for j in range(1, 4):
            total = total + xrs[m][j].astype(F32)
        return total

    def x_first_start(m, layer):
        x_send(m, layer, lambda to: gbufs[m].at[layer, pl.ds(to * nz, nz)])

    def x_first_middle(m):
        await_bytes(xrs[m], xsem.at[m])
        zsums[m][...] = sum4(m).astype(BF16)
        for j in range(1, nz):
            remote(
                zsums[m].at[lax.rem(z + j, nz)],
                zrs[m].at[j - 1],
                zsend.at[m, 0],
                zsem.at[m, 0],
                z_peer(j),
            )

    def x_first_finish(m):
        total = zsums[m][z].astype(F32)
        if nz > 1:
            await_bytes(zrs[m], zsem.at[m, 0])
        for j in range(nz - 1):
            total = total + zrs[m][j].astype(F32)
        return total

    ones = jnp.ones((8, chunks * ROWS), BF16)
    left_half = lax.broadcasted_iota(jnp.int32, (ROWS, 128), 1) < HD

    def heads(value):
        zero = jnp.zeros_like(value)
        return jnp.where(left_half, value, zero), jnp.where(left_half, zero, value)

    def each(count, body):
        def step(i, carry):
            body(i)
            return carry

        lax.fori_loop(0, count, step, 0)

    @pl.when(native)
    def _():
        pltpu.make_async_copy(vec_in, vec.at[c], vsem.at[c]).start()

    @pl.when(jnp.logical_not(native))
    def _():
        remote(vec_in, vec.at[c], vsend.at[0], vsem.at[c], home)

    remote(vec_in, vec.at[c], vsend.at[0], vsem.at[c], partner)

    @pl.when(c == 0)
    def _():
        send_weight(0)
        send_weight(1)
        send_weight(2)
        send_weight(3)

    gpack[...] = jnp.zeros_like(gpack)
    lanes = lax.broadcasted_iota(jnp.int32, (ROWS, ROWS), 1)
    places = lax.broadcasted_iota(jnp.int32, (ROWS, ROWS), 0)

    def visibility(k):
        segment = docs_ref[pl.ds(xh * chunks + k, 1)].astype(F32)
        segment = jnp.broadcast_to(segment, (ROWS, ROWS))
        visible = jnp.logical_and(lanes <= places, segment == segment.T)
        mask_ref[span(k)] = jnp.where(visible, 1.0, 0.0)

    each(chunks, visibility)
    x_copy.wait()
    ct_copy.wait()

    def start(k):
        unit, _ = standardize(x_ref[span(k)].astype(F32))
        n1[0, span(k)] = (unit * vec[0, 0:1] + vec[0, 2:3]).astype(BF16)
        hrow[0, k] = x_ref[mine(k)].astype(F32)

    await_bytes(vec.at[0], vsem.at[0])
    await_bytes(vec.at[1], vsem.at[1])
    relay(0, 0, (0,))
    each(chunks, start)
    relay(0, 0, (1,))
    relay(1, 0)

    @pl.when(c == 0)
    def _():
        weight_left(0)

    need(0, 0)
    need(1, 0)

    def attention(layer, k):
        ph = layer * 2

        @pl.when(layer == 1)
        def _():
            gather_finish(0, n1, 1, k)

        packed = mm(n1[layer, span(k)], wqkv[layer]) + vec[layer, 6:7, 0:384]
        packed = packed.astype(BF16)
        qkv[layer, span(k)] = packed
        queries, keys, values = packed[:, 0:128], packed[:, 128:256], packed[:, 256:384]
        visible = mask_ref[span(k)] > 0
        parts = []
        for head, query in enumerate(heads(queries)):
            scores = jnp.where(visible, mm_nt(query, keys) * SCALE, -1e30)
            weights_ = jnp.exp(scores - jnp.max(scores, -1, keepdims=True))
            p = weights_ * (1.0 / jnp.sum(weights_, -1, keepdims=True))
            prob[layer, k, head] = p
            parts.append(mm(p.astype(BF16), values))
        mixture = jnp.where(left_half, parts[0], parts[1]).astype(BF16)
        mix[layer, span(k)] = mixture
        part[ph, span(k)] = mm(mixture, wout[layer]).astype(BF16)
        reduce_start(ph, k)

    def second_norm(layer, k):
        rows = hrow[layer, k] + reduce_finish(layer * 2, k) + vec[layer, 3:4]
        mrow[layer, k] = rows
        unit, _ = standardize(rows)
        n2[layer, mine(k)] = (unit * vec[layer, 1:2] + vec[layer, 4:5]).astype(BF16)
        gather_start(1, n2, layer, k)

    def feed(layer, k):
        ph = layer * 2 + 1
        gather_finish(1, n2, layer, k)
        u = mm(n2[layer, span(k)], w1[layer]) + vec[layer, 7:8, 0:512]
        up[layer, span(k)] = u
        g = 0.5 * u * (1.0 + jnp.tanh(GELU_C * (u + GELU_A * (u * u * u))))
        g = g.astype(BF16)
        act[layer, span(k)] = g
        part[ph, span(k)] = mm(g, w2[layer]).astype(BF16)
        reduce_start(ph, k)

    def finish(layer, k):
        rows = mrow[layer, k] + reduce_finish(layer * 2 + 1, k) + vec[layer, 5:6]

        @pl.when(layer == 0)
        def _():
            entering = rows.astype(BF16).astype(F32)
            hrow[1, k] = entering
            unit, _ = standardize(entering)
            n1[1, mine(k)] = (unit * vec[1, 0:1] + vec[1, 2:3]).astype(BF16)
            gather_start(0, n1, 1, k)

        ledger[0, k] = rows

    def feed_back(layer, k):
        ph = 6 - layer * 2

        @pl.when(layer == 0)
        def _():
            gather_finish(3, dyr, 0, k)

        grad = mm_nt(dyr[layer, span(k)], w2[layer])
        u = up[layer, span(k)]
        bend = jnp.tanh(GELU_C * (u + GELU_A * (u * u * u)))
        slope = 0.5 * (1.0 + bend) + (0.5 * u) * (1.0 - bend * bend) * (
            GELU_C * (1.0 + (3.0 * GELU_A) * (u * u))
        )
        du = (grad * slope).astype(BF16)
        dup[span(k)] = du
        part[ph, span(k)] = mm_nt(du, w1[layer]).astype(BF16)
        reduce_start(ph, k)

    def middle(layer, k):
        grad = dyr[layer, mine(k)].astype(F32)
        inner = reduce_finish(6 - layer * 2, k)
        slope, product = norm_back(mrow[layer, k], vec[layer, 1:2], inner)
        dm = grad + slope
        mrow[layer, k] = dm
        low = dm.astype(BF16)
        dmr[layer, mine(k)] = low
        gather_start(2, dmr, layer, k)
        ledger[0, k] = product
        ledger[1, k] = inner
        ledger[2, k] = low.astype(F32)
        ledger[3, k] = grad

    def attention_back(layer, k):
        ph = 7 - layer * 2
        gather_finish(2, dmr, layer, k)
        da = mm_nt(dmr[layer, span(k)], wout[layer]).astype(BF16)
        packed = qkv[layer, span(k)]
        queries, keys, values = packed[:, 0:128], packed[:, 128:256], packed[:, 256:384]
        dqs, dks, dvs = [], [], []
        for head, grad in enumerate(heads(da)):
            p = prob[layer, k, head]
            dvs.append(mm_tn(p.astype(BF16), da))
            dp = mm_nt(grad, values)
            ds = p * (dp - jnp.sum(p * dp, -1, keepdims=True))
            ds = ds.astype(BF16)
            dqs.append(mm(ds, keys))
            dks.append(mm_tn(ds, queries))
        grads = jnp.concatenate(
            [
                jnp.where(left_half, dqs[0], dqs[1]) * SCALE,
                jnp.where(left_half, dks[0], dks[1]) * SCALE,
                jnp.where(left_half, dvs[0], dvs[1]),
            ],
            1,
        ).astype(BF16)
        dqkv[span(k)] = grads
        part[ph, span(k)] = mm_nt(grads, wqkv[layer]).astype(BF16)
        reduce_start(ph, k)

    def column_sum(layer, row, which):
        total = jnp.sum(ledger[which, 0], 0, keepdims=True)
        for k in range(1, chunks):
            total = total + jnp.sum(ledger[which, k], 0, keepdims=True)
        gpack[layer, row : row + 1] = total

    def last(layer, k):
        inner = reduce_finish(7 - layer * 2, k)
        slope, product = norm_back(hrow[layer, k], vec[layer, 0:1], inner)
        rows = mrow[layer, k] + slope

        @pl.when(layer == 1)
        def _():
            dyr[0, mine(k)] = rows.astype(BF16)
            gather_start(3, dyr, 0, k)

        ledger[0, k] = product
        ledger[1, k] = inner
        ledger[2, k] = rows

    pieces = 2 * nz
    wide = D // pieces

    def grad_down(layer, b):
        cols = pl.ds(pl.multiple_of(b * 128, 128), 128)
        block = mm_tn(act[layer, :, cols], dyr[layer]).astype(BF16)
        for q in range(pieces):
            gbufs[0][layer, q, cols] = block[:, q * wide : (q + 1) * wide]

    up_wide = max(256 // wide, 1)
    up_steps = pieces // up_wide

    def grad_up(layer, b):
        size = wide * up_wide
        cols = pl.ds(pl.multiple_of(b * size, size), size)
        block = mm_tn(n2[layer, :, cols], dup[...]).astype(BF16)
        for q in range(up_wide):
            gbufs[1][layer, b * up_wide + q] = block[q * wide : (q + 1) * wide]

    def grad_out(layer):
        block = mm_tn(mix[layer], dmr[layer]).astype(BF16)
        for q in range(pieces):
            gbufs[4][layer, q] = block[:, q * wide : (q + 1) * wide]

    def grad_qkv(layer, b):
        size = wide * up_wide
        cols = pl.ds(pl.multiple_of(b * size, size), size)
        block = mm_tn(n1[layer, :, cols], dqkv[...]).astype(BF16)
        for q in range(up_wide):
            rows = slice(q * wide, (q + 1) * wide)
            gbufs[2][layer, b * up_wide + q] = block[rows, 0:256]
            gbufs[3][layer, b * up_wide + q] = block[rows, 256:384]

    def small_start(layer):
        for j in range(T):
            sstage[layer, j] = gpack[layer, :, j * 128 : (j + 1) * 128]
            sbias[layer, j : j + 1] = gpack[layer, 6:7, j * 128 : (j + 1) * 128]

        def send(src, dst, to, self_):
            @pl.when(self_)
            def _():
                pltpu.make_async_copy(src, dst, ssem.at[0]).start()

            @pl.when(jnp.logical_not(self_))
            def _():
                remote(src, dst, ssend.at[layer], ssem.at[0], (layer, to, d))

        for j in range(T):
            to = lax.rem(t + j, T)
            src, dst = sstage.at[layer, to], sgot.at[c * T + t]
            if j:
                remote(src, dst, ssend.at[layer], ssem.at[0], (layer, to, d))
            else:
                send(src, dst, to, c == layer)
        send(
            sbias.at[layer],
            sgot.at[2 * T + xh],
            c * Y + y,
            jnp.logical_and(c == layer, native),
        )

    def small_middle():
        await_bytes(sgot, ssem.at[0])
        total = sgot[0]
        for j in range(1, 2 * T):
            total = total + sgot[j]
        ssum[0] = total
        ssum[1] = sgot[2 * T] + sgot[2 * T + 1]
        for j in range(1, 2 * nz):
            to = lax.rem(d + j, 2 * nz)
            remote(ssum, sall.at[j - 1], ssend.at[2], ssem.at[1], (c, t, to))

    def small_finish():
        await_bytes(sall, ssem.at[1])
        total = ssum[...]
        for j in range(2 * nz - 1):
            total = total + sall[j]
        return total

    def collect_attention(layer):
        z_first_middle(2, layer)

        @pl.when(c == layer)
        def _():
            x_first_middle(3)
            x_first_middle(4)
            small_middle()

    def on(condition, body, *args):
        @pl.when(condition)
        def _():
            body(*args)

    def stage_body(stage):
        odd = lax.rem(stage, 2)
        ahead = stage < 4
        layer = jnp.where(ahead, stage // 2, 3 - stage // 2)
        front_even = jnp.logical_and(ahead, odd == 0)
        front_odd = jnp.logical_and(ahead, odd == 1)
        back_even = jnp.logical_and(stage >= 4, odd == 0)
        back_odd = jnp.logical_and(stage >= 4, odd == 1)

        @pl.when(stage == 1)
        def _():
            need(2, 0)
            need(3, 0)

        @pl.when(stage == 2)
        def _():
            need(0, 1)
            need(1, 1)

        @pl.when(stage == 3)
        def _():
            need(2, 1)
            need(3, 1)

        def step(s):
            @pl.when(s < chunks)
            def _():
                on(front_odd, gather_middle, 1, n2, layer, s)
                on(stage == 2, gather_middle, 0, n1, 1, s)
                on(back_odd, gather_middle, 2, dmr, layer, s)
                on(stage == 6, gather_middle, 3, dyr, 0, s)

            @pl.when(jnp.logical_and(s >= 1, s < chunks + 1))
            def _():
                on(front_even, attention, layer, s - 1)
                on(front_odd, feed, layer, s - 1)
                on(back_even, feed_back, layer, s - 1)
                on(back_odd, attention_back, layer, s - 1)

            @pl.when(s >= 2)
            def _():
                reduce_middle(stage, s - 2)

            @pl.when(jnp.logical_and(stage == 0, s == 1))
            def _():
                relay(2, 0)
            @pl.when(jnp.logical_and(stage == 0, s == 3))
            def _():
                relay(3, 0)

        each(chunks + 2, step)
        @pl.when(stage == 1)
        def _():
            relay(0, 1)
        @pl.when(stage == 1)
        def _():
            relay(1, 1)

        @pl.when(stage == 0)
        def _():
            @pl.when(c == 1)
            def _():
                for i in range(4):
                    send_weight(i)

        @pl.when(stage == 4)
        def _():
            each(chunks, lambda k: finish(1, k))
            each(chunks, lambda k: emit(0, 1, k, ledger[0, k]))

        @pl.when(back_even)
        def _():
            each(4, lambda b: grad_down(layer, b))
            z_first_start(0, layer)

        @pl.when(back_odd)
        def _():
            grad_out(layer)
            x_first_start(4, layer)
            each(up_steps, lambda b: grad_qkv(layer, b))
            z_first_start(2, layer)
            x_first_start(3, layer)
            gpack[layer, 6:7, 0:384] = mm(ones, dqkv[...])[0:1]

        def settle(k):
            on(front_even, second_norm, layer, k)
            on(stage == 1, finish, 0, k)
            on(back_even, middle, layer, k)
            on(back_odd, last, layer, k)

        on(stage != 3, each, chunks, settle)
        @pl.when(stage == 1)
        def _():
            relay(2, 1)
        @pl.when(stage == 1)
        def _():
            relay(3, 1)


        @pl.when(back_even)
        def _():
            each(up_steps, lambda b: grad_up(layer, b))
            x_first_start(1, layer)
            column_sum(layer, 1, 0)
            column_sum(layer, 4, 1)
            column_sum(layer, 3, 2)
            column_sum(layer, 5, 3)
            gpack[layer, 6:7, 384:896] = mm(ones, dup[...])[0:1]

        @pl.when(stage == 1)
        def _():
            each(chunks, lambda k: emit(0, 0, k, ledger[0, k]))

        @pl.when(back_odd)
        def _():
            column_sum(layer, 0, 0)
            column_sum(layer, 2, 1)
            small_start(layer)
            each(chunks, lambda k: emit(1, layer, k, ledger[2, k]))

        on(stage == 5, z_first_middle, 0, layer)
        on(jnp.logical_and(stage == 5, c == 1), x_first_middle, 1)
        on(stage == 6, collect_attention, 1)

    each(8, stage_body)
    z_first_middle(0, 0)
    on(c == 0, x_first_middle, 1)
    collect_attention(0)

    places_ = layout(nz)

    def put(name, value, start=0):
        rows = value.shape[0]
        first = places_[name] + start * rows
        for j in range(value.shape[1] // 128):
            grads_ref[first + j * rows : first + (j + 1) * rows] = value[:, j * 128 : (j + 1) * 128]

    put("down", z_first_finish(0))
    put("up", x_first_finish(1))
    small = small_finish()
    put("small", small[0])
    put("bias", small[1])
    put("qkv", x_first_finish(3), 2)
    put("out", x_first_finish(4))
    put("qkv", z_first_finish(2))
    for kind in range(2):
        await_bytes(obuf.at[kind], osem.at[kind])
    rows_ref[...] = obuf[...]

    for i in range(4):
        both = weights[i][1]

        @pl.when(jnp.logical_not(native))
        def _():
            await_bytes(both.at[0], whome.at[i])
            for layer in range(2):
                await_bytes(whole_half(i), wrelay.at[i, layer])

        if i:
            weight_left(i)

    @pl.when(c == 1)
    def _():
        weight_left(0)

    @pl.when(jnp.logical_not(native))
    def _():
        await_bytes(vec.at[0], vsend.at[0])

    await_bytes(vec.at[0], vsend.at[0])
    for ph in range(8):
        await_bytes(cbuf.at[ph], csend.at[ph])
        await_bytes(rs.at[ph], rsend.at[ph])
    for which, layer in ((0, 1), (1, 0), (1, 1), (2, 0), (2, 1), (3, 0)):
        await_bytes(rs.at[0], gsend.at[which, layer])
        await_bytes(cbuf.at[0], hsend.at[which, layer])
    for layer in range(2):
        for kind in range(2):

            @pl.when(c == layer)
            def _():
                view = ostage.at[kind, layer, :, pl.ds(0, T - 1)]
                await_bytes(view, osend.at[kind, layer])

            @pl.when(c != layer)
            def _():
                await_bytes(ostage.at[kind, layer], osend.at[kind, layer])

        self_ = jnp.logical_and(c == layer, native)
        for m in range(5):
            if nz > 1 and m in (0, 2):
                await_bytes(zrs[m].at[layer], zsend.at[m, layer])
            await_bytes(xrs[m].at[0], xsend.at[m, layer])

            @pl.when(jnp.logical_not(self_))
            def _():
                await_bytes(xrs[m].at[0], xsend.at[m, layer])

        await_bytes(sgot.at[pl.ds(0, T - 1)], ssend.at[layer])

        @pl.when(c != layer)
        def _():
            await_bytes(sgot.at[0], ssend.at[layer])

        @pl.when(jnp.logical_not(self_))
        def _():
            await_bytes(sgot.at[0], ssend.at[layer])

    if nz > 1:
        for m in (1, 3, 4):
            await_bytes(zrs[m], zsend.at[m, 0])
    await_bytes(sall, ssend.at[2])


def layout(nz):
    wide = D // (2 * nz)
    sizes = (
        ("qkv", 3 * wide),
        ("up", 4 * wide),
        ("down", 4 * wide),
        ("out", wide),
        ("small", 8),
        ("bias", 8),
    )
    places, first = {}, 0
    for name, size in sizes:
        places[name] = first
        first += size
    places["end"] = first
    return places


def core(chunks, nz, x, ct, docs, wqkv, wout, w1, w2, qb, b1, gains, shifts):
    n = chunks * ROWS
    vm = pl.BlockSpec(memory_space=pltpu.VMEM)
    hbm = pl.BlockSpec(memory_space=pl.ANY)
    pieces = 2 * nz
    wide = D // pieces
    out_shape = (
        jax.ShapeDtypeStruct((2, 2 * n, 128), BF16),
        jax.ShapeDtypeStruct((layout(nz)["end"], 128), F32),
    )
    dma = pltpu.SemaphoreType.DMA
    shape = ((512, wide), (wide, 512), (wide, 256), (wide, 128), (128, wide))
    back = max(nz - 1, 1)
    gbufs = [pltpu.VMEM((2, pieces) + s, BF16) for s in shape]
    zrs, zsums, xrs = [], [], []
    for m, s in enumerate(shape):
        if m in (0, 2):
            zrs.append(pltpu.VMEM((2, back, 2) + s, BF16))
            zsums.append(pltpu.VMEM((2, 2) + s, BF16))
            xrs.append(pltpu.VMEM((4,) + s, BF16))
        else:
            zrs.append(pltpu.VMEM((back,) + s, BF16))
            zsums.append(pltpu.VMEM((nz,) + s, BF16))
            xrs.append(pltpu.VMEM((4, nz) + s, BF16))
    scratch = [
        pltpu.VMEM((n, D), BF16),
        pltpu.VMEM((n, ROWS), F32),
        pltpu.VMEM((8, D), F32),
        pltpu.VMEM((2, D, 384), BF16),
        pltpu.VMEM((2, 128, D), BF16),
        pltpu.VMEM((2, D, 512), BF16),
        pltpu.VMEM((2, 512, D), BF16),
        pltpu.VMEM((2, 8, D), F32),
        pltpu.VMEM((2, n, D), BF16),
        pltpu.VMEM((2, n, D), BF16),
        pltpu.VMEM((2, n, D), BF16),
        pltpu.VMEM((2, n, D), BF16),
        pltpu.VMEM((2, n, 384), BF16),
        pltpu.VMEM((2, n, 128), BF16),
        pltpu.VMEM((2, chunks, 2, ROWS, ROWS), F32),
        pltpu.VMEM((2, n, 512), F32),
        pltpu.VMEM((2, n, 512), BF16),
        pltpu.VMEM((n, 512), BF16),
        pltpu.VMEM((n, 384), BF16),
        pltpu.VMEM((2, chunks, OWN, D), F32),
        pltpu.VMEM((2, chunks, OWN, D), F32),
        pltpu.VMEM((4, chunks, OWN, D), F32),
        pltpu.VMEM((8, n, D), BF16),
        pltpu.VMEM((8, chunks, ROWS // 2, D), BF16),
        pltpu.VMEM((8, chunks, ROWS // 2, D), BF16),
        pltpu.VMEM((8, chunks, Y - 1, OWN, D), BF16),
        pltpu.VMEM((2, 2, chunks, T, OWN, 128), BF16),
        pltpu.VMEM((2, 2 * n, 128), BF16),
        gbufs,
        zrs,
        zsums,
        xrs,
        pltpu.VMEM((2, 8, D), F32),
        pltpu.VMEM((2, T, 8, 128), F32),
        pltpu.VMEM((2, 8, 128), F32),
        pltpu.VMEM((2 * T + 2, 8, 128), F32),
        pltpu.VMEM((2, 8, 128), F32),
        pltpu.VMEM((pieces - 1, 2, 8, 128), F32),
        dma((2,)),
        dma((4, 2, 2, PARTS)),
        dma((4,)),
        dma((4,)),
        dma((4, 2)),
        dma((2,)),
        dma((1,)),
        dma((8, chunks)),
        dma((8,)),
        dma((8, chunks)),
        dma((8,)),
        dma((4, 2, chunks)),
        dma((4, 2)),
        dma((4, 2, chunks)),
        dma((4, 2)),
        dma((2,)),
        dma((2, 2)),
        dma((5, 2)),
        dma((5, 2)),
        dma((5,)),
        dma((5, 2)),
        dma((2,)),
        dma((3,)),
    ]
    return pl.pallas_call(
        functools.partial(kernel, chunks, nz),
        out_shape=out_shape,
        in_specs=[hbm, hbm, vm, hbm, hbm, hbm, hbm, vm, vm, vm, vm],
        out_specs=[vm] * 2,
        scratch_shapes=scratch,
        compiler_params=pltpu.CompilerParams(
            collective_id=0, has_side_effects=True, vmem_limit_bytes=62 * 2**20
        ),
        name="layers",
    )(x, ct, docs, wqkv, wout, w1, w2, qb, b1, gains, shifts)


def closing(
    m,
    rows_in,
    grads_in,
    sec_out,
    ing_out,
    gqkv_out,
    qb_out,
    gout_out,
    g1_out,
    b1_out,
    g2_out,
    gains_out,
    shifts_out,
    rows,
    grads,
    sems,
):
    d = lax.axis_index("dp")
    rows_copy = pltpu.make_async_copy(rows_in, rows, sems.at[0])
    grads_copy = pltpu.make_async_copy(grads_in, grads, sems.at[1])
    rows_copy.start()
    grads_copy.start()
    rows_copy.wait()
    sec_out[0] = rows[0].astype(F32)
    ing_out[0] = rows[1].astype(F32)
    grads_copy.wait()
    places = layout(m // 2)
    width = D // m

    def get(name, height, j):
        first = places[name] + j * height
        return grads[first : first + height]

    for j in range(3):
        gqkv_out[0, j] = get("qkv", width, j)
    for j in range(4):
        g1_out[0, :, j * 128 : (j + 1) * 128] = get("up", width, j)
    for j in range(width // 128):
        gout_out[0, :, j * 128 : (j + 1) * 128] = get("out", 128, j)
        g2_out[0, :, j * 128 : (j + 1) * 128] = get("down", 512, j)
    share = 128 // m
    shift = lax.rem(128 - d * share, 128)
    rolled = pltpu.roll(get("small", 8, 0), shift, 1)
    gains_out[0] = rolled[0:2, 0:share]
    shifts_out[0] = rolled[2:6, 0:share]
    bias = get("bias", 8, 0)
    rolled = pltpu.roll(bias, shift, 1)
    for j in range(2):
        qb_out[0, j : j + 1] = rolled[2 * j : 2 * j + 1, 0:share]
    lines = lax.broadcasted_iota(jnp.int32, (8, 128), 0)

    def line(block, which):
        return jnp.sum(jnp.where(lines == which, block, 0.0), 0, keepdims=True)

    wide = 512 // m
    if wide >= 128:
        for j in range(wide // 128):
            b1_out[:, j * 128 : (j + 1) * 128] = line(bias, 3 + d * (wide // 128) + j)
    else:
        per = 128 // wide
        rolled = pltpu.roll(bias, lax.rem(128 - lax.rem(d, per) * wide, 128), 1)
        b1_out[...] = line(rolled, 3 + d // per)[:, 0:wide]


def shards(
    inputs,
    cotangent,
    doc_ids,
    qkv_weight,
    qkv_bias,
    out_weight,
    fc1_weight,
    fc1_bias,
    fc2_weight,
    norm_gains,
    shifts,
):
    m = lax.axis_size("dp")
    chunks = doc_ids.shape[0] // 2
    n = chunks * ROWS
    results = core(
        chunks,
        m // 2,
        inputs,
        cotangent,
        doc_ids,
        qkv_weight[0].transpose(1, 0, 2),
        out_weight[0],
        fc1_weight[0],
        fc2_weight[0],
        qkv_bias,
        fc1_bias,
        norm_gains,
        shifts,
    )
    vm = pl.BlockSpec(memory_space=pltpu.VMEM)
    shapes = (
        (1, 2 * n, 128),
        (1, 2 * n, 128),
        (1, 3, D // m, 128),
        (1, 2, 128 // m),
        (1, 128, D // m),
        (1, D // m, 512),
        (1, 512 // m),
        (1, 512, D // m),
        (1, 2, 128 // m),
        (1, 4, 128 // m),
    )
    outs = pl.pallas_call(
        functools.partial(closing, m),
        out_shape=[jax.ShapeDtypeStruct(shape, F32) for shape in shapes],
        in_specs=[pl.BlockSpec(memory_space=pl.ANY)] * 2,
        out_specs=[vm] * 10,
        scratch_shapes=[
            pltpu.VMEM(results[0].shape, BF16),
            pltpu.VMEM(results[1].shape, F32),
            pltpu.SemaphoreType.DMA((2,)),
        ],
        compiler_params=pltpu.CompilerParams(vmem_limit_bytes=62 * 2**20),
        name="closing",
    )(*results)
    return (*outs[:2], outs[2].transpose(0, 2, 1, 3), *outs[3:])


def solution(mesh):
    return jax.shard_map(
        shards,
        mesh=mesh,
        in_specs=(
            P("dp", None),
            P("dp", None),
            P("dp", None),
            P("pipe", None, None, "tensor"),
            P("pipe", None, "tensor"),
            P("pipe", "tensor", None),
            P("pipe", None, "tensor"),
            P("pipe", "tensor"),
            P("pipe", "tensor", None),
            P("pipe", None, None),
            P("pipe", None, None),
        ),
        out_specs=(
            P("pipe", "dp", "tensor"),
            P("pipe", "dp", "tensor"),
            P("pipe", "dp", None, "tensor"),
            P("pipe", None, ("tensor", "dp")),
            P("pipe", "tensor", "dp"),
            P("pipe", "dp", "tensor"),
            P("pipe", ("tensor", "dp")),
            P("pipe", "tensor", "dp"),
            P("pipe", None, ("tensor", "dp")),
            P("pipe", None, ("tensor", "dp")),
        ),
        check_vma=False,
    )
```

```python
import functools

import jax
import jax.numpy as jnp
from jax import lax
from jax.experimental import pallas as pl
from jax.experimental.pallas import tpu as pltpu
from jax.sharding import PartitionSpec as P

MESH = pl.DeviceIdType.MESH
F32 = jnp.float32
BF16 = jnp.bfloat16
EPSILON = 1e-05
HD = 64
SCALE = HD**-0.5
D = 1024
ROWS = 128
T = 8
Y = 4
PARTS = 2
OWN = ROWS // T
GELU_C = 0.7978845608028654
GELU_A = 0.044715


def mm(a, b):
    return lax.dot_general(a, b, (((1,), (0,)), ((), ())), preferred_element_type=F32)


def mm_nt(a, b):
    return lax.dot_general(a, b, (((1,), (1,)), ((), ())), preferred_element_type=F32)


def mm_tn(a, b):
    return lax.dot_general(a, b, (((0,), (0,)), ((), ())), preferred_element_type=F32)


def standardize(rows):
    centered = rows - jnp.mean(rows, -1, keepdims=True)
    variance = jnp.mean(centered * centered, -1, keepdims=True)
    root = lax.rsqrt(variance + EPSILON)
    return centered * root, root


def norm_back(rows, gain, grad):
    unit, root = standardize(rows)
    e = grad * gain
    slope = root * (
        e - jnp.mean(e, -1, keepdims=True) - unit * jnp.mean(e * unit, -1, keepdims=True)
    )
    return slope, grad * unit


def kernel(
    chunks,
    nz,
    x_in,
    ct_in,
    docs_ref,
    wqkv_in,
    wout_in,
    w1_in,
    w2_in,
    qb_in,
    b1_in,
    gains_in,
    shifts_in,
    rows_ref,
    grads_ref,
    x_ref,
    mask_ref,
    vec_in,
    wqkv,
    wout,
    w1,
    w2,
    vec,
    n1,
    n2,
    dmr,
    dyr,
    qkv,
    mix,
    prob,
    up,
    act,
    dup,
    dqkv,
    hrow,
    mrow,
    ledger,
    part,
    cbuf,
    psum,
    rs,
    ostage,
    obuf,
    gbufs,
    zrs,
    zsums,
    xrs,
    gpack,
    sstage,
    sbias,
    sgot,
    ssum,
    sall,
    insem,
    wsem,
    wsend,
    whome,
    wrelay,
    vsem,
    vsend,
    csem,
    csend,
    rsem,
    rsend,
    gsem,
    gsend,
    hsem,
    hsend,
    osem,
    osend,
    zsem,
    zsend,
    xsem,
    xsend,
    ssem,
    ssend,
):
    c = lax.axis_index("pipe")
    t = lax.axis_index("tensor")
    d = lax.axis_index("dp")
    xh = t // Y
    y = lax.rem(t, Y)
    xl = d // nz
    z = lax.rem(d, nz)
    sib = (1 - c, t, d)

    first_row = pl.ds(pl.multiple_of(xh * (chunks * ROWS), ROWS), chunks * ROWS)
    x_copy = pltpu.make_async_copy(x_in.at[first_row], x_ref, insem.at[0])
    ct_copy = pltpu.make_async_copy(ct_in.at[first_row], dyr.at[1], insem.at[1])
    x_copy.start()
    ct_copy.start()

    barrier = pltpu.get_barrier_semaphore()

    def greet(device):
        pl.semaphore_signal(barrier, inc=1, device_id=device, device_id_type=MESH)

    for j in range(T):
        other = lax.rem(t + j, T)
        if j:
            greet((c, other, d))
        greet((1 - c, other, d))
    far = (1 - xl) * nz + z
    for core_ in range(2):
        for j in range(2):
            greet((core_, j * Y + y, far))
    for j in range(1, nz):
        greet((c, t, xl * nz + lax.rem(z + j, nz)))
        greet((c, t, (1 - xl) * nz + lax.rem(z + j, nz)))
    vec_in[...] = jnp.zeros_like(vec_in)
    vec_in[0:2] = gains_in[0].astype(F32)
    vec_in[2:6] = shifts_in[0].astype(F32)
    vec_in[6:7, 0:128] = qb_in[0, 0:1].astype(F32)
    vec_in[6:7, 256:384] = qb_in[0, 1:2].astype(F32)
    vec_in[7:8, 0:512] = b1_in[...].astype(F32)
    pl.semaphore_wait(barrier, 2 * T - 1 + 4 + 2 * (nz - 1))

    def remote(src, dst, send, recv, device):
        pltpu.make_async_remote_copy(
            src_ref=src,
            dst_ref=dst,
            send_sem=send,
            recv_sem=recv,
            device_id=device,
            device_id_type=MESH,
        ).start()

    def await_bytes(view, sem):
        pltpu.make_async_copy(view, view, sem).wait()

    weights = ((wqkv_in, wqkv), (wout_in, wout), (w1_in, w1), (w2_in, w2))
    native = c == xh
    partner = (xh, (1 - xh) * Y + y, far)
    home = (xh, t, d)

    def half(i, which, q):
        size = weights[i][1].shape[1] // (2 * PARTS)
        return pl.ds(pl.multiple_of((which * PARTS + q) * size, size), size)

    def views(i, h, q):
        own, both = weights[i]
        piece = half(i, h, q)
        if i:
            return [(own.at[piece], both.at[c, piece])]
        return [
            (own.at[j, piece], both.at[c, piece, pl.ds(j * 128, 128)]) for j in range(3)
        ]

    def send_weight(i):
        for q in range(PARTS):
            for src, dst in views(i, xl, q):
                remote(src, dst, wsend.at[i], wsem.at[i, c, xl, q], partner)
        for h in range(2):
            for q in range(PARTS):
                for src, dst in views(i, h, q):

                    @pl.when(native)
                    def _():
                        pltpu.make_async_copy(src, dst, wsem.at[i, c, h, q]).start()

                    @pl.when(jnp.logical_not(native))
                    def _():
                        remote(src, dst, whome.at[i], wsem.at[i, c, h, q], home)

    def whole_half(i):
        return weights[i][1].at[0, pl.ds(0, weights[i][1].shape[1] // 2)]

    def weight_left(i):
        await_bytes(whole_half(i), wsend.at[i])

    def await_half(i, layer, h, q):
        await_bytes(weights[i][1].at[layer, half(i, h, q)], wsem.at[i, layer, h, q])

    def relay(i, layer, parts=tuple(range(PARTS))):
        both = weights[i][1]

        @pl.when(jnp.logical_not(native))
        def _():
            for q in parts:
                await_half(i, layer, 1 - xl, q)
                piece = both.at[layer, half(i, 1 - xl, q)]
                remote(
                    piece, piece, wrelay.at[i, layer], wsem.at[i, layer, 1 - xl, q], (c, t, far)
                )

    def need(i, layer):
        for q in range(PARTS):

            @pl.when(native)
            def _():
                await_half(i, layer, 1 - xl, q)

            await_half(i, layer, xl, q)

    def span(k):
        return pl.ds(pl.multiple_of(k * ROWS, ROWS), ROWS)

    def side(k, who):
        return pl.ds(pl.multiple_of(k * ROWS + who * (ROWS // 2), ROWS // 2), ROWS // 2)

    own_start = (c * Y + y) * OWN

    def mine(k):
        return pl.ds(pl.multiple_of(k * ROWS + own_start, OWN), OWN)

    def y_peer(j):
        return (c, xh * Y + lax.rem(y + j, Y), d)

    def reduce_start(ph, k):
        remote(
            part.at[ph, side(k, 1 - c)], cbuf.at[ph, k], csend.at[ph], csem.at[ph, k], sib
        )

    def reduce_middle(ph, k):
        await_bytes(cbuf.at[ph, k], csem.at[ph, k])
        psum[ph, k] = (part[ph, side(k, c)].astype(F32) + cbuf[ph, k].astype(F32)).astype(BF16)
        for j in (2, 1, 3):
            rows = pl.ds(pl.multiple_of(lax.rem(y + j, Y) * OWN, OWN), OWN)
            remote(
                psum.at[ph, k, rows], rs.at[ph, k, j - 1], rsend.at[ph], rsem.at[ph, k], y_peer(j)
            )

    def reduce_finish(ph, k):
        await_bytes(rs.at[ph, k], rsem.at[ph, k])
        rows = pl.ds(pl.multiple_of(y * OWN, OWN), OWN)
        total = psum[ph, k, rows].astype(F32)
        for j in range(Y - 1):
            total = total + rs[ph, k, j].astype(F32)
        return total

    def gather_start(which, buf, layer, k):
        for j in (2, 1, 3):
            view = buf.at[layer, mine(k)]
            remote(view, view, gsend.at[which, layer], gsem.at[which, layer, k], y_peer(j))

    def gather_middle(which, buf, layer, k):
        await_bytes(buf.at[layer, pl.ds(0, (Y - 1) * OWN)], gsem.at[which, layer, k])
        view = buf.at[layer, side(k, c)]
        remote(view, view, hsend.at[which, layer], hsem.at[which, layer, k], sib)

    def gather_finish(which, buf, layer, k):
        await_bytes(buf.at[layer, side(k, 1 - c)], hsem.at[which, layer, k])

    def emit(kind, layer, k, rows):
        low = rows.astype(BF16)
        for j in range(T):
            ostage[kind, layer, k, j] = low[:, j * 128 : (j + 1) * 128]
        first = xh * (chunks * ROWS) + k * ROWS + own_start
        target = pl.ds(pl.multiple_of(first, OWN), OWN)

        def away(j):
            other = lax.rem(t + j, T)
            remote(
                ostage.at[kind, layer, k, other],
                obuf.at[kind, target],
                osend.at[kind, layer],
                osem.at[kind],
                (layer, other, d),
            )

        for j in range(1, T):
            away(j)

        @pl.when(c == layer)
        def _():
            pltpu.make_async_copy(
                ostage.at[kind, layer, k, t], obuf.at[kind, target], osem.at[kind]
            ).start()

        @pl.when(c != layer)
        def _():
            away(0)

    slot = xh * 2 + xl

    def x_send(m, layer, source):
        for to in range(2):
            self_ = jnp.logical_and(jnp.logical_and(c == layer, native), xl == to)
            src, dst = source(to), xrs[m].at[slot]

            @pl.when(self_)
            def _():
                pltpu.make_async_copy(src, dst, xsem.at[m]).start()

            @pl.when(jnp.logical_not(self_))
            def _():
                remote(
                    src, dst, xsend.at[m, layer], xsem.at[m], (layer, c * Y + y, to * nz + z)
                )

    def z_peer(j):
        return (c, t, xl * nz + lax.rem(z + j, nz))

    def z_first_start(m, layer):
        for j in range(1, nz):
            for to in range(2):
                remote(
                    gbufs[m].at[layer, to * nz + lax.rem(z + j, nz)],
                    zrs[m].at[layer, j - 1, to],
                    zsend.at[m, layer],
                    zsem.at[m, layer],
                    z_peer(j),
                )

    def z_first_middle(m, layer):
        if nz > 1:
            await_bytes(zrs[m].at[layer], zsem.at[m, layer])
        for to in range(2):
            total = gbufs[m][layer, to * nz + z].astype(F32)
            for j in range(nz - 1):
                total = total + zrs[m][layer, j, to].astype(F32)
            zsums[m][layer, to] = total.astype(BF16)
        x_send(m, layer, lambda to: zsums[m].at[layer, to])

    def z_first_finish(m):
        await_bytes(xrs[m], xsem.at[m])
        return sum4(m)

    def sum4(m):
        total = xrs[m][0].astype(F32)
        for j in range(1, 4):
            total = total + xrs[m][j].astype(F32)
        return total

    def x_first_start(m, layer):
        x_send(m, layer, lambda to: gbufs[m].at[layer, pl.ds(to * nz, nz)])

    def x_first_middle(m):
        await_bytes(xrs[m], xsem.at[m])
        zsums[m][...] = sum4(m).astype(BF16)
        for j in range(1, nz):
            remote(
                zsums[m].at[lax.rem(z + j, nz)],
                zrs[m].at[j - 1],
                zsend.at[m, 0],
                zsem.at[m, 0],
                z_peer(j),
            )

    def x_first_finish(m):
        total = zsums[m][z].astype(F32)
        if nz > 1:
            await_bytes(zrs[m], zsem.at[m, 0])
        for j in range(nz - 1):
            total = total + zrs[m][j].astype(F32)
        return total

    ones = jnp.ones((8, chunks * ROWS), BF16)
    left_half = lax.broadcasted_iota(jnp.int32, (ROWS, 128), 1) < HD

    def heads(value):
        zero = jnp.zeros_like(value)
        return jnp.concatenate(
            [jnp.where(left_half, value, zero), jnp.where(left_half, zero, value)], 0
        )

    def beside(value):
        return jnp.concatenate([value[0:ROWS], value[ROWS:]], 1)

    def each(count, body):
        def step(i, carry):
            body(i)
            return carry

        lax.fori_loop(0, count, step, 0)

    @pl.when(native)
    def _():
        pltpu.make_async_copy(vec_in, vec.at[c], vsem.at[c]).start()

    @pl.when(jnp.logical_not(native))
    def _():
        remote(vec_in, vec.at[c], vsend.at[0], vsem.at[c], home)

    remote(vec_in, vec.at[c], vsend.at[0], vsem.at[c], partner)

    @pl.when(c == 0)
    def _():
        send_weight(0)
        send_weight(1)
        send_weight(2)
        send_weight(3)

    gpack[...] = jnp.zeros_like(gpack)
    lanes = lax.broadcasted_iota(jnp.int32, (ROWS, ROWS), 1)
    places = lax.broadcasted_iota(jnp.int32, (ROWS, ROWS), 0)

    def visibility(k):
        segment = docs_ref[pl.ds(xh * chunks + k, 1)].astype(F32)
        segment = jnp.broadcast_to(segment, (ROWS, ROWS))
        visible = jnp.logical_and(lanes <= places, segment == segment.T)
        mask_ref[span(k)] = jnp.where(visible, 1.0, 0.0)

    each(chunks, visibility)
    x_copy.wait()
    ct_copy.wait()

    def start(k):
        unit, _ = standardize(x_ref[span(k)].astype(F32))
        n1[0, span(k)] = (unit * vec[0, 0:1] + vec[0, 2:3]).astype(BF16)
        hrow[0, k] = x_ref[mine(k)].astype(F32)

    await_bytes(vec.at[0], vsem.at[0])
    await_bytes(vec.at[1], vsem.at[1])
    relay(0, 0, (0,))
    each(chunks, start)
    relay(0, 0, (1,))
    relay(1, 0)

    @pl.when(c == 0)
    def _():
        weight_left(0)

    need(0, 0)
    need(1, 0)

    def attention(layer, k):
        ph = layer * 2

        @pl.when(layer == 1)
        def _():
            gather_finish(0, n1, 1, k)

        packed = mm(n1[layer, span(k)], wqkv[layer]) + vec[layer, 6:7, 0:384]
        packed = packed.astype(BF16)
        qkv[layer, span(k)] = packed
        queries, keys, values = packed[:, 0:128], packed[:, 128:256], packed[:, 256:384]
        visible = mask_ref[span(k)] > 0
        visible = jnp.concatenate([visible, visible], 0)
        scores = mm_nt(heads(queries * SCALE), keys)
        scores = jnp.where(visible, scores, -1e30)
        weights_ = jnp.exp(scores - jnp.max(scores, -1, keepdims=True))
        p = weights_ * (1.0 / jnp.sum(weights_, -1, keepdims=True))
        prob[layer, k] = p
        mixture = mm(beside(p.astype(BF16)), heads(values)).astype(BF16)
        mix[layer, span(k)] = mixture
        part[ph, span(k)] = mm(mixture, wout[layer]).astype(BF16)
        reduce_start(ph, k)

    def second_norm(layer, k):
        rows = hrow[layer, k] + reduce_finish(layer * 2, k) + vec[layer, 3:4]
        mrow[layer, k] = rows
        unit, _ = standardize(rows)
        n2[layer, mine(k)] = (unit * vec[layer, 1:2] + vec[layer, 4:5]).astype(BF16)
        gather_start(1, n2, layer, k)

    def feed(layer, k):
        ph = layer * 2 + 1
        gather_finish(1, n2, layer, k)
        u = mm(n2[layer, span(k)], w1[layer]) + vec[layer, 7:8, 0:512]
        up[layer, span(k)] = u
        g = 0.5 * u * (1.0 + jnp.tanh(GELU_C * (u + GELU_A * (u * u * u))))
        g = g.astype(BF16)
        act[layer, span(k)] = g
        part[ph, span(k)] = mm(g, w2[layer]).astype(BF16)
        reduce_start(ph, k)

    def finish(layer, k):
        rows = mrow[layer, k] + reduce_finish(layer * 2 + 1, k) + vec[layer, 5:6]

        @pl.when(layer == 0)
        def _():
            entering = rows.astype(BF16).astype(F32)
            hrow[1, k] = entering
            unit, _ = standardize(entering)
            n1[1, mine(k)] = (unit * vec[1, 0:1] + vec[1, 2:3]).astype(BF16)
            gather_start(0, n1, 1, k)

        ledger[0, k] = rows

    def feed_back(layer, k):
        ph = 6 - layer * 2

        @pl.when(layer == 0)
        def _():
            gather_finish(3, dyr, 0, k)

        grad = mm_nt(dyr[layer, span(k)], w2[layer])
        u = up[layer, span(k)]
        bend = jnp.tanh(GELU_C * (u + GELU_A * (u * u * u)))
        slope = 0.5 * (1.0 + bend) + (0.5 * u) * (1.0 - bend * bend) * (
            GELU_C * (1.0 + (3.0 * GELU_A) * (u * u))
        )
        du = (grad * slope).astype(BF16)
        dup[span(k)] = du
        part[ph, span(k)] = mm_nt(du, w1[layer]).astype(BF16)
        reduce_start(ph, k)

    def middle(layer, k):
        grad = dyr[layer, mine(k)].astype(F32)
        inner = reduce_finish(6 - layer * 2, k)
        slope, product = norm_back(mrow[layer, k], vec[layer, 1:2], inner)
        dm = grad + slope
        mrow[layer, k] = dm
        low = dm.astype(BF16)
        dmr[layer, mine(k)] = low
        gather_start(2, dmr, layer, k)
        ledger[0, k] = product
        ledger[1, k] = inner
        ledger[2, k] = low.astype(F32)
        ledger[3, k] = grad

    def attention_back(layer, k):
        ph = 7 - layer * 2
        gather_finish(2, dmr, layer, k)
        da = mm_nt(dmr[layer, span(k)], wout[layer]).astype(BF16)
        packed = qkv[layer, span(k)]
        queries, keys, values = packed[:, 0:128], packed[:, 128:256], packed[:, 256:384]
        p = prob[layer, k]
        outer = heads(da)
        dv = mm_tn(p.astype(BF16), outer)
        dp = mm_nt(outer, values)
        ds = (p * (dp - jnp.sum(p * dp, -1, keepdims=True))).astype(BF16)
        dq = mm(beside(ds), heads(keys)) * SCALE
        dk = mm_tn(ds, heads(queries)) * SCALE
        grads = jnp.concatenate([dq, dk, dv], 1).astype(BF16)
        dqkv[span(k)] = grads
        part[ph, span(k)] = mm_nt(grads, wqkv[layer]).astype(BF16)
        reduce_start(ph, k)

    def column_sum(layer, row, which):
        total = jnp.sum(ledger[which, 0], 0, keepdims=True)
        for k in range(1, chunks):
            total = total + jnp.sum(ledger[which, k], 0, keepdims=True)
        gpack[layer, row : row + 1] = total

    def last(layer, k):
        inner = reduce_finish(7 - layer * 2, k)
        slope, product = norm_back(hrow[layer, k], vec[layer, 0:1], inner)
        rows = mrow[layer, k] + slope

        @pl.when(layer == 1)
        def _():
            dyr[0, mine(k)] = rows.astype(BF16)
            gather_start(3, dyr, 0, k)

        ledger[0, k] = product
        ledger[1, k] = inner
        ledger[2, k] = rows

    pieces = 2 * nz
    wide = D // pieces

    def grad_down(layer, b):
        cols = pl.ds(pl.multiple_of(b * 128, 128), 128)
        block = mm_tn(act[layer, :, cols], dyr[layer]).astype(BF16)
        for q in range(pieces):
            gbufs[0][layer, q, cols] = block[:, q * wide : (q + 1) * wide]

    up_wide = max(256 // wide, 1)
    up_steps = pieces // up_wide

    def grad_up(layer, b):
        size = wide * up_wide
        cols = pl.ds(pl.multiple_of(b * size, size), size)
        block = mm_tn(n2[layer, :, cols], dup[...]).astype(BF16)
        for q in range(up_wide):
            gbufs[1][layer, b * up_wide + q] = block[q * wide : (q + 1) * wide]

    def grad_out(layer):
        block = mm_tn(mix[layer], dmr[layer]).astype(BF16)
        for q in range(pieces):
            gbufs[4][layer, q] = block[:, q * wide : (q + 1) * wide]

    def grad_qkv(layer, b):
        size = wide * up_wide
        cols = pl.ds(pl.multiple_of(b * size, size), size)
        block = mm_tn(n1[layer, :, cols], dqkv[...]).astype(BF16)
        for q in range(up_wide):
            rows = slice(q * wide, (q + 1) * wide)
            gbufs[2][layer, b * up_wide + q] = block[rows, 0:256]
            gbufs[3][layer, b * up_wide + q] = block[rows, 256:384]

    def small_start(layer):
        for j in range(T):
            sstage[layer, j] = gpack[layer, :, j * 128 : (j + 1) * 128]
            sbias[layer, j : j + 1] = gpack[layer, 6:7, j * 128 : (j + 1) * 128]

        def send(src, dst, to, self_):
            @pl.when(self_)
            def _():
                pltpu.make_async_copy(src, dst, ssem.at[0]).start()

            @pl.when(jnp.logical_not(self_))
            def _():
                remote(src, dst, ssend.at[layer], ssem.at[0], (layer, to, d))

        for j in range(T):
            to = lax.rem(t + j, T)
            src, dst = sstage.at[layer, to], sgot.at[c * T + t]
            if j:
                remote(src, dst, ssend.at[layer], ssem.at[0], (layer, to, d))
            else:
                send(src, dst, to, c == layer)
        send(
            sbias.at[layer],
            sgot.at[2 * T + xh],
            c * Y + y,
            jnp.logical_and(c == layer, native),
        )

    def small_middle():
        await_bytes(sgot, ssem.at[0])
        total = sgot[0]
        for j in range(1, 2 * T):
            total = total + sgot[j]
        ssum[0] = total
        ssum[1] = sgot[2 * T] + sgot[2 * T + 1]
        for j in range(1, 2 * nz):
            to = lax.rem(d + j, 2 * nz)
            remote(ssum, sall.at[j - 1], ssend.at[2], ssem.at[1], (c, t, to))

    def small_finish():
        await_bytes(sall, ssem.at[1])
        total = ssum[...]
        for j in range(2 * nz - 1):
            total = total + sall[j]
        return total

    def collect_attention(layer):
        z_first_middle(2, layer)

        @pl.when(c == layer)
        def _():
            x_first_middle(3)
            x_first_middle(4)
            small_middle()

    def on(condition, body, *args):
        @pl.when(condition)
        def _():
            body(*args)

    def stage_body(stage):
        odd = lax.rem(stage, 2)
        ahead = stage < 4
        layer = jnp.where(ahead, stage // 2, 3 - stage // 2)
        front_even = jnp.logical_and(ahead, odd == 0)
        front_odd = jnp.logical_and(ahead, odd == 1)
        back_even = jnp.logical_and(stage >= 4, odd == 0)
        back_odd = jnp.logical_and(stage >= 4, odd == 1)

        @pl.when(stage == 1)
        def _():
            need(2, 0)
            need(3, 0)

        @pl.when(stage == 2)
        def _():
            need(0, 1)
            need(1, 1)

        @pl.when(stage == 3)
        def _():
            need(2, 1)
            need(3, 1)

        def step(s):
            @pl.when(s < chunks)
            def _():
                on(front_odd, gather_middle, 1, n2, layer, s)
                on(stage == 2, gather_middle, 0, n1, 1, s)
                on(back_odd, gather_middle, 2, dmr, layer, s)
                on(stage == 6, gather_middle, 3, dyr, 0, s)

            @pl.when(jnp.logical_and(s >= 1, s < chunks + 1))
            def _():
                on(front_even, attention, layer, s - 1)
                on(front_odd, feed, layer, s - 1)
                on(back_even, feed_back, layer, s - 1)
                on(back_odd, attention_back, layer, s - 1)

            @pl.when(s >= 2)
            def _():
                reduce_middle(stage, s - 2)

            @pl.when(jnp.logical_and(stage == 0, s == 1))
            def _():
                relay(2, 0)
            @pl.when(jnp.logical_and(stage == 0, s == 3))
            def _():
                relay(3, 0)

        each(chunks + 2, step)
        @pl.when(stage == 1)
        def _():
            relay(0, 1)
        @pl.when(stage == 1)
        def _():
            relay(1, 1)

        @pl.when(stage == 0)
        def _():
            @pl.when(c == 1)
            def _():
                for i in range(4):
                    send_weight(i)

        @pl.when(stage == 4)
        def _():
            each(chunks, lambda k: finish(1, k))
            each(chunks, lambda k: emit(0, 1, k, ledger[0, k]))

        @pl.when(back_even)
        def _():
            each(4, lambda b: grad_down(layer, b))
            z_first_start(0, layer)

            @pl.when(layer == 0)
            def _():
                each(up_steps, lambda b: grad_up(layer, b))
                x_first_start(1, layer)

        @pl.when(back_odd)
        def _():
            grad_out(layer)
            x_first_start(4, layer)
            each(up_steps, lambda b: grad_qkv(layer, b))
            z_first_start(2, layer)
            x_first_start(3, layer)
            gpack[layer, 6:7, 0:384] = mm(ones, dqkv[...])[0:1]

        def settle(k):
            on(front_even, second_norm, layer, k)
            on(stage == 1, finish, 0, k)
            on(back_even, middle, layer, k)
            on(back_odd, last, layer, k)

        on(stage != 3, each, chunks, settle)
        @pl.when(stage == 1)
        def _():
            relay(2, 1)
        @pl.when(stage == 1)
        def _():
            relay(3, 1)


        @pl.when(back_even)
        def _():
            @pl.when(layer == 1)
            def _():
                each(up_steps, lambda b: grad_up(layer, b))
                x_first_start(1, layer)

            column_sum(layer, 1, 0)
            column_sum(layer, 4, 1)
            column_sum(layer, 3, 2)
            column_sum(layer, 5, 3)
            gpack[layer, 6:7, 384:896] = mm(ones, dup[...])[0:1]

        @pl.when(stage == 1)
        def _():
            each(chunks, lambda k: emit(0, 0, k, ledger[0, k]))

        @pl.when(back_odd)
        def _():
            column_sum(layer, 0, 0)
            column_sum(layer, 2, 1)
            small_start(layer)
            each(chunks, lambda k: emit(1, layer, k, ledger[2, k]))

        on(stage == 5, z_first_middle, 0, layer)
        on(jnp.logical_and(stage == 5, c == 1), x_first_middle, 1)
        on(stage == 6, collect_attention, 1)

    each(8, stage_body)
    z_first_middle(0, 0)
    on(c == 0, x_first_middle, 1)
    collect_attention(0)

    places_ = layout(nz)

    def put(name, value, start=0):
        rows = value.shape[0]
        first = places_[name] + start * rows
        for j in range(value.shape[1] // 128):
            grads_ref[first + j * rows : first + (j + 1) * rows] = value[:, j * 128 : (j + 1) * 128]

    put("down", z_first_finish(0))
    put("up", x_first_finish(1))
    small = small_finish()
    put("small", small[0])
    put("bias", small[1])
    put("qkv", x_first_finish(3), 2)
    put("out", x_first_finish(4))
    put("qkv", z_first_finish(2))
    for kind in range(2):
        await_bytes(obuf.at[kind], osem.at[kind])
    rows_ref[...] = obuf[...]

    for i in range(4):
        both = weights[i][1]

        @pl.when(jnp.logical_not(native))
        def _():
            await_bytes(both.at[0], whome.at[i])
            for layer in range(2):
                await_bytes(whole_half(i), wrelay.at[i, layer])

        if i:
            weight_left(i)

    @pl.when(c == 1)
    def _():
        weight_left(0)

    @pl.when(jnp.logical_not(native))
    def _():
        await_bytes(vec.at[0], vsend.at[0])

    await_bytes(vec.at[0], vsend.at[0])
    for ph in range(8):
        await_bytes(cbuf.at[ph], csend.at[ph])
        await_bytes(rs.at[ph], rsend.at[ph])
    for which, layer in ((0, 1), (1, 0), (1, 1), (2, 0), (2, 1), (3, 0)):
        await_bytes(rs.at[0], gsend.at[which, layer])
        await_bytes(cbuf.at[0], hsend.at[which, layer])
    for layer in range(2):
        for kind in range(2):

            @pl.when(c == layer)
            def _():
                view = ostage.at[kind, layer, :, pl.ds(0, T - 1)]
                await_bytes(view, osend.at[kind, layer])

            @pl.when(c != layer)
            def _():
                await_bytes(ostage.at[kind, layer], osend.at[kind, layer])

        self_ = jnp.logical_and(c == layer, native)
        for m in range(5):
            if nz > 1 and m in (0, 2):
                await_bytes(zrs[m].at[layer], zsend.at[m, layer])
            await_bytes(xrs[m].at[0], xsend.at[m, layer])

            @pl.when(jnp.logical_not(self_))
            def _():
                await_bytes(xrs[m].at[0], xsend.at[m, layer])

        await_bytes(sgot.at[pl.ds(0, T - 1)], ssend.at[layer])

        @pl.when(c != layer)
        def _():
            await_bytes(sgot.at[0], ssend.at[layer])

        @pl.when(jnp.logical_not(self_))
        def _():
            await_bytes(sgot.at[0], ssend.at[layer])

    if nz > 1:
        for m in (1, 3, 4):
            await_bytes(zrs[m], zsend.at[m, 0])
    await_bytes(sall, ssend.at[2])


def layout(nz):
    wide = D // (2 * nz)
    sizes = (
        ("qkv", 3 * wide),
        ("up", 4 * wide),
        ("down", 4 * wide),
        ("out", wide),
        ("small", 8),
        ("bias", 8),
    )
    places, first = {}, 0
    for name, size in sizes:
        places[name] = first
        first += size
    places["end"] = first
    return places


def core(chunks, nz, x, ct, docs, wqkv, wout, w1, w2, qb, b1, gains, shifts):
    n = chunks * ROWS
    vm = pl.BlockSpec(memory_space=pltpu.VMEM)
    hbm = pl.BlockSpec(memory_space=pl.ANY)
    pieces = 2 * nz
    wide = D // pieces
    out_shape = (
        jax.ShapeDtypeStruct((2, 2 * n, 128), BF16),
        jax.ShapeDtypeStruct((layout(nz)["end"], 128), F32),
    )
    dma = pltpu.SemaphoreType.DMA
    shape = ((512, wide), (wide, 512), (wide, 256), (wide, 128), (128, wide))
    back = max(nz - 1, 1)
    gbufs = [pltpu.VMEM((2, pieces) + s, BF16) for s in shape]
    zrs, zsums, xrs = [], [], []
    for m, s in enumerate(shape):
        if m in (0, 2):
            zrs.append(pltpu.VMEM((2, back, 2) + s, BF16))
            zsums.append(pltpu.VMEM((2, 2) + s, BF16))
            xrs.append(pltpu.VMEM((4,) + s, BF16))
        else:
            zrs.append(pltpu.VMEM((back,) + s, BF16))
            zsums.append(pltpu.VMEM((nz,) + s, BF16))
            xrs.append(pltpu.VMEM((4, nz) + s, BF16))
    scratch = [
        pltpu.VMEM((n, D), BF16),
        pltpu.VMEM((n, ROWS), F32),
        pltpu.VMEM((8, D), F32),
        pltpu.VMEM((2, D, 384), BF16),
        pltpu.VMEM((2, 128, D), BF16),
        pltpu.VMEM((2, D, 512), BF16),
        pltpu.VMEM((2, 512, D), BF16),
        pltpu.VMEM((2, 8, D), F32),
        pltpu.VMEM((2, n, D), BF16),
        pltpu.VMEM((2, n, D), BF16),
        pltpu.VMEM((2, n, D), BF16),
        pltpu.VMEM((2, n, D), BF16),
        pltpu.VMEM((2, n, 384), BF16),
        pltpu.VMEM((2, n, 128), BF16),
        pltpu.VMEM((2, chunks, 2 * ROWS, ROWS), F32),
        pltpu.VMEM((2, n, 512), F32),
        pltpu.VMEM((2, n, 512), BF16),
        pltpu.VMEM((n, 512), BF16),
        pltpu.VMEM((n, 384), BF16),
        pltpu.VMEM((2, chunks, OWN, D), F32),
        pltpu.VMEM((2, chunks, OWN, D), F32),
        pltpu.VMEM((4, chunks, OWN, D), F32),
        pltpu.VMEM((8, n, D), BF16),
        pltpu.VMEM((8, chunks, ROWS // 2, D), BF16),
        pltpu.VMEM((8, chunks, ROWS // 2, D), BF16),
        pltpu.VMEM((8, chunks, Y - 1, OWN, D), BF16),
        pltpu.VMEM((2, 2, chunks, T, OWN, 128), BF16),
        pltpu.VMEM((2, 2 * n, 128), BF16),
        gbufs,
        zrs,
        zsums,
        xrs,
        pltpu.VMEM((2, 8, D), F32),
        pltpu.VMEM((2, T, 8, 128), F32),
        pltpu.VMEM((2, 8, 128), F32),
        pltpu.VMEM((2 * T + 2, 8, 128), F32),
        pltpu.VMEM((2, 8, 128), F32),
        pltpu.VMEM((pieces - 1, 2, 8, 128), F32),
        dma((2,)),
        dma((4, 2, 2, PARTS)),
        dma((4,)),
        dma((4,)),
        dma((4, 2)),
        dma((2,)),
        dma((1,)),
        dma((8, chunks)),
        dma((8,)),
        dma((8, chunks)),
        dma((8,)),
        dma((4, 2, chunks)),
        dma((4, 2)),
        dma((4, 2, chunks)),
        dma((4, 2)),
        dma((2,)),
        dma((2, 2)),
        dma((5, 2)),
        dma((5, 2)),
        dma((5,)),
        dma((5, 2)),
        dma((2,)),
        dma((3,)),
    ]
    return pl.pallas_call(
        functools.partial(kernel, chunks, nz),
        out_shape=out_shape,
        in_specs=[hbm, hbm, vm, hbm, hbm, hbm, hbm, vm, vm, vm, vm],
        out_specs=[vm] * 2,
        scratch_shapes=scratch,
        compiler_params=pltpu.CompilerParams(
            collective_id=0, has_side_effects=True, vmem_limit_bytes=62 * 2**20
        ),
        name="layers",
    )(x, ct, docs, wqkv, wout, w1, w2, qb, b1, gains, shifts)


def closing(
    m,
    rows_in,
    grads_in,
    sec_out,
    ing_out,
    gqkv_out,
    qb_out,
    gout_out,
    g1_out,
    b1_out,
    g2_out,
    gains_out,
    shifts_out,
    rows,
    grads,
    sems,
):
    d = lax.axis_index("dp")
    rows_copy = pltpu.make_async_copy(rows_in, rows, sems.at[0])
    grads_copy = pltpu.make_async_copy(grads_in, grads, sems.at[1])
    rows_copy.start()
    grads_copy.start()
    rows_copy.wait()
    sec_out[0] = rows[0].astype(F32)
    ing_out[0] = rows[1].astype(F32)
    grads_copy.wait()
    places = layout(m // 2)
    width = D // m

    def get(name, height, j):
        first = places[name] + j * height
        return grads[first : first + height]

    for j in range(3):
        gqkv_out[0, j] = get("qkv", width, j)
    for j in range(4):
        g1_out[0, :, j * 128 : (j + 1) * 128] = get("up", width, j)
    for j in range(width // 128):
        gout_out[0, :, j * 128 : (j + 1) * 128] = get("out", 128, j)
        g2_out[0, :, j * 128 : (j + 1) * 128] = get("down", 512, j)
    share = 128 // m
    shift = lax.rem(128 - d * share, 128)
    rolled = pltpu.roll(get("small", 8, 0), shift, 1)
    gains_out[0] = rolled[0:2, 0:share]
    shifts_out[0] = rolled[2:6, 0:share]
    bias = get("bias", 8, 0)
    rolled = pltpu.roll(bias, shift, 1)
    for j in range(2):
        qb_out[0, j : j + 1] = rolled[2 * j : 2 * j + 1, 0:share]
    lines = lax.broadcasted_iota(jnp.int32, (8, 128), 0)

    def line(block, which):
        return jnp.sum(jnp.where(lines == which, block, 0.0), 0, keepdims=True)

    wide = 512 // m
    if wide >= 128:
        for j in range(wide // 128):
            b1_out[:, j * 128 : (j + 1) * 128] = line(bias, 3 + d * (wide // 128) + j)
    else:
        per = 128 // wide
        rolled = pltpu.roll(bias, lax.rem(128 - lax.rem(d, per) * wide, 128), 1)
        b1_out[...] = line(rolled, 3 + d // per)[:, 0:wide]


def shards(
    inputs,
    cotangent,
    doc_ids,
    qkv_weight,
    qkv_bias,
    out_weight,
    fc1_weight,
    fc1_bias,
    fc2_weight,
    norm_gains,
    shifts,
):
    m = lax.axis_size("dp")
    chunks = doc_ids.shape[0] // 2
    n = chunks * ROWS
    results = core(
        chunks,
        m // 2,
        inputs,
        cotangent,
        doc_ids,
        qkv_weight[0].transpose(1, 0, 2),
        out_weight[0],
        fc1_weight[0],
        fc2_weight[0],
        qkv_bias,
        fc1_bias,
        norm_gains,
        shifts,
    )
    vm = pl.BlockSpec(memory_space=pltpu.VMEM)
    shapes = (
        (1, 2 * n, 128),
        (1, 2 * n, 128),
        (1, 3, D // m, 128),
        (1, 2, 128 // m),
        (1, 128, D // m),
        (1, D // m, 512),
        (1, 512 // m),
        (1, 512, D // m),
        (1, 2, 128 // m),
        (1, 4, 128 // m),
    )
    outs = pl.pallas_call(
        functools.partial(closing, m),
        out_shape=[jax.ShapeDtypeStruct(shape, F32) for shape in shapes],
        in_specs=[pl.BlockSpec(memory_space=pl.ANY)] * 2,
        out_specs=[vm] * 10,
        scratch_shapes=[
            pltpu.VMEM(results[0].shape, BF16),
            pltpu.VMEM(results[1].shape, F32),
            pltpu.SemaphoreType.DMA((2,)),
        ],
        compiler_params=pltpu.CompilerParams(vmem_limit_bytes=62 * 2**20),
        name="closing",
    )(*results)
    return (*outs[:2], outs[2].transpose(0, 2, 1, 3), *outs[3:])


def solution(mesh):
    return jax.shard_map(
        shards,
        mesh=mesh,
        in_specs=(
            P("dp", None),
            P("dp", None),
            P("dp", None),
            P("pipe", None, None, "tensor"),
            P("pipe", None, "tensor"),
            P("pipe", "tensor", None),
            P("pipe", None, "tensor"),
            P("pipe", "tensor"),
            P("pipe", "tensor", None),
            P("pipe", None, None),
            P("pipe", None, None),
        ),
        out_specs=(
            P("pipe", "dp", "tensor"),
            P("pipe", "dp", "tensor"),
            P("pipe", "dp", None, "tensor"),
            P("pipe", None, ("tensor", "dp")),
            P("pipe", "tensor", "dp"),
            P("pipe", "dp", "tensor"),
            P("pipe", ("tensor", "dp")),
            P("pipe", "tensor", "dp"),
            P("pipe", None, ("tensor", "dp")),
            P("pipe", None, ("tensor", "dp")),
        ),
        check_vma=False,
    )
```

```python
import functools

import jax
import jax.numpy as jnp
from jax import lax
from jax.experimental import pallas as pl
from jax.experimental.pallas import tpu as pltpu
from jax.sharding import PartitionSpec as P

MESH = pl.DeviceIdType.MESH
F32 = jnp.float32
BF16 = jnp.bfloat16
EPSILON = 1e-05
HD = 64
SCALE = HD**-0.5
D = 1024
ROWS = 128
T = 8
Y = 4
PARTS = 2
OWN = ROWS // T
GELU_C = 0.7978845608028654
GELU_A = 0.044715


def mm(a, b):
    return lax.dot_general(a, b, (((1,), (0,)), ((), ())), preferred_element_type=F32)


def mm_nt(a, b):
    return lax.dot_general(a, b, (((1,), (1,)), ((), ())), preferred_element_type=F32)


def mm_tn(a, b):
    return lax.dot_general(a, b, (((0,), (0,)), ((), ())), preferred_element_type=F32)


def standardize(rows):
    centered = rows - jnp.mean(rows, -1, keepdims=True)
    variance = jnp.mean(centered * centered, -1, keepdims=True)
    root = lax.rsqrt(variance + EPSILON)
    return centered * root, root


def norm_back(rows, gain, grad):
    unit, root = standardize(rows)
    e = grad * gain
    slope = root * (
        e - jnp.mean(e, -1, keepdims=True) - unit * jnp.mean(e * unit, -1, keepdims=True)
    )
    return slope, grad * unit


def kernel(
    chunks,
    nz,
    x_in,
    ct_in,
    docs_ref,
    wqkv_in,
    wout_in,
    w1_in,
    w2_in,
    qb_in,
    b1_in,
    gains_in,
    shifts_in,
    rows_ref,
    grads_ref,
    x_ref,
    mask_ref,
    vec_in,
    wqkv,
    wout,
    w1,
    w2,
    vec,
    n1,
    n2,
    dmr,
    dyr,
    qkv,
    mix,
    prob,
    up,
    act,
    dup,
    dqkv,
    hrow,
    mrow,
    ledger,
    part,
    cbuf,
    psum,
    rs,
    ostage,
    obuf,
    gbufs,
    zrs,
    zsums,
    xrs,
    gpack,
    sstage,
    sbias,
    sgot,
    ssum,
    sall,
    insem,
    wsem,
    wsend,
    whome,
    wrelay,
    vsem,
    vsend,
    csem,
    csend,
    rsem,
    rsend,
    gsem,
    gsend,
    hsem,
    hsend,
    osem,
    osend,
    zsem,
    zsend,
    xsem,
    xsend,
    ssem,
    ssend,
):
    c = lax.axis_index("pipe")
    t = lax.axis_index("tensor")
    d = lax.axis_index("dp")
    xh = t // Y
    y = lax.rem(t, Y)
    xl = d // nz
    z = lax.rem(d, nz)
    sib = (1 - c, t, d)

    first_row = pl.ds(pl.multiple_of(xh * (chunks * ROWS), ROWS), chunks * ROWS)
    x_copy = pltpu.make_async_copy(x_in.at[first_row], x_ref, insem.at[0])
    ct_copy = pltpu.make_async_copy(ct_in.at[first_row], dyr.at[1], insem.at[1])
    x_copy.start()
    ct_copy.start()

    barrier = pltpu.get_barrier_semaphore()

    def greet(device):
        pl.semaphore_signal(barrier, inc=1, device_id=device, device_id_type=MESH)

    for j in range(T):
        other = lax.rem(t + j, T)
        if j:
            greet((c, other, d))
        greet((1 - c, other, d))
    far = (1 - xl) * nz + z
    for core_ in range(2):
        for j in range(2):
            greet((core_, j * Y + y, far))
    for j in range(1, nz):
        greet((c, t, xl * nz + lax.rem(z + j, nz)))
        greet((c, t, (1 - xl) * nz + lax.rem(z + j, nz)))
    vec_in[...] = jnp.zeros_like(vec_in)
    vec_in[0:2] = gains_in[0].astype(F32)
    vec_in[2:6] = shifts_in[0].astype(F32)
    vec_in[6:7, 0:128] = qb_in[0, 0:1].astype(F32)
    vec_in[6:7, 256:384] = qb_in[0, 1:2].astype(F32)
    vec_in[7:8, 0:512] = b1_in[...].astype(F32)
    pl.semaphore_wait(barrier, 2 * T - 1 + 4 + 2 * (nz - 1))

    def remote(src, dst, send, recv, device):
        pltpu.make_async_remote_copy(
            src_ref=src,
            dst_ref=dst,
            send_sem=send,
            recv_sem=recv,
            device_id=device,
            device_id_type=MESH,
        ).start()

    def await_bytes(view, sem):
        pltpu.make_async_copy(view, view, sem).wait()

    weights = ((wqkv_in, wqkv), (wout_in, wout), (w1_in, w1), (w2_in, w2))
    native = c == xh
    partner = (xh, (1 - xh) * Y + y, far)
    home = (xh, t, d)

    def half(i, which, q):
        size = weights[i][1].shape[1] // (2 * PARTS)
        return pl.ds(pl.multiple_of((which * PARTS + q) * size, size), size)

    def views(i, h, q):
        own, both = weights[i]
        piece = half(i, h, q)
        if i:
            return [(own.at[piece], both.at[c, piece])]
        return [
            (own.at[j, piece], both.at[c, piece, pl.ds(j * 128, 128)]) for j in range(3)
        ]

    def send_weight(i):
        for q in range(PARTS):
            for src, dst in views(i, xl, q):
                remote(src, dst, wsend.at[i], wsem.at[i, c, xl, q], partner)
        for h in range(2):
            for q in range(PARTS):
                for src, dst in views(i, h, q):

                    @pl.when(native)
                    def _():
                        pltpu.make_async_copy(src, dst, wsem.at[i, c, h, q]).start()

                    @pl.when(jnp.logical_not(native))
                    def _():
                        remote(src, dst, whome.at[i], wsem.at[i, c, h, q], home)

    def whole_half(i):
        return weights[i][1].at[0, pl.ds(0, weights[i][1].shape[1] // 2)]

    def weight_left(i):
        await_bytes(whole_half(i), wsend.at[i])

    def await_half(i, layer, h, q):
        await_bytes(weights[i][1].at[layer, half(i, h, q)], wsem.at[i, layer, h, q])

    def relay(i, layer, parts=tuple(range(PARTS))):
        both = weights[i][1]

        @pl.when(jnp.logical_not(native))
        def _():
            for q in parts:
                await_half(i, layer, 1 - xl, q)
                piece = both.at[layer, half(i, 1 - xl, q)]
                remote(
                    piece, piece, wrelay.at[i, layer], wsem.at[i, layer, 1 - xl, q], (c, t, far)
                )

    def need(i, layer):
        for q in range(PARTS):

            @pl.when(native)
            def _():
                await_half(i, layer, 1 - xl, q)

            await_half(i, layer, xl, q)

    def span(k):
        return pl.ds(pl.multiple_of(k * ROWS, ROWS), ROWS)

    def side(k, who):
        return pl.ds(pl.multiple_of(k * ROWS + who * (ROWS // 2), ROWS // 2), ROWS // 2)

    own_start = (c * Y + y) * OWN

    def mine(k):
        return pl.ds(pl.multiple_of(k * ROWS + own_start, OWN), OWN)

    def y_peer(j):
        return (c, xh * Y + lax.rem(y + j, Y), d)

    def reduce_start(ph, k):
        remote(
            part.at[ph, side(k, 1 - c)], cbuf.at[ph, k], csend.at[ph], csem.at[ph, k], sib
        )

    def reduce_middle(ph, k):
        await_bytes(cbuf.at[ph, k], csem.at[ph, k])
        psum[ph, k] = (part[ph, side(k, c)].astype(F32) + cbuf[ph, k].astype(F32)).astype(BF16)
        for j in (2, 1, 3):
            rows = pl.ds(pl.multiple_of(lax.rem(y + j, Y) * OWN, OWN), OWN)
            remote(
                psum.at[ph, k, rows], rs.at[ph, k, j - 1], rsend.at[ph], rsem.at[ph, k], y_peer(j)
            )

    def reduce_finish(ph, k):
        await_bytes(rs.at[ph, k], rsem.at[ph, k])
        rows = pl.ds(pl.multiple_of(y * OWN, OWN), OWN)
        total = psum[ph, k, rows].astype(F32)
        for j in range(Y - 1):
            total = total + rs[ph, k, j].astype(F32)
        return total

    def gather_start(which, buf, layer, k):
        for j in (2, 1, 3):
            view = buf.at[layer, mine(k)]
            remote(view, view, gsend.at[which, layer], gsem.at[which, layer, k], y_peer(j))

    def gather_middle(which, buf, layer, k):
        await_bytes(buf.at[layer, pl.ds(0, (Y - 1) * OWN)], gsem.at[which, layer, k])
        view = buf.at[layer, side(k, c)]
        remote(view, view, hsend.at[which, layer], hsem.at[which, layer, k], sib)

    def gather_finish(which, buf, layer, k):
        await_bytes(buf.at[layer, side(k, 1 - c)], hsem.at[which, layer, k])

    def emit(kind, layer, k, rows):
        low = rows.astype(BF16)
        for j in range(T):
            ostage[kind, layer, k, j] = low[:, j * 128 : (j + 1) * 128]
        first = xh * (chunks * ROWS) + k * ROWS + own_start
        target = pl.ds(pl.multiple_of(first, OWN), OWN)

        def away(j):
            other = lax.rem(t + j, T)
            remote(
                ostage.at[kind, layer, k, other],
                obuf.at[kind, target],
                osend.at[kind, layer],
                osem.at[kind],
                (layer, other, d),
            )

        for j in range(1, T):
            away(j)

        @pl.when(c == layer)
        def _():
            pltpu.make_async_copy(
                ostage.at[kind, layer, k, t], obuf.at[kind, target], osem.at[kind]
            ).start()

        @pl.when(c != layer)
        def _():
            away(0)

    slot = xh * 2 + xl

    def x_send(m, layer, source):
        for to in range(2):
            self_ = jnp.logical_and(jnp.logical_and(c == layer, native), xl == to)
            src, dst = source(to), xrs[m].at[slot]

            @pl.when(self_)
            def _():
                pltpu.make_async_copy(src, dst, xsem.at[m]).start()

            @pl.when(jnp.logical_not(self_))
            def _():
                remote(
                    src, dst, xsend.at[m, layer], xsem.at[m], (layer, c * Y + y, to * nz + z)
                )

    def z_peer(j):
        return (c, t, xl * nz + lax.rem(z + j, nz))

    def z_first_start(m, layer):
        for j in range(1, nz):
            for to in range(2):
                remote(
                    gbufs[m].at[layer, to * nz + lax.rem(z + j, nz)],
                    zrs[m].at[layer, j - 1, to],
                    zsend.at[m, layer],
                    zsem.at[m, layer],
                    z_peer(j),
                )

    def z_first_middle(m, layer):
        if nz > 1:
            await_bytes(zrs[m].at[layer], zsem.at[m, layer])
        for to in range(2):
            total = gbufs[m][layer, to * nz + z].astype(F32)
            for j in range(nz - 1):
                total = total + zrs[m][layer, j, to].astype(F32)
            zsums[m][layer, to] = total.astype(BF16)
        x_send(m, layer, lambda to: zsums[m].at[layer, to])

    def z_first_finish(m):
        await_bytes(xrs[m], xsem.at[m])
        return sum4(m)

    def sum4(m):
        total = xrs[m][0].astype(F32)
        for j in range(1, 4):
            total = total + xrs[m][j].astype(F32)
        return total

    def x_first_start(m, layer):
        x_send(m, layer, lambda to: gbufs[m].at[layer, pl.ds(to * nz, nz)])

    def x_first_middle(m):
        await_bytes(xrs[m], xsem.at[m])
        zsums[m][...] = sum4(m).astype(BF16)
        for j in range(1, nz):
            remote(
                zsums[m].at[lax.rem(z + j, nz)],
                zrs[m].at[j - 1],
                zsend.at[m, 0],
                zsem.at[m, 0],
                z_peer(j),
            )

    def x_first_finish(m):
        total = zsums[m][z].astype(F32)
        if nz > 1:
            await_bytes(zrs[m], zsem.at[m, 0])
        for j in range(nz - 1):
            total = total + zrs[m][j].astype(F32)
        return total

    ones = jnp.ones((8, chunks * ROWS), BF16)
    left_half = lax.broadcasted_iota(jnp.int32, (ROWS, 128), 1) < HD

    def heads(value):
        zero = jnp.zeros_like(value)
        return jnp.concatenate(
            [jnp.where(left_half, value, zero), jnp.where(left_half, zero, value)], 0
        )

    def beside(value):
        return jnp.concatenate([value[0:ROWS], value[ROWS:]], 1)

    def each(count, body):
        def step(i, carry):
            body(i)
            return carry

        lax.fori_loop(0, count, step, 0)

    @pl.when(native)
    def _():
        pltpu.make_async_copy(vec_in, vec.at[c], vsem.at[c]).start()

    @pl.when(jnp.logical_not(native))
    def _():
        remote(vec_in, vec.at[c], vsend.at[0], vsem.at[c], home)

    remote(vec_in, vec.at[c], vsend.at[0], vsem.at[c], partner)

    @pl.when(c == 0)
    def _():
        send_weight(0)
        send_weight(1)
        send_weight(2)
        send_weight(3)

    gpack[...] = jnp.zeros_like(gpack)
    lanes = lax.broadcasted_iota(jnp.int32, (ROWS, ROWS), 1)
    places = lax.broadcasted_iota(jnp.int32, (ROWS, ROWS), 0)

    def visibility(k):
        segment = docs_ref[pl.ds(xh * chunks + k, 1)].astype(F32)
        segment = jnp.broadcast_to(segment, (ROWS, ROWS))
        visible = jnp.logical_and(lanes <= places, segment == segment.T)
        mask_ref[span(k)] = jnp.where(visible, 1.0, 0.0)

    each(chunks, visibility)
    x_copy.wait()
    ct_copy.wait()

    def start(k):
        unit, _ = standardize(x_ref[span(k)].astype(F32))
        n1[0, span(k)] = (unit * vec[0, 0:1] + vec[0, 2:3]).astype(BF16)
        hrow[0, k] = x_ref[mine(k)].astype(F32)

    await_bytes(vec.at[0], vsem.at[0])
    await_bytes(vec.at[1], vsem.at[1])
    relay(0, 0, (0,))
    each(chunks, start)
    relay(0, 0, (1,))
    relay(1, 0)

    @pl.when(c == 0)
    def _():
        weight_left(0)

    need(0, 0)
    need(1, 0)

    def attention(layer, k):
        ph = layer * 2

        @pl.when(layer == 1)
        def _():
            gather_finish(0, n1, 1, k)

        packed = mm(n1[layer, span(k)], wqkv[layer]) + vec[layer, 6:7, 0:384]
        packed = packed.astype(BF16)
        qkv[layer, span(k)] = packed
        queries, keys, values = packed[:, 0:128], packed[:, 128:256], packed[:, 256:384]
        visible = mask_ref[span(k)] > 0
        visible = jnp.concatenate([visible, visible], 0)
        scores = mm_nt(heads(queries * SCALE), keys)
        scores = jnp.where(visible, scores, -1e30)
        weights_ = jnp.exp(scores - jnp.max(scores, -1, keepdims=True))
        p = weights_ * (1.0 / jnp.sum(weights_, -1, keepdims=True))
        prob[layer, k] = p
        mixture = mm(beside(p.astype(BF16)), heads(values)).astype(BF16)
        mix[layer, span(k)] = mixture
        part[ph, span(k)] = mm(mixture, wout[layer]).astype(BF16)
        reduce_start(ph, k)

    def second_norm(layer, k):
        rows = hrow[layer, k] + reduce_finish(layer * 2, k) + vec[layer, 3:4]
        mrow[layer, k] = rows
        unit, _ = standardize(rows)
        n2[layer, mine(k)] = (unit * vec[layer, 1:2] + vec[layer, 4:5]).astype(BF16)
        gather_start(1, n2, layer, k)

    def feed(layer, k):
        ph = layer * 2 + 1
        gather_finish(1, n2, layer, k)
        u = mm(n2[layer, span(k)], w1[layer]) + vec[layer, 7:8, 0:512]
        up[layer, span(k)] = u
        g = 0.5 * u * (1.0 + jnp.tanh(GELU_C * (u + GELU_A * (u * u * u))))
        g = g.astype(BF16)
        act[layer, span(k)] = g
        part[ph, span(k)] = mm(g, w2[layer]).astype(BF16)
        reduce_start(ph, k)

    def finish(layer, k):
        rows = mrow[layer, k] + reduce_finish(layer * 2 + 1, k) + vec[layer, 5:6]

        @pl.when(layer == 0)
        def _():
            entering = rows.astype(BF16).astype(F32)
            hrow[1, k] = entering
            unit, _ = standardize(entering)
            n1[1, mine(k)] = (unit * vec[1, 0:1] + vec[1, 2:3]).astype(BF16)
            gather_start(0, n1, 1, k)

        ledger[0, k] = rows

    def feed_back(layer, k):
        ph = 6 - layer * 2

        @pl.when(layer == 0)
        def _():
            gather_finish(3, dyr, 0, k)

        grad = mm_nt(dyr[layer, span(k)], w2[layer])
        u = up[layer, span(k)]
        bend = jnp.tanh(GELU_C * (u + GELU_A * (u * u * u)))
        slope = 0.5 * (1.0 + bend) + (0.5 * u) * (1.0 - bend * bend) * (
            GELU_C * (1.0 + (3.0 * GELU_A) * (u * u))
        )
        du = (grad * slope).astype(BF16)
        dup[span(k)] = du
        part[ph, span(k)] = mm_nt(du, w1[layer]).astype(BF16)
        reduce_start(ph, k)

    def middle(layer, k):
        grad = dyr[layer, mine(k)].astype(F32)
        inner = reduce_finish(6 - layer * 2, k)
        slope, product = norm_back(mrow[layer, k], vec[layer, 1:2], inner)
        dm = grad + slope
        mrow[layer, k] = dm
        low = dm.astype(BF16)
        dmr[layer, mine(k)] = low
        gather_start(2, dmr, layer, k)
        ledger[0, k] = product
        ledger[1, k] = inner
        ledger[2, k] = low.astype(F32)
        ledger[3, k] = grad

    def attention_back(layer, k):
        ph = 7 - layer * 2
        gather_finish(2, dmr, layer, k)
        da = mm_nt(dmr[layer, span(k)], wout[layer]).astype(BF16)
        packed = qkv[layer, span(k)]
        queries, keys, values = packed[:, 0:128], packed[:, 128:256], packed[:, 256:384]
        p = prob[layer, k]
        outer = heads(da)
        dv = mm_tn(p.astype(BF16), outer)
        dp = mm_nt(outer, values)
        ds = (p * (dp - jnp.sum(p * dp, -1, keepdims=True))).astype(BF16)
        dq = mm(beside(ds), heads(keys)) * SCALE
        dk = mm_tn(ds, heads(queries)) * SCALE
        grads = jnp.concatenate([dq, dk, dv], 1).astype(BF16)
        dqkv[span(k)] = grads
        part[ph, span(k)] = mm_nt(grads, wqkv[layer]).astype(BF16)
        reduce_start(ph, k)

    def column_sum(layer, row, which):
        total = jnp.sum(ledger[which, 0], 0, keepdims=True)
        for k in range(1, chunks):
            total = total + jnp.sum(ledger[which, k], 0, keepdims=True)
        gpack[layer, row : row + 1] = total

    def last(layer, k):
        inner = reduce_finish(7 - layer * 2, k)
        slope, product = norm_back(hrow[layer, k], vec[layer, 0:1], inner)
        rows = mrow[layer, k] + slope

        @pl.when(layer == 1)
        def _():
            dyr[0, mine(k)] = rows.astype(BF16)
            gather_start(3, dyr, 0, k)

        ledger[0, k] = product
        ledger[1, k] = inner
        ledger[2, k] = rows

    pieces = 2 * nz
    wide = D // pieces

    def grad_down(layer, b):
        cols = pl.ds(pl.multiple_of(b * 128, 128), 128)
        block = mm_tn(act[layer, :, cols], dyr[layer]).astype(BF16)
        for q in range(pieces):
            gbufs[0][layer, q, cols] = block[:, q * wide : (q + 1) * wide]

    up_wide = max(256 // wide, 1)
    up_steps = pieces // up_wide

    def grad_up(layer, b):
        size = wide * up_wide
        cols = pl.ds(pl.multiple_of(b * size, size), size)
        block = mm_tn(n2[layer, :, cols], dup[...]).astype(BF16)
        for q in range(up_wide):
            gbufs[1][layer, b * up_wide + q] = block[q * wide : (q + 1) * wide]

    def grad_out(layer):
        block = mm_tn(mix[layer], dmr[layer]).astype(BF16)
        for q in range(pieces):
            gbufs[4][layer, q] = block[:, q * wide : (q + 1) * wide]

    def grad_qkv(layer, b):
        size = wide * up_wide
        cols = pl.ds(pl.multiple_of(b * size, size), size)
        block = mm_tn(n1[layer, :, cols], dqkv[...]).astype(BF16)
        for q in range(up_wide):
            rows = slice(q * wide, (q + 1) * wide)
            gbufs[2][layer, b * up_wide + q] = block[rows, 0:256]
            gbufs[3][layer, b * up_wide + q] = block[rows, 256:384]

    def small_start(layer):
        for j in range(T):
            sstage[layer, j] = gpack[layer, :, j * 128 : (j + 1) * 128]
            sbias[layer, j : j + 1] = gpack[layer, 6:7, j * 128 : (j + 1) * 128]

        def send(src, dst, to, self_):
            @pl.when(self_)
            def _():
                pltpu.make_async_copy(src, dst, ssem.at[0]).start()

            @pl.when(jnp.logical_not(self_))
            def _():
                remote(src, dst, ssend.at[layer], ssem.at[0], (layer, to, d))

        for j in range(T):
            to = lax.rem(t + j, T)
            src, dst = sstage.at[layer, to], sgot.at[c * T + t]
            if j:
                remote(src, dst, ssend.at[layer], ssem.at[0], (layer, to, d))
            else:
                send(src, dst, to, c == layer)
        send(
            sbias.at[layer],
            sgot.at[2 * T + xh],
            c * Y + y,
            jnp.logical_and(c == layer, native),
        )

    def small_middle():
        await_bytes(sgot, ssem.at[0])
        total = sgot[0]
        for j in range(1, 2 * T):
            total = total + sgot[j]
        ssum[0] = total
        ssum[1] = sgot[2 * T] + sgot[2 * T + 1]
        for j in range(1, 2 * nz):
            to = lax.rem(d + j, 2 * nz)
            remote(ssum, sall.at[j - 1], ssend.at[2], ssem.at[1], (c, t, to))

    def small_finish():
        await_bytes(sall, ssem.at[1])
        total = ssum[...]
        for j in range(2 * nz - 1):
            total = total + sall[j]
        return total

    def collect_attention(layer):
        z_first_middle(2, layer)

        @pl.when(c == layer)
        def _():
            x_first_middle(3)
            x_first_middle(4)
            small_middle()

    def on(condition, body, *args):
        @pl.when(condition)
        def _():
            body(*args)

    def stage_body(stage):
        odd = lax.rem(stage, 2)
        ahead = stage < 4
        layer = jnp.where(ahead, stage // 2, 3 - stage // 2)
        front_even = jnp.logical_and(ahead, odd == 0)
        front_odd = jnp.logical_and(ahead, odd == 1)
        back_even = jnp.logical_and(stage >= 4, odd == 0)
        back_odd = jnp.logical_and(stage >= 4, odd == 1)

        @pl.when(stage == 1)
        def _():
            need(2, 0)
            need(3, 0)

        @pl.when(stage == 2)
        def _():
            need(0, 1)
            need(1, 1)

        @pl.when(stage == 3)
        def _():
            need(2, 1)
            need(3, 1)

        def step(s):
            @pl.when(s < chunks)
            def _():
                on(front_odd, gather_middle, 1, n2, layer, s)
                on(stage == 2, gather_middle, 0, n1, 1, s)
                on(back_odd, gather_middle, 2, dmr, layer, s)
                on(stage == 6, gather_middle, 3, dyr, 0, s)

            @pl.when(jnp.logical_and(s >= 1, s < chunks + 1))
            def _():
                on(front_even, attention, layer, s - 1)
                on(front_odd, feed, layer, s - 1)
                on(back_even, feed_back, layer, s - 1)
                on(back_odd, attention_back, layer, s - 1)

            @pl.when(s >= 2)
            def _():
                reduce_middle(stage, s - 2)

            @pl.when(jnp.logical_and(stage == 0, s == 1))
            def _():
                relay(2, 0)
            @pl.when(jnp.logical_and(stage == 0, s == 3))
            def _():
                relay(3, 0)
            @pl.when(jnp.logical_and(stage == 1, s == 3))
            def _():
                relay(0, 1)

        each(chunks + 2, step)
        @pl.when(stage == 1)
        def _():
            relay(1, 1)

        @pl.when(stage == 0)
        def _():
            @pl.when(c == 1)
            def _():
                for i in range(4):
                    send_weight(i)

        @pl.when(stage == 4)
        def _():
            each(chunks, lambda k: finish(1, k))
            each(chunks, lambda k: emit(0, 1, k, ledger[0, k]))

        @pl.when(back_even)
        def _():
            each(4, lambda b: grad_down(layer, b))
            z_first_start(0, layer)

            @pl.when(layer == 0)
            def _():
                each(up_steps, lambda b: grad_up(layer, b))
                x_first_start(1, layer)

        @pl.when(back_odd)
        def _():
            grad_out(layer)
            x_first_start(4, layer)
            each(up_steps, lambda b: grad_qkv(layer, b))
            z_first_start(2, layer)
            x_first_start(3, layer)
            gpack[layer, 6:7, 0:384] = mm(ones, dqkv[...])[0:1]

        def settle(k):
            on(front_even, second_norm, layer, k)
            on(stage == 1, finish, 0, k)
            on(back_even, middle, layer, k)
            on(back_odd, last, layer, k)

        on(stage != 3, each, chunks, settle)
        @pl.when(stage == 1)
        def _():
            relay(2, 1)
        @pl.when(stage == 1)
        def _():
            relay(3, 1)


        @pl.when(back_even)
        def _():
            @pl.when(layer == 1)
            def _():
                each(up_steps, lambda b: grad_up(layer, b))
                x_first_start(1, layer)

            column_sum(layer, 1, 0)
            column_sum(layer, 4, 1)
            column_sum(layer, 3, 2)
            column_sum(layer, 5, 3)
            gpack[layer, 6:7, 384:896] = mm(ones, dup[...])[0:1]

        @pl.when(stage == 1)
        def _():
            each(chunks, lambda k: emit(0, 0, k, ledger[0, k]))

        @pl.when(back_odd)
        def _():
            column_sum(layer, 0, 0)
            column_sum(layer, 2, 1)
            small_start(layer)
            each(chunks, lambda k: emit(1, layer, k, ledger[2, k]))

        on(stage == 5, z_first_middle, 0, layer)
        on(jnp.logical_and(stage == 5, c == 1), x_first_middle, 1)
        on(stage == 6, collect_attention, 1)

    each(8, stage_body)
    z_first_middle(0, 0)
    on(c == 0, x_first_middle, 1)
    collect_attention(0)

    places_ = layout(nz)

    def put(name, value, start=0):
        rows = value.shape[0]
        first = places_[name] + start * rows
        for j in range(value.shape[1] // 128):
            grads_ref[first + j * rows : first + (j + 1) * rows] = value[:, j * 128 : (j + 1) * 128]

    put("down", z_first_finish(0))
    put("up", x_first_finish(1))
    small = small_finish()
    put("small", small[0])
    put("bias", small[1])
    put("qkv", x_first_finish(3), 2)
    put("out", x_first_finish(4))
    put("qkv", z_first_finish(2))
    for kind in range(2):
        await_bytes(obuf.at[kind], osem.at[kind])
    rows_ref[...] = obuf[...]

    for i in range(4):
        both = weights[i][1]

        @pl.when(jnp.logical_not(native))
        def _():
            await_bytes(both.at[0], whome.at[i])
            for layer in range(2):
                await_bytes(whole_half(i), wrelay.at[i, layer])

        if i:
            weight_left(i)

    @pl.when(c == 1)
    def _():
        weight_left(0)

    @pl.when(jnp.logical_not(native))
    def _():
        await_bytes(vec.at[0], vsend.at[0])

    await_bytes(vec.at[0], vsend.at[0])
    for ph in range(8):
        await_bytes(cbuf.at[ph], csend.at[ph])
        await_bytes(rs.at[ph], rsend.at[ph])
    for which, layer in ((0, 1), (1, 0), (1, 1), (2, 0), (2, 1), (3, 0)):
        await_bytes(rs.at[0], gsend.at[which, layer])
        await_bytes(cbuf.at[0], hsend.at[which, layer])
    for layer in range(2):
        for kind in range(2):

            @pl.when(c == layer)
            def _():
                view = ostage.at[kind, layer, :, pl.ds(0, T - 1)]
                await_bytes(view, osend.at[kind, layer])

            @pl.when(c != layer)
            def _():
                await_bytes(ostage.at[kind, layer], osend.at[kind, layer])

        self_ = jnp.logical_and(c == layer, native)
        for m in range(5):
            if nz > 1 and m in (0, 2):
                await_bytes(zrs[m].at[layer], zsend.at[m, layer])
            await_bytes(xrs[m].at[0], xsend.at[m, layer])

            @pl.when(jnp.logical_not(self_))
            def _():
                await_bytes(xrs[m].at[0], xsend.at[m, layer])

        await_bytes(sgot.at[pl.ds(0, T - 1)], ssend.at[layer])

        @pl.when(c != layer)
        def _():
            await_bytes(sgot.at[0], ssend.at[layer])

        @pl.when(jnp.logical_not(self_))
        def _():
            await_bytes(sgot.at[0], ssend.at[layer])

    if nz > 1:
        for m in (1, 3, 4):
            await_bytes(zrs[m], zsend.at[m, 0])
    await_bytes(sall, ssend.at[2])


def layout(nz):
    wide = D // (2 * nz)
    sizes = (
        ("qkv", 3 * wide),
        ("up", 4 * wide),
        ("down", 4 * wide),
        ("out", wide),
        ("small", 8),
        ("bias", 8),
    )
    places, first = {}, 0
    for name, size in sizes:
        places[name] = first
        first += size
    places["end"] = first
    return places


def core(chunks, nz, x, ct, docs, wqkv, wout, w1, w2, qb, b1, gains, shifts):
    n = chunks * ROWS
    vm = pl.BlockSpec(memory_space=pltpu.VMEM)
    hbm = pl.BlockSpec(memory_space=pl.ANY)
    pieces = 2 * nz
    wide = D // pieces
    out_shape = (
        jax.ShapeDtypeStruct((2, 2 * n, 128), BF16),
        jax.ShapeDtypeStruct((layout(nz)["end"], 128), F32),
    )
    dma = pltpu.SemaphoreType.DMA
    shape = ((512, wide), (wide, 512), (wide, 256), (wide, 128), (128, wide))
    back = max(nz - 1, 1)
    gbufs = [pltpu.VMEM((2, pieces) + s, BF16) for s in shape]
    zrs, zsums, xrs = [], [], []
    for m, s in enumerate(shape):
        if m in (0, 2):
            zrs.append(pltpu.VMEM((2, back, 2) + s, BF16))
            zsums.append(pltpu.VMEM((2, 2) + s, BF16))
            xrs.append(pltpu.VMEM((4,) + s, BF16))
        else:
            zrs.append(pltpu.VMEM((back,) + s, BF16))
            zsums.append(pltpu.VMEM((nz,) + s, BF16))
            xrs.append(pltpu.VMEM((4, nz) + s, BF16))
    scratch = [
        pltpu.VMEM((n, D), BF16),
        pltpu.VMEM((n, ROWS), F32),
        pltpu.VMEM((8, D), F32),
        pltpu.VMEM((2, D, 384), BF16),
        pltpu.VMEM((2, 128, D), BF16),
        pltpu.VMEM((2, D, 512), BF16),
        pltpu.VMEM((2, 512, D), BF16),
        pltpu.VMEM((2, 8, D), F32),
        pltpu.VMEM((2, n, D), BF16),
        pltpu.VMEM((2, n, D), BF16),
        pltpu.VMEM((2, n, D), BF16),
        pltpu.VMEM((2, n, D), BF16),
        pltpu.VMEM((2, n, 384), BF16),
        pltpu.VMEM((2, n, 128), BF16),
        pltpu.VMEM((2, chunks, 2 * ROWS, ROWS), F32),
        pltpu.VMEM((2, n, 512), F32),
        pltpu.VMEM((2, n, 512), BF16),
        pltpu.VMEM((n, 512), BF16),
        pltpu.VMEM((n, 384), BF16),
        pltpu.VMEM((2, chunks, OWN, D), F32),
        pltpu.VMEM((2, chunks, OWN, D), F32),
        pltpu.VMEM((4, chunks, OWN, D), F32),
        pltpu.VMEM((8, n, D), BF16),
        pltpu.VMEM((8, chunks, ROWS // 2, D), BF16),
        pltpu.VMEM((8, chunks, ROWS // 2, D), BF16),
        pltpu.VMEM((8, chunks, Y - 1, OWN, D), BF16),
        pltpu.VMEM((2, 2, chunks, T, OWN, 128), BF16),
        pltpu.VMEM((2, 2 * n, 128), BF16),
        gbufs,
        zrs,
        zsums,
        xrs,
        pltpu.VMEM((2, 8, D), F32),
        pltpu.VMEM((2, T, 8, 128), F32),
        pltpu.VMEM((2, 8, 128), F32),
        pltpu.VMEM((2 * T + 2, 8, 128), F32),
        pltpu.VMEM((2, 8, 128), F32),
        pltpu.VMEM((pieces - 1, 2, 8, 128), F32),
        dma((2,)),
        dma((4, 2, 2, PARTS)),
        dma((4,)),
        dma((4,)),
        dma((4, 2)),
        dma((2,)),
        dma((1,)),
        dma((8, chunks)),
        dma((8,)),
        dma((8, chunks)),
        dma((8,)),
        dma((4, 2, chunks)),
        dma((4, 2)),
        dma((4, 2, chunks)),
        dma((4, 2)),
        dma((2,)),
        dma((2, 2)),
        dma((5, 2)),
        dma((5, 2)),
        dma((5,)),
        dma((5, 2)),
        dma((2,)),
        dma((3,)),
    ]
    return pl.pallas_call(
        functools.partial(kernel, chunks, nz),
        out_shape=out_shape,
        in_specs=[hbm, hbm, vm, hbm, hbm, hbm, hbm, vm, vm, vm, vm],
        out_specs=[vm] * 2,
        scratch_shapes=scratch,
        compiler_params=pltpu.CompilerParams(
            collective_id=0, has_side_effects=True, vmem_limit_bytes=62 * 2**20
        ),
        name="layers",
    )(x, ct, docs, wqkv, wout, w1, w2, qb, b1, gains, shifts)


def closing(
    m,
    rows_in,
    grads_in,
    sec_out,
    ing_out,
    gqkv_out,
    qb_out,
    gout_out,
    g1_out,
    b1_out,
    g2_out,
    gains_out,
    shifts_out,
    rows,
    grads,
    sems,
):
    d = lax.axis_index("dp")
    rows_copy = pltpu.make_async_copy(rows_in, rows, sems.at[0])
    grads_copy = pltpu.make_async_copy(grads_in, grads, sems.at[1])
    rows_copy.start()
    grads_copy.start()
    rows_copy.wait()
    sec_out[0] = rows[0].astype(F32)
    ing_out[0] = rows[1].astype(F32)
    grads_copy.wait()
    places = layout(m // 2)
    width = D // m

    def get(name, height, j):
        first = places[name] + j * height
        return grads[first : first + height]

    for j in range(3):
        gqkv_out[0, j] = get("qkv", width, j)
    for j in range(4):
        g1_out[0, :, j * 128 : (j + 1) * 128] = get("up", width, j)
    for j in range(width // 128):
        gout_out[0, :, j * 128 : (j + 1) * 128] = get("out", 128, j)
        g2_out[0, :, j * 128 : (j + 1) * 128] = get("down", 512, j)
    share = 128 // m
    shift = lax.rem(128 - d * share, 128)
    rolled = pltpu.roll(get("small", 8, 0), shift, 1)
    gains_out[0] = rolled[0:2, 0:share]
    shifts_out[0] = rolled[2:6, 0:share]
    bias = get("bias", 8, 0)
    rolled = pltpu.roll(bias, shift, 1)
    for j in range(2):
        qb_out[0, j : j + 1] = rolled[2 * j : 2 * j + 1, 0:share]
    lines = lax.broadcasted_iota(jnp.int32, (8, 128), 0)

    def line(block, which):
        return jnp.sum(jnp.where(lines == which, block, 0.0), 0, keepdims=True)

    wide = 512 // m
    if wide >= 128:
        for j in range(wide // 128):
            b1_out[:, j * 128 : (j + 1) * 128] = line(bias, 3 + d * (wide // 128) + j)
    else:
        per = 128 // wide
        rolled = pltpu.roll(bias, lax.rem(128 - lax.rem(d, per) * wide, 128), 1)
        b1_out[...] = line(rolled, 3 + d // per)[:, 0:wide]


def shards(
    inputs,
    cotangent,
    doc_ids,
    qkv_weight,
    qkv_bias,
    out_weight,
    fc1_weight,
    fc1_bias,
    fc2_weight,
    norm_gains,
    shifts,
):
    m = lax.axis_size("dp")
    chunks = doc_ids.shape[0] // 2
    n = chunks * ROWS
    results = core(
        chunks,
        m // 2,
        inputs,
        cotangent,
        doc_ids,
        qkv_weight[0].transpose(1, 0, 2),
        out_weight[0],
        fc1_weight[0],
        fc2_weight[0],
        qkv_bias,
        fc1_bias,
        norm_gains,
        shifts,
    )
    vm = pl.BlockSpec(memory_space=pltpu.VMEM)
    shapes = (
        (1, 2 * n, 128),
        (1, 2 * n, 128),
        (1, 3, D // m, 128),
        (1, 2, 128 // m),
        (1, 128, D // m),
        (1, D // m, 512),
        (1, 512 // m),
        (1, 512, D // m),
        (1, 2, 128 // m),
        (1, 4, 128 // m),
    )
    outs = pl.pallas_call(
        functools.partial(closing, m),
        out_shape=[jax.ShapeDtypeStruct(shape, F32) for shape in shapes],
        in_specs=[pl.BlockSpec(memory_space=pl.ANY)] * 2,
        out_specs=[vm] * 10,
        scratch_shapes=[
            pltpu.VMEM(results[0].shape, BF16),
            pltpu.VMEM(results[1].shape, F32),
            pltpu.SemaphoreType.DMA((2,)),
        ],
        compiler_params=pltpu.CompilerParams(vmem_limit_bytes=62 * 2**20),
        name="closing",
    )(*results)
    return (*outs[:2], outs[2].transpose(0, 2, 1, 3), *outs[3:])


def solution(mesh):
    return jax.shard_map(
        shards,
        mesh=mesh,
        in_specs=(
            P("dp", None),
            P("dp", None),
            P("dp", None),
            P("pipe", None, None, "tensor"),
            P("pipe", None, "tensor"),
            P("pipe", "tensor", None),
            P("pipe", None, "tensor"),
            P("pipe", "tensor"),
            P("pipe", "tensor", None),
            P("pipe", None, None),
            P("pipe", None, None),
        ),
        out_specs=(
            P("pipe", "dp", "tensor"),
            P("pipe", "dp", "tensor"),
            P("pipe", "dp", None, "tensor"),
            P("pipe", None, ("tensor", "dp")),
            P("pipe", "tensor", "dp"),
            P("pipe", "dp", "tensor"),
            P("pipe", ("tensor", "dp")),
            P("pipe", "tensor", "dp"),
            P("pipe", None, ("tensor", "dp")),
            P("pipe", None, ("tensor", "dp")),
        ),
        check_vma=False,
    )
```
